32 devices in a mesh: grp: 2 (over x), pts: 16 (over z, y, core).
Axes of the slice: x: 2, y: 2, z: 4, core: 2. Of those that a mesh axis runs over, the one named last changes fastest.
Arguments:
- points: bfloat16 [131072, 256], P(('grp', 'pts')), parts along dimension 0, may hold values from -24 to 24
- hil_dest: int32 [1024], P(('grp', 'pts')), parts along dimension 0, may hold values from 0 to 15, as said below
- hil_slot: int32 [1024], P(('grp', 'pts')), parts along dimension 0, may hold values from 0 to 31, as said below
- patch_ids: int32 [128, 1024], P(('grp', 'pts')), parts along dimension 0, may hold values from 0 to 3, never falling along the last dimension, each value on 1 to 512 neighbouring positions
- child_counts: int32 [32, 1024], P(('grp', 'pts')), parts along dimension 0, may hold values from 1 to 8, 4096 in all within a row
- parent_order: int32 [32, 1024], P(('grp', 'pts')), parts along dimension 0, may hold values from 0 to 1023, each once within a row
- w_qkv: bfloat16 [256, 768], replicated, may hold values from -0.375 to 0.375
- w_out: bfloat16 [256, 256], replicated, may hold values from -0.375 to 0.375
- w_pool: bfloat16 [256, 512], replicated, may hold values from -0.375 to 0.375
- norm_gain: float32 [512], replicated, may hold values from 0.1 to 1.9
- norm_shift: float32 [512], replicated, may hold values from -3 to 3
- cotangent: bfloat16 [32768, 512], P(('grp', 'pts')), parts along dimension 0, may hold values from -6 to 6
Outputs:
- pooled: bfloat16 [32768, 512], P(('grp', 'pts')), parts along dimension 0
- grad_points: bfloat16 [131072, 256], P(('grp', 'pts')), parts along dimension 0
- grad_weight: float32 [512, 512], P('grp'), parts along dimension 0
- grad_norm: float32 [4, 512], P('grp'), parts along dimension 0
The draws below stay inside these ranges and needn't reach their ends.
There are 2 independent parts, one for each index of `grp`. The reference program is written for one: setup_inputs(seed, part) draws one part's arguments, and reference() takes and returns one part's arrays. A program takes and returns all parts, laid end to end along the dimension named above; an argument that names none is the same for every part. Nothing has to cross between parts.
Inputs may be any that keep to these rules, and one draw needn't show every extreme that they name: `hil_dest`: every device is the destination of exactly 32 blocks; no device sends more than 2 blocks to one device, and some device sends exactly 2 to one. `hil_slot`: the blocks sent to one device take each of its positions once.
All inputs are finite; a program needn't handle non-finite values.
Results may differ from the reference program's by a relative error of at most 0.012.
Values may be sent and summed in bfloat16 or wider, within the bound.
No kernel may reach another device: no remote copies, remote signals or barrier semaphores. Data moves between devices by JAX's collectives and lax.ppermute only.
A program may use at most 128 MiB of HBM per device.

```python
import math
import jax
import jax.numpy as jnp
import numpy as np
from jax import lax

D = 256
DO = 512
HEADS = 16
HDIM = 16
PATCH = 1024
ROWS = 128
CHILD_MOST = 8
PATCH_SEG = 4
BLK = 32
BLOCKS = 512
TOKENS = 65536
TILES = 64
PAR_DEV = 1024
PARENTS = 16384
QPAR = 64
N_PTS = 16


def routing_tables(key):
    key_order, key_base, key_send, key_recv = jax.random.split(key, 4)
    device_order = jax.random.permutation(key_order, N_PTS).astype(jnp.int32)
    device_rank = jnp.argsort(device_order, stable=True).astype(jnp.int32)
    offsets = jax.random.permutation(key_base, N_PTS).astype(jnp.int32)[jnp.arange(BLK) % N_PTS]
    send_perm = jax.vmap(lambda k: jax.random.permutation(k, BLK))(jax.random.split(key_send, N_PTS)).astype(jnp.int32)
    recv_perm = jax.vmap(lambda k: jax.random.permutation(k, BLK))(jax.random.split(key_recv, N_PTS)).astype(jnp.int32)
    destination = device_order[(device_rank[:, None] + offsets[send_perm]) % N_PTS]
    position = recv_perm[destination, send_perm]
    return (destination.reshape(-1).astype(jnp.int32), position.reshape(-1).astype(jnp.int32))


def draw_hil_dest(key, part):
    return routing_tables(key)[0]


def draw_hil_slot(key, part):
    return routing_tables(key)[1]


def draw_points(key, part):
    key = jax.random.fold_in(key, 7)
    key_main = jax.random.fold_in(key, 0)
    base = jnp.clip(jax.random.normal(key_main, (TOKENS, D), jnp.float32), -4.0, 4.0)
    return base.astype(jnp.bfloat16)


def block_levels(own_key, extent, cuts, least, top_value):
    loudness = 1.0
    for dim, parts in cuts:
        draws = jax.random.uniform(jax.random.fold_in(jax.random.fold_in(own_key, 6), dim), (parts,), jnp.float32, least / len(cuts), top_value / len(cuts))
        loudness = loudness * jnp.repeat(jnp.exp(draws), extent[dim] // parts).reshape((-1,) + (1,) * (len(extent) - 1 - dim))
    return loudness


def length_profile(count, total, reach, slope):
    portions = [(1 << 20) // math.isqrt(rank ** slope) + 1 for rank in range(2, count + 1)]
    surplus, counts = total - reach - (count - 1), [1] * (count - 1)
    while surplus > 0:
        candidates = [i for i in range(count - 1) if counts[i] < reach]
        pool, left = sum([portions[i] for i in candidates]), surplus
        for i in candidates:
            more = min(reach - counts[i], max(1, left * portions[i] // pool), surplus)
            counts[i] = counts[i] + more
            surplus = surplus - more
    return np.array([reach] + counts)


def ragged_sizes(stream_key, amount, total, bound, slope):
    if amount == 2:
        one = jax.random.randint(stream_key, (), max(1, total - bound), min(bound, total - 1) + 1)
        return jnp.stack([one, total - one])
    tallies = jnp.asarray(length_profile(amount, total, bound, slope), jnp.int32)
    couples = (amount - 1) // 2
    giver, receiver = tallies[1:1 + 2 * couples:2], tallies[2:2 + 2 * couples:2]
    room = jnp.minimum(giver - 1, bound - receiver)
    moved = jax.random.randint(jax.random.fold_in(stream_key, 1), (couples,), 0, 1 << 20) % (room + 1)
    tallies = tallies.at[1:1 + 2 * couples:2].set(giver - moved).at[2:2 + 2 * couples:2].set(receiver + moved)
    return tallies[jax.random.permutation(jax.random.fold_in(stream_key, 2), amount)]


def noise(rng, shape, spread, limit, cuts=(), kind=jnp.bfloat16):
    gain = block_levels(rng, shape, cuts, -0.22, 0.18) if cuts else 1.0
    drawn = jax.random.normal(rng, shape, jnp.float32) * spread * gain
    return jnp.minimum(jnp.maximum(drawn, -limit), limit).astype(kind)


def setup_inputs(seed: int = 0, part: int = 0) -> dict:
    key_of = jax.random.split(jax.random.key(seed), 13)
    part_keys = jax.random.split(jax.random.fold_in(key_of[12], part), 13)
    points = draw_points(jax.random.fold_in(jax.random.fold_in(key_of[12], part), 71), part)
    hil_dest = draw_hil_dest(jax.random.fold_in(jax.random.fold_in(key_of[12], part), 71), part)
    hil_slot = draw_hil_slot(jax.random.fold_in(jax.random.fold_in(key_of[12], part), 71), part)
    patch_ids = jax.vmap(lambda own: jnp.searchsorted(jnp.cumsum(ragged_sizes(own, PATCH_SEG, PATCH, PATCH // 2, 1)), jnp.arange(PATCH), side="right"))(jax.random.split(part_keys[3], TILES)).reshape((TILES, PATCH)).astype(jnp.int32)
    child_counts = jax.vmap(lambda own: ragged_sizes(own, PAR_DEV, BLK * ROWS, CHILD_MOST, 1))(jax.random.split(part_keys[4], N_PTS)).reshape((N_PTS, PAR_DEV)).astype(jnp.int32)
    parent_order = jax.vmap(lambda own: jax.random.permutation(own, PAR_DEV))(jax.random.split(part_keys[5], N_PTS)).reshape((N_PTS, PAR_DEV)).astype(jnp.int32)
    w_qkv = noise(key_of[6], (D, 3 * D), D ** -0.5, 0.375)
    w_out = noise(key_of[7], (D, D), D ** -0.5, 0.375)
    w_pool = noise(key_of[8], (D, DO), D ** -0.5, 0.375)
    norm_gain = jnp.clip(1.0 + 0.18 * jax.random.normal(key_of[9], (DO,), jnp.float32), 0.1, 1.9)
    norm_shift = noise(key_of[10], (DO,), 0.5, 3.0, (), jnp.float32)
    cotangent = noise(part_keys[11], (PARENTS, DO), 1.0, 6.0, ((0, 16),))
    return {"points": points, "hil_dest": hil_dest, "hil_slot": hil_slot, "patch_ids": patch_ids, "child_counts": child_counts, "parent_order": parent_order, "w_qkv": w_qkv, "w_out": w_out, "w_pool": w_pool, "norm_gain": norm_gain, "norm_shift": norm_shift, "cotangent": cotangent}


inv_sqrt_two = 0.7071067811865476
inv_sqrt_tau = 0.3989422804014327
norm_eps = 1e-05

def parent_index(child_total, rows):
    run_ends = jnp.cumsum(child_total).astype(jnp.int32)
    run_starts = (run_ends - child_total).astype(jnp.int32)
    run_marks = jnp.zeros((rows,), jnp.int32).at[run_starts].add(1)
    return (jnp.cumsum(run_marks) - 1).astype(jnp.int32)

def attend_tile(tile_rows, patch_index, w_qkv, w_out):
    qkv_rows = jnp.dot(tile_rows, w_qkv, preferred_element_type=jnp.float32).astype(jnp.bfloat16)
    groups = HEADS // 4

    def split_heads(which):
        columns = qkv_rows[:, which * D:(which + 1) * D]
        return columns.reshape(PATCH, groups, 4, HDIM).transpose(1, 0, 2, 3)
    queries = split_heads(0)
    key_heads = split_heads(1)
    values = split_heads(2)
    allowed = patch_index[:, None] == patch_index[None, :]

    def one_group(triple):
        query_g, key_g, value_g = triple
        scores = jnp.einsum('qhd,khd->hqk', query_g.astype(jnp.float32), key_g.astype(jnp.float32)) * HDIM ** (-0.5)
        scores = jnp.where(allowed[None], scores, -jnp.inf)
        row_max = lax.optimization_barrier(jnp.max(scores, axis=-1, keepdims=True))
        weights_exp = jnp.exp(scores - row_max)
        probability = (weights_exp / lax.optimization_barrier(jnp.sum(weights_exp, axis=-1, keepdims=True))).astype(jnp.bfloat16)
        return jnp.einsum('hqk,khd->qhd', probability.astype(jnp.float32), value_g.astype(jnp.float32))
    attended = lax.map(one_group, (queries, key_heads, values))
    attended = attended.transpose(1, 0, 2, 3).reshape(PATCH, D).astype(jnp.bfloat16)
    return (tile_rows.astype(jnp.float32) + jnp.dot(attended, w_out, preferred_element_type=jnp.float32)).astype(jnp.bfloat16)

def reference(points, hil_dest, hil_slot, patch_ids, child_counts, parent_order, w_qkv, w_out, w_pool, norm_gain, norm_shift, cotangent):
    z_blocks = points.reshape(BLOCKS, ROWS * D)
    hil_place = (hil_dest * BLK + hil_slot).astype(jnp.int32)
    ordered = jnp.zeros_like(z_blocks).at[hil_place].set(z_blocks)
    patch_tiles = ordered.reshape(TILES, PATCH, D)

    def tile_step(pair):
        return attend_tile(pair[0], pair[1], w_qkv, w_out)
    mixed_rows = lax.map(tile_step, (patch_tiles, patch_ids))
    home_rows = mixed_rows.reshape(BLOCKS, ROWS * D)[hil_place].reshape(N_PTS, BLK * ROWS, D)

    def pool_device(triple):
        home_part, child_total, send_order = triple
        parent_ids = parent_index(child_total, BLK * ROWS)
        child_sums = jax.ops.segment_sum(home_part.astype(jnp.float32), parent_ids, num_segments=PAR_DEV)
        parent_means = (child_sums / child_total.astype(jnp.float32)[:, None]).astype(jnp.bfloat16)
        return parent_means[send_order]
    outgoing = lax.map(pool_device, (home_rows, child_counts, parent_order))
    parent_in = outgoing.reshape(N_PTS, N_PTS, QPAR, D).transpose(1, 0, 2, 3).reshape(PARENTS, D)
    projected = jnp.dot(parent_in, w_pool, preferred_element_type=jnp.float32)
    centred = projected - lax.optimization_barrier(jnp.mean(projected, axis=-1, keepdims=True))
    variance = lax.optimization_barrier(jnp.mean(centred * centred, axis=-1, keepdims=True))
    inv_std = lax.rsqrt(variance + norm_eps)
    normed = centred * inv_std
    shifted = normed * norm_gain + norm_shift
    normal_cdf = 0.5 * (1.0 + jax.scipy.special.erf(shifted * inv_sqrt_two))
    pooled = (shifted * normal_cdf).astype(jnp.bfloat16)
    grad_act = cotangent.astype(jnp.float32) * (normal_cdf + shifted * jnp.exp(-0.5 * shifted * shifted) * inv_sqrt_tau)
    grad_norm = jnp.stack([lax.optimization_barrier(jnp.sum(grad_act * normed, axis=0)), lax.optimization_barrier(jnp.sum(grad_act, axis=0))])
    grad_scaled = grad_act * norm_gain
    grad_proj = ((grad_scaled - lax.optimization_barrier(jnp.mean(grad_scaled, axis=-1, keepdims=True)) - normed * lax.optimization_barrier(jnp.mean(grad_scaled * normed, axis=-1, keepdims=True))) * inv_std).astype(jnp.bfloat16)
    grad_weight = jnp.dot(parent_in.T, grad_proj, preferred_element_type=jnp.float32)
    grad_parent = jnp.dot(grad_proj, w_pool.T, preferred_element_type=jnp.float32)
    grad_parent = grad_parent.reshape(N_PTS, N_PTS, QPAR, D).transpose(1, 0, 2, 3).reshape(N_PTS, PAR_DEV, D)

    def spread_device(triple):
        grad_rows, child_total, send_order = triple
        parent_ids = parent_index(child_total, BLK * ROWS)
        placed = jnp.zeros((PAR_DEV, D), jnp.float32).at[send_order].set(grad_rows)
        share = placed[parent_ids] / child_total.astype(jnp.float32)[parent_ids][:, None]
        return share.astype(jnp.bfloat16)
    grad_points = lax.map(spread_device, (grad_parent, child_counts, parent_order)).reshape(TOKENS, D)
    return (pooled, grad_points, grad_weight, grad_norm)
```

```python
import functools
import math

import jax
import jax.numpy as jnp
from jax import lax
from jax.experimental import pallas as pl
from jax.experimental.pallas import tpu as pltpu
from jax.sharding import PartitionSpec as P

HDIM = 16
HEAD_GROUP = 8
ROWS = 128
WINDOW = 256
PATCHES = 4
FAR = 2.0**100
SCORE_SCALE = HDIM**-0.5 * math.log2(math.e)
SCORE_SAFE = 98.0

inv_sqrt_two = 0.7071067811865476
inv_sqrt_tau = 0.3989422804014327
norm_eps = 1e-05

BF = jnp.bfloat16
F32 = jnp.float32
NT = (((1,), (1,)), ((), ()))
TN = (((0,), (0,)), ((), ()))
VMEM = pl.BlockSpec(memory_space=pltpu.VMEM)
SMEM = pl.BlockSpec(memory_space=pltpu.SMEM)
ANY = pl.BlockSpec(memory_space=pl.ANY)
ROOM = pltpu.CompilerParams(vmem_limit_bytes=48 << 20)


def iota(shape, dim):
    return lax.broadcasted_iota(jnp.int32, shape, dim)


def mm(a, b, dims=(((1,), (0,)), ((), ()))):
    return lax.dot_general(a, b, dims, preferred_element_type=F32)


def cost(flops, bytes_accessed, transcendentals=0):
    return pl.CostEstimate(
        flops=int(flops), bytes_accessed=int(bytes_accessed), transcendentals=int(transcendentals)
    )


def pack_kernel(capacity, dest_ref, points_ref, payload_ref, place_ref, used, sem):
    blocks = dest_ref.shape[0]

    def clear(d, _):
        used[d] = 0
        return 0

    lax.fori_loop(0, used.shape[0], clear, 0)

    def send(b, _):
        d = dest_ref[b]
        place = d * capacity + used[d]
        used[d] = used[d] + 1
        place_ref[b] = place
        pltpu.make_async_copy(
            points_ref.at[pl.ds(pl.multiple_of(b * ROWS, ROWS), ROWS)],
            payload_ref.at[pl.ds(pl.multiple_of(place * ROWS, ROWS), ROWS)],
            sem,
        ).start()
        return 0

    lax.fori_loop(0, blocks, send, 0)
    whole = pl.ds(0, blocks * ROWS)
    pltpu.make_async_copy(points_ref.at[whole], payload_ref.at[whole], sem).wait()


def pack_blocks(hil_dest, points, devices, capacity):
    return pl.pallas_call(
        functools.partial(pack_kernel, capacity),
        out_shape=(
            jax.ShapeDtypeStruct((devices * capacity * ROWS, points.shape[1]), BF),
            jax.ShapeDtypeStruct(hil_dest.shape, jnp.int32),
        ),
        in_specs=[SMEM, ANY],
        out_specs=(ANY, SMEM),
        scratch_shapes=[pltpu.SMEM((devices,), jnp.int32), pltpu.SemaphoreType.DMA],
        compiler_params=ROOM,
        cost_estimate=cost(0, 4 * points.size),
    )(hil_dest, points)


def attend_kernel(
    group, index_ref, low_ref, count_ref, ids_ref, w_ref, rows_ref, out_ref, x, qx, kx, vx, sems
):
    tiles, span = ids_ref.shape
    width = w_ref.shape[0]
    cols = HEAD_GROUP * HDIM
    per_tile = span // ROWS

    for t in range(tiles):
        for b in range(per_tile):
            s = t * per_tile + b
            pltpu.make_async_copy(
                rows_ref.at[pl.ds(pl.multiple_of(index_ref[s] * ROWS, ROWS), ROWS)],
                x.at[pl.ds(s * ROWS, ROWS)],
                sems.at[t],
            ).start()

    lane = iota((ROWS, 2 * cols), 1)
    of_head = [(lane // HDIM == h) | (lane >= cols) for h in range(HEAD_GROUP)]
    lane_out = iota((ROWS, 2 * cols), 1) % cols // HDIM
    vx[:, cols:] = jnp.ones((span, cols), BF)
    r_i = iota((cols, cols), 0)
    c_i = iota((cols, cols), 1)
    far = jnp.where((r_i != c_i) & (c_i < PATCHES), -FAR, 0.0).astype(BF)
    first = group * cols

    def tile(t, _):
        at = pl.ds(pl.multiple_of(t * span, span), span)
        pltpu.make_async_copy(rows_ref.at[pl.ds(0, span)], x.at[at], sems.at[t]).wait()
        tile_rows = x[at, :]
        same = ids_ref[pl.ds(t, 1), :] == iota((cols, span), 0)
        patch_hot = jnp.where(same, 1.0, 0.0).astype(BF)
        query = mm(tile_rows, w_ref[:, first : first + cols])
        keys = mm(
            w_ref[:, width + first : width + first + cols], tile_rows, (((0,), (1,)), ((), ()))
        )
        qx[:, :cols] = query.astype(BF)
        qx[:, cols:] = mm(patch_hot, far, TN).astype(BF)
        kx[:cols, :] = keys.astype(BF)
        kx[cols:, :] = patch_hot
        vx[:, :cols] = mm(tile_rows, w_ref[:, 2 * width + first : 2 * width + first + cols]).astype(BF)
        query_most = jnp.max(jnp.abs(query), axis=0, keepdims=True)
        key_most = jnp.max(jnp.abs(keys), axis=1, keepdims=True)
        by_head = jnp.where(iota((8, cols), 1) // HDIM == iota((8, cols), 0), query_most, 0.0)
        bound = jnp.max(mm(by_head.astype(BF), jnp.broadcast_to(key_most, (cols, cols)).astype(BF)))
        safe = bound * SCORE_SCALE < SCORE_SAFE

        def block(b, _):
            s_id = t * per_tile + b
            low = pl.multiple_of(low_ref[s_id], ROWS)
            steps = count_ref[s_id]
            put = pl.ds(pl.multiple_of(index_ref[s_id] * ROWS, ROWS), ROWS)

            def run(start, length, exact):
                q = qx[pl.ds(pl.multiple_of(b * ROWS, ROWS), ROWS), :]
                stacked = jnp.concatenate(
                    [jnp.where(of_head[h], q, jnp.zeros_like(q)) for h in range(HEAD_GROUP)], axis=0
                )
                scores = mm(stacked, kx[:, pl.ds(start, length)]) * SCORE_SCALE
                if exact:
                    scores = scores - jnp.max(scores, axis=1, keepdims=True)
                weights = jnp.exp2(scores).astype(BF)
                mixed = mm(weights, vx[pl.ds(start, length), :]).reshape(HEAD_GROUP, ROWS, 2 * cols)
                own = mixed[0]
                for h in range(1, HEAD_GROUP):
                    own = jnp.where(lane_out == h, mixed[h], own)
                out_ref[put, :] = (own[:, :cols] / own[:, cols:]).astype(BF)

            for i in range(span // WINDOW):
                pl.when(safe & (steps == i + 1))(
                    functools.partial(run, low, (i + 1) * WINDOW, False)
                )
            pl.when(jnp.logical_not(safe))(functools.partial(run, 0, span, True))
            return 0

        lax.fori_loop(0, per_tile, block, 0)
        return 0

    lax.fori_loop(0, tiles, tile, 0)


def attend(group, index, low, count, ids, w_qkv, rows):
    tiles, span = ids.shape
    cols = HEAD_GROUP * HDIM
    pairs = tiles * span * span * HEAD_GROUP // 2
    return pl.pallas_call(
        functools.partial(attend_kernel, group),
        out_shape=jax.ShapeDtypeStruct((rows.shape[0], cols), BF),
        in_specs=[SMEM, SMEM, SMEM, VMEM, VMEM, ANY],
        out_specs=VMEM,
        scratch_shapes=[
            pltpu.VMEM((tiles * span, rows.shape[1]), BF),
            pltpu.VMEM((span, 2 * cols), BF),
            pltpu.VMEM((2 * cols, span), BF),
            pltpu.VMEM((span, 2 * cols), BF),
            pltpu.SemaphoreType.DMA((tiles,)),
        ],
        compiler_params=ROOM,
        cost_estimate=cost(pairs * 1024, 4 * rows.size, pairs),
    )(index, low, count, ids, w_qkv, rows)


def home_kernel(
    counts_ref, order_ref, points_ref, spread_ref, base_ref, length_ref, first_row, last_row, acc
):
    step = pl.program_id(0)
    chunk, parents = spread_ref.shape

    @pl.when(step == 0)
    def _():
        counts = jnp.broadcast_to(counts_ref[...], (8, parents)).astype(F32)
        upper = jnp.where(iota((parents, parents), 0) <= iota((parents, parents), 1), 1.0, 0.0)
        starts = mm(counts.astype(BF), upper.astype(BF)) - counts
        coarse = jnp.floor(starts * (1.0 / 64.0))
        which = iota((8, parents), 0)
        fields = jnp.where(
            which == 0, coarse, jnp.where(which == 1, starts - 64.0 * coarse, counts)
        ).astype(BF)
        pick = jnp.where(iota((parents, parents), 0) == order_ref[...], 1.0, 0.0).astype(BF)
        ordered = mm(fields, pick)
        first_row[...] = (64.0 * ordered[0:1] + ordered[1:2]).astype(jnp.int32)
        last_row[...] = (64.0 * ordered[0:1] + ordered[1:2] + ordered[2:3]).astype(jnp.int32)
        select = jnp.where(iota((8, 128), 0) == 2, 1.0, 0.0).astype(BF)
        length_ref[...] = mm(ordered.astype(BF), select, TN)
        acc[...] = jnp.zeros_like(acc)

    row = iota((chunk, parents), 0) + step * chunk
    inside = (row >= first_row[...]) & (row < last_row[...])
    spread = jnp.where(inside, 1.0, 0.0).astype(BF)
    spread_ref[...] = spread
    acc[...] += mm(spread, points_ref[...], TN)

    @pl.when(step == pl.num_programs(0) - 1)
    def _():
        base_ref[...] = acc[...]


def home_tables(child_counts, parent_order, points):
    rows, width = points.shape
    parents = child_counts.shape[1]
    chunk = 512
    return pl.pallas_call(
        home_kernel,
        grid=(rows // chunk,),
        out_shape=(
            jax.ShapeDtypeStruct((rows, parents), BF),
            jax.ShapeDtypeStruct((parents, width), F32),
            jax.ShapeDtypeStruct((parents, 128), F32),
        ),
        in_specs=[
            pl.BlockSpec((1, parents), lambda i: (0, 0)),
            pl.BlockSpec((1, parents), lambda i: (0, 0)),
            pl.BlockSpec((chunk, width), lambda i: (i, 0)),
        ],
        out_specs=(
            pl.BlockSpec((chunk, parents), lambda i: (i, 0)),
            pl.BlockSpec((parents, width), lambda i: (0, 0)),
            pl.BlockSpec((parents, 128), lambda i: (0, 0)),
        ),
        scratch_shapes=[
            pltpu.VMEM((1, parents), jnp.int32),
            pltpu.VMEM((1, parents), jnp.int32),
            pltpu.VMEM((parents, width), F32),
        ],
        compiler_params=ROOM,
        cost_estimate=cost(2 * rows * parents * width, 2 * rows * parents),
    )(child_counts, parent_order, points)


def gather_kernel(
    last, place_ref, spread_ref, returned_ref, base_ref, w_ref, length_ref, out_ref, rows, acc, sem
):
    step = pl.program_id(0)
    chunk = spread_ref.shape[0]
    blocks = place_ref.shape[0]

    @pl.when(step == 0)
    def _():
        for b in range(blocks):
            pltpu.make_async_copy(
                returned_ref.at[pl.ds(pl.multiple_of(place_ref[b] * ROWS, ROWS), ROWS)],
                rows.at[pl.ds(b * ROWS, ROWS)],
                sem,
            ).start()
        acc[...] = jnp.zeros_like(acc)
        pltpu.make_async_copy(returned_ref.at[pl.ds(0, blocks * ROWS)], rows, sem).wait()

    acc[...] += mm(
        spread_ref[...], rows[pl.ds(pl.multiple_of(step * chunk, chunk), chunk), :], TN
    )

    @pl.when(step == pl.num_programs(0) - 1)
    def _():
        total = base_ref[...] + mm(acc[...].astype(BF), w_ref[...])
        if last:
            total = total / jnp.concatenate([length_ref[...]] * (total.shape[1] // 128), axis=1)
        out_ref[...] = total.astype(out_ref.dtype)


def gather_means(last, place, spread, returned, base, w_out, length, group):
    rows, parents = spread.shape
    width = base.shape[1]
    cols = returned.shape[1]
    chunk = 512
    fixed = lambda i: (0, 0)
    return pl.pallas_call(
        functools.partial(gather_kernel, last),
        grid=(rows // chunk,),
        out_shape=jax.ShapeDtypeStruct((parents, width), BF if last else F32),
        in_specs=[
            SMEM,
            pl.BlockSpec((chunk, parents), lambda i: (i, 0)),
            ANY,
            pl.BlockSpec((parents, width), fixed),
            pl.BlockSpec((cols, width), lambda i: (group, 0)),
            pl.BlockSpec((parents, 128), fixed),
        ],
        out_specs=pl.BlockSpec((parents, width), fixed),
        scratch_shapes=[
            pltpu.VMEM((rows, cols), BF),
            pltpu.VMEM((parents, cols), F32),
            pltpu.SemaphoreType.DMA,
        ],
        compiler_params=ROOM,
        cost_estimate=cost(2 * rows * parents * cols, 2 * rows * parents),
    )(place, spread, returned, base, w_out, length)


def pool_kernel(
    in_ref, w_ref, gain_ref, shift_ref, cot_ref, pooled_ref, back_ref, weight_ref, norm_ref, acc, sums
):
    step = pl.program_id(0)

    @pl.when(step == 0)
    def _():
        acc[...] = jnp.zeros_like(acc)
        sums[...] = jnp.zeros_like(sums)

    parent_in = in_ref[...]
    w_pool = w_ref[...]
    gain = gain_ref[...]
    projected = mm(parent_in, w_pool)
    centred = projected - jnp.mean(projected, axis=-1, keepdims=True)
    variance = jnp.mean(centred * centred, axis=-1, keepdims=True)
    inv_std = lax.rsqrt(variance + norm_eps)
    normed = centred * inv_std
    shifted = normed * gain + shift_ref[...]
    normal_cdf = 0.5 * (1.0 + lax.erf(shifted * inv_sqrt_two))
    pooled_ref[...] = (shifted * normal_cdf).astype(BF)
    grad_act = cot_ref[...].astype(F32) * (
        normal_cdf + shifted * jnp.exp(-0.5 * shifted * shifted) * inv_sqrt_tau
    )
    sums[0:1, :] += jnp.sum(grad_act * normed, axis=0, keepdims=True)
    sums[1:2, :] += jnp.sum(grad_act, axis=0, keepdims=True)
    scaled = grad_act * gain
    grad_proj = (
        (
            scaled
            - jnp.mean(scaled, axis=-1, keepdims=True)
            - normed * jnp.mean(scaled * normed, axis=-1, keepdims=True)
        )
        * inv_std
    ).astype(BF)
    acc[...] += mm(parent_in, grad_proj, TN)
    back_ref[...] = mm(grad_proj, w_pool, NT).astype(BF)

    @pl.when(step == pl.num_programs(0) - 1)
    def _():
        weight_ref[...] = acc[...].astype(BF)
        norm_ref[...] = sums[...]


def pool(parent_in, w_pool, gain, shift, cotangent):
    parents, width = parent_in.shape
    wide = w_pool.shape[1]
    chunk = 256
    fixed = lambda i: (0, 0)
    along = lambda i: (i, 0)
    return pl.pallas_call(
        pool_kernel,
        grid=(parents // chunk,),
        out_shape=(
            jax.ShapeDtypeStruct((parents, wide), BF),
            jax.ShapeDtypeStruct((parents, width), BF),
            jax.ShapeDtypeStruct((width, wide), BF),
            jax.ShapeDtypeStruct((8, wide), F32),
        ),
        in_specs=[
            pl.BlockSpec((chunk, width), along),
            pl.BlockSpec((width, wide), fixed),
            pl.BlockSpec((1, wide), fixed),
            pl.BlockSpec((1, wide), fixed),
            pl.BlockSpec((chunk, wide), along),
        ],
        out_specs=(
            pl.BlockSpec((chunk, wide), along),
            pl.BlockSpec((chunk, width), along),
            pl.BlockSpec((width, wide), fixed),
            pl.BlockSpec((8, wide), fixed),
        ),
        scratch_shapes=[pltpu.VMEM((width, wide), F32), pltpu.VMEM((8, wide), F32)],
        compiler_params=ROOM,
        cost_estimate=cost(6 * parents * width * wide, 8 * parents * wide, 2 * parents * wide),
    )(parent_in, w_pool, gain, shift, cotangent)


def spread_kernel(spread_ref, grad_ref, length_ref, out_ref, share):
    @pl.when(pl.program_id(0) == 0)
    def _():
        lengths = jnp.concatenate([length_ref[...]] * (share.shape[1] // 128), axis=1)
        share[...] = (grad_ref[...].astype(F32) / lengths).astype(BF)

    out_ref[...] = mm(spread_ref[...], share[...]).astype(BF)


def spread_grads(spread, grad_back, length):
    rows, parents = spread.shape
    width = grad_back.shape[1]
    chunk = 512
    fixed = lambda i: (0, 0)
    return pl.pallas_call(
        spread_kernel,
        grid=(rows // chunk,),
        out_shape=jax.ShapeDtypeStruct((rows, width), BF),
        in_specs=[
            pl.BlockSpec((chunk, parents), lambda i: (i, 0)),
            pl.BlockSpec((parents, width), fixed),
            pl.BlockSpec((parents, 128), fixed),
        ],
        out_specs=pl.BlockSpec((chunk, width), lambda i: (i, 0)),
        scratch_shapes=[pltpu.VMEM((parents, width), BF)],
        compiler_params=ROOM,
        cost_estimate=cost(2 * rows * parents * width, 2 * rows * parents),
    )(spread, grad_back, length)


def exchange(rows, devices):
    parts = rows.reshape(devices, rows.shape[0] // devices, rows.shape[1])
    moved = lax.all_to_all(parts, "pts", split_axis=0, concat_axis=0, tiled=True)
    return moved.reshape(rows.shape)


def received_index(hil_dest, hil_slot, devices, capacity):
    blocks = hil_dest.shape[0]
    codes = lax.all_gather(hil_dest * blocks + hil_slot, "pts")
    mine = codes // blocks == lax.axis_index("pts")
    slots = codes % blocks
    earlier = jnp.arange(blocks)[None, :] < jnp.arange(blocks)[:, None]
    rank = jnp.sum(mine[:, None, :] & earlier[None], axis=2)
    index = jnp.arange(devices)[:, None] * capacity + rank
    hit = mine[:, :, None] & (slots[:, :, None] == jnp.arange(blocks)[None, None, :])
    return jnp.sum(jnp.where(hit, index[:, :, None], 0), axis=(0, 1)).astype(jnp.int32)


def key_windows(patch_ids):
    tiles, span = patch_ids.shape
    patch = jnp.arange(PATCHES + 1)
    starts = jnp.sum(patch_ids[:, None, :] < patch[None, :, None], axis=2)
    by_block = patch_ids.reshape(tiles, span // ROWS, ROWS)
    first, last = by_block[:, :, 0], by_block[:, :, -1]
    pick = lambda which: jnp.sum(
        jnp.where(which[:, :, None] == patch[None, None, :], starts[:, None, :], 0), axis=2
    )
    low = pick(first) // ROWS * ROWS
    count = (pick(last + 1) - low + WINDOW - 1) // WINDOW
    low = jnp.minimum(low, span - count * WINDOW)
    return low.reshape(-1).astype(jnp.int32), count.reshape(-1).astype(jnp.int32)


def local(
    points,
    hil_dest,
    hil_slot,
    patch_ids,
    child_counts,
    parent_order,
    w_qkv,
    w_out,
    w_pool,
    norm_gain,
    norm_shift,
    cotangent,
):
    devices = lax.axis_size("pts")
    blocks = hil_dest.shape[0]
    width = points.shape[1]
    wide = w_pool.shape[1]
    parents = child_counts.shape[1]
    capacity = (blocks + devices - 1) // devices

    index = received_index(hil_dest, hil_slot, devices, capacity)
    payload, place = pack_blocks(hil_dest, points, devices, capacity)
    received = exchange(payload, devices)
    low, count = key_windows(patch_ids)
    spread, total, length = home_tables(child_counts, parent_order, points)

    groups = width // (HEAD_GROUP * HDIM)
    for group in range(groups):
        attended = attend(group, index, low, count, patch_ids, w_qkv, received)
        returned = exchange(attended, devices)
        total = gather_means(
            group == groups - 1, place, spread, returned, total, w_out, length, group
        )

    parent_in = exchange(total, devices)
    pooled, back, weight, norm = pool(
        parent_in, w_pool, norm_gain[None], norm_shift[None], cotangent
    )
    norm_high = norm.astype(BF)
    norm_low = (norm - norm_high.astype(F32)).astype(BF)
    norm_parts = jnp.concatenate([norm_high[:2], norm_low[:2]], axis=0).reshape(1, -1, width)
    outgoing = jnp.concatenate(
        [
            back.reshape(devices, -1, width),
            weight.reshape(devices, -1, width),
            jnp.broadcast_to(norm_parts, (devices,) + norm_parts.shape[1:]),
        ],
        axis=1,
    )
    arrived = lax.all_to_all(outgoing, "pts", split_axis=0, concat_axis=0, tiled=True)
    per_owner = parents // devices
    weight_rows = width * wide // width // devices
    grad_back = arrived[:, :per_owner].reshape(parents, width)
    weight_sum = jnp.sum(arrived[:, per_owner : per_owner + weight_rows].astype(F32), axis=0)
    norm_sum = jnp.sum(arrived[:, per_owner + weight_rows :].astype(F32), axis=0)
    norm_sum = norm_sum.reshape(4, wide)
    grad_norm = norm_sum[:2] + norm_sum[2:]
    shared = jnp.broadcast_to(weight_sum.astype(BF)[None], (devices,) + weight_sum.shape)
    grad_weight = (
        lax.all_to_all(shared, "pts", split_axis=0, concat_axis=0, tiled=True)
        .reshape(width, wide)
        .astype(F32)
    )
    grad_points = spread_grads(spread, grad_back, length)
    return (pooled, grad_points, grad_weight, grad_norm)


def solution(mesh):
    in_specs = (
        P(("grp", "pts"), None),
        P(("grp", "pts")),
        P(("grp", "pts")),
        P(("grp", "pts"), None),
        P(("grp", "pts"), None),
        P(("grp", "pts"), None),
        P(),
        P(),
        P(),
        P(),
        P(),
        P(("grp", "pts"), None),
    )
    out_specs = (P(("grp", "pts"), None), P(("grp", "pts"), None), P("grp", None), P("grp", None))
    return jax.shard_map(local, mesh=mesh, in_specs=in_specs, out_specs=out_specs, check_vma=False)
```

```python
import functools
import math

import jax
import jax.numpy as jnp
from jax import lax
from jax.experimental import pallas as pl
from jax.experimental.pallas import tpu as pltpu
from jax.sharding import PartitionSpec as P

HDIM = 16
HEAD_GROUP = 8
ROWS = 128
SEAT = 128
SEATS = 112
INFO = 16
WINDOW = 256
PATCHES = 4
FAR = 2.0**100
SCORE_SCALE = HDIM**-0.5 * math.log2(math.e)
SCORE_SAFE = 98.0

inv_sqrt_two = 0.7071067811865476
inv_sqrt_tau = 0.3989422804014327
norm_eps = 1e-05

BF = jnp.bfloat16
F32 = jnp.float32
NT = (((1,), (1,)), ((), ()))
TN = (((0,), (0,)), ((), ()))
VMEM = pl.BlockSpec(memory_space=pltpu.VMEM)
HBM = pl.BlockSpec(memory_space=pltpu.HBM)
SMEM = pl.BlockSpec(memory_space=pltpu.SMEM)
ANY = pl.BlockSpec(memory_space=pl.ANY)
ROOM = pltpu.CompilerParams(vmem_limit_bytes=48 << 20)


def iota(shape, dim):
    return lax.broadcasted_iota(jnp.int32, shape, dim)


def mm(a, b, dims=(((1,), (0,)), ((), ()))):
    return lax.dot_general(a, b, dims, preferred_element_type=F32)


def cost(flops, bytes_accessed, transcendentals=0):
    return pl.CostEstimate(
        flops=int(flops), bytes_accessed=int(bytes_accessed), transcendentals=int(transcendentals)
    )


def pack_kernel(capacity, dest_ref, points_ref, payload_ref, used, sem):
    blocks = dest_ref.shape[0]

    def clear(d, _):
        used[d] = 0
        return 0

    lax.fori_loop(0, used.shape[0], clear, 0)

    def send(b, _):
        d = dest_ref[b]
        place = d * capacity + used[d]
        used[d] = used[d] + 1
        pltpu.make_async_copy(
            points_ref.at[pl.ds(pl.multiple_of(b * ROWS, ROWS), ROWS)],
            payload_ref.at[pl.ds(pl.multiple_of(place * ROWS, ROWS), ROWS)],
            sem,
        ).start()
        return 0

    lax.fori_loop(0, blocks, send, 0)
    whole = pl.ds(0, blocks * ROWS)
    pltpu.make_async_copy(points_ref.at[whole], payload_ref.at[whole], sem).wait()


def pack_blocks(hil_dest, points, devices, capacity):
    return pl.pallas_call(
        functools.partial(pack_kernel, capacity),
        out_shape=jax.ShapeDtypeStruct((devices * capacity * ROWS, points.shape[1]), BF),
        in_specs=[SMEM, HBM],
        out_specs=HBM,
        scratch_shapes=[pltpu.SMEM((devices,), jnp.int32), pltpu.SemaphoreType.DMA],
        compiler_params=ROOM,
        cost_estimate=cost(0, 4 * points.size),
    )(hil_dest, points)


def order_kernel(counts_ref, order_ref, dest_ref, slot_ref, info_ref, span_ref, code):
    parents = counts_ref.shape[1]
    blocks = dest_ref.shape[1]
    counts = jnp.broadcast_to(counts_ref[...], (8, parents)).astype(F32)
    upper = jnp.where(iota((parents, parents), 0) <= iota((parents, parents), 1), 1.0, 0.0)
    starts = mm(counts.astype(BF), upper.astype(BF)) - counts
    coarse = jnp.floor(starts * (1.0 / 64.0))
    which = iota((8, parents), 0)
    fields = jnp.where(which == 0, coarse, jnp.where(which == 1, starts - 64.0 * coarse, counts))
    pick = jnp.where(iota((parents, parents), 0) == order_ref[...], 1.0, 0.0).astype(BF)
    ordered = mm(fields.astype(BF), pick).astype(jnp.int32)
    first = 64 * ordered[0:1] + ordered[1:2]
    length = ordered[2:3]
    span_ref[...] = jnp.where(which == 0, first, jnp.where(which == 1, first + length, length))
    both = 16 * first + length
    code[...] = jnp.zeros_like(code)
    code[0:1, :blocks] = dest_ref[...] * blocks + slot_ref[...]
    tile = jnp.concatenate(
        [both[:, i * 128 : (i + 1) * 128] for i in range(parents // 128)] + [code[...]], axis=0
    )
    for d in range(info_ref.shape[0]):
        info_ref[d] = tile


def order_tables(child_counts, parent_order, hil_dest, hil_slot, devices):
    parents = child_counts.shape[1]
    return pl.pallas_call(
        order_kernel,
        out_shape=(
            jax.ShapeDtypeStruct((devices, INFO, 128), jnp.int32),
            jax.ShapeDtypeStruct((8, parents), jnp.int32),
        ),
        in_specs=[VMEM] * 4,
        out_specs=(VMEM, VMEM),
        scratch_shapes=[pltpu.VMEM((INFO - parents // 128, 128), jnp.int32)],
        compiler_params=ROOM,
        cost_estimate=cost(32 * parents * parents, 8 * parents),
    )(child_counts, parent_order, hil_dest[None], hil_slot[None])


def seat_kernel(per_owner, source_ref, block_ref, info_ref, seat_ref, most_ref, owner, place, origin):
    blocks = owner.shape[0]
    parents = 128 * 8
    devices = info_ref.shape[0] // INFO
    which = iota((16, parents), 0)
    rank = iota((16, parents), 1)
    fields = jnp.where(which == 0, rank // per_owner, jnp.where(which == 1, rank % per_owner, 0))
    fields = fields.astype(F32).astype(BF)

    def one(v, _):
        source = source_ref[v]
        packed = info_ref[pl.ds(pl.multiple_of(source * INFO, INFO), 8), :]
        line = jnp.concatenate([packed[i : i + 1] for i in range(8)], axis=1)
        first = line // 16
        row = block_ref[v] * ROWS + iota((ROWS, parents), 0)
        inside = (row >= first) & (row < first + line % 16)
        found = mm(fields, jnp.where(inside, 1.0, 0.0).astype(BF), NT)
        owner[pl.ds(v, 1), :] = found[0:1]
        place[pl.ds(v, 1), :] = found[1:2]
        origin[pl.ds(v, 1), :] = jnp.full((1, ROWS), source, jnp.int32).astype(F32)
        return 0

    lax.fori_loop(0, blocks, one, 0)
    own = owner[...]
    own_place = place[...]
    run = own * per_owner + own_place
    opens = (iota((blocks, ROWS), 1) == 0) | (run != pltpu.roll(run, 1, 1))
    opened = jnp.where(opens, 1.0, 0.0)
    upper = jnp.where(iota((ROWS, ROWS), 0) <= iota((ROWS, ROWS), 1), 1.0, 0.0).astype(BF)
    every = jnp.ones((ROWS, ROWS), BF)
    before = jnp.where(iota((blocks, blocks), 1) < iota((blocks, blocks), 0), 1.0, 0.0).astype(BF)

    def count(e, carry):
        seat, most = carry
        here = own == e.astype(F32)
        marks = jnp.where(here, opened, 0.0).astype(BF)
        total = mm(marks, upper) + mm(before, mm(marks, every).astype(BF))
        return jnp.where(here, total - 1.0, seat), jnp.maximum(most, total)

    zero = jnp.zeros((blocks, ROWS), F32)
    seat, most = lax.fori_loop(0, devices, count, (zero, zero))
    seat_ref[...] = jnp.zeros_like(seat_ref)
    for i, value in enumerate((own, seat, opened * origin[...], opened * own_place)):
        for v in range(blocks):
            seat_ref[i : i + 1, v * ROWS : (v + 1) * ROWS] = value[v : v + 1]
    most_ref[...] = jnp.full((8, 128), jnp.max(most), F32)


def seat_rows(source, block, info, per_owner):
    blocks = source.shape[0]
    rows = blocks * ROWS
    return pl.pallas_call(
        functools.partial(seat_kernel, per_owner),
        out_shape=(jax.ShapeDtypeStruct((8, rows), F32), jax.ShapeDtypeStruct((8, 128), F32)),
        in_specs=[SMEM, SMEM, VMEM],
        out_specs=(VMEM, VMEM),
        scratch_shapes=[pltpu.VMEM((blocks, ROWS), F32)] * 3,
        compiler_params=ROOM,
        cost_estimate=cost(40 * rows * 1024, 8 * rows),
    )(source, block, info)


def attend_kernel(
    index_ref, low_ref, count_ref, ids_ref, w_ref, wo_ref, rows_ref, out_ref, x, qx, kx, vx, att, sems
):
    tiles, span = ids_ref.shape
    width = w_ref.shape[0]
    cols = HEAD_GROUP * HDIM
    groups = width // cols
    heads = width // HDIM
    per_tile = span // ROWS

    for t in range(tiles):
        for b in range(per_tile):
            s = t * per_tile + b
            pltpu.make_async_copy(
                rows_ref.at[pl.ds(pl.multiple_of(index_ref[s] * ROWS, ROWS), ROWS)],
                x.at[pl.ds(s * ROWS, ROWS)],
                sems.at[t],
            ).start()

    lane = iota((ROWS, 2 * cols), 1)
    of_head = [(lane // HDIM == h) | (lane >= cols) for h in range(HEAD_GROUP)]
    lane_out = lane % cols // HDIM
    for g in range(groups):
        vx[g, :, cols:] = jnp.ones((span, cols), BF)
    r_i = iota((cols, cols), 0)
    c_i = iota((cols, cols), 1)
    far = jnp.where((r_i != c_i) & (c_i < PATCHES), -FAR, 0.0).astype(BF)

    def tile(t, _):
        at = pl.ds(pl.multiple_of(t * span, span), span)
        pltpu.make_async_copy(rows_ref.at[pl.ds(0, span)], x.at[at], sems.at[t]).wait()
        tile_rows = x[at, :]
        same = ids_ref[pl.ds(t, 1), :] == iota((cols, span), 0)
        patch_hot = jnp.where(same, 1.0, 0.0).astype(BF)
        query = mm(tile_rows, w_ref[:, :width])
        keys = mm(w_ref[:, width : 2 * width], tile_rows, (((0,), (1,)), ((), ())))
        value = mm(tile_rows, w_ref[:, 2 * width :]).astype(BF)
        patch_far = mm(patch_hot, far, TN).astype(BF)
        for g in range(groups):
            some = slice(g * cols, (g + 1) * cols)
            qx[g, :, :cols] = query[:, some].astype(BF)
            qx[g, :, cols:] = patch_far
            kx[g, :cols, :] = keys[some].astype(BF)
            kx[g, cols:, :] = patch_hot
            vx[g, :, :cols] = value[:, some]
        query_most = jnp.max(jnp.abs(query), axis=0, keepdims=True)
        key_most = jnp.max(jnp.abs(keys), axis=1, keepdims=True)
        by_head = jnp.where(
            iota((heads, width), 1) // HDIM == iota((heads, width), 0), query_most, 0.0
        )
        bound = jnp.max(mm(by_head.astype(BF), jnp.broadcast_to(key_most, (width, 128)).astype(BF)))
        safe = bound * SCORE_SCALE < SCORE_SAFE

        def block(b, _):
            low = pl.multiple_of(low_ref[t * per_tile + b], ROWS)
            steps = count_ref[t * per_tile + b]
            here = pl.ds(pl.multiple_of(b * ROWS, ROWS), ROWS)

            def run(start, length, exact):
                scores = []
                for g in range(groups):
                    q = qx[g, here, :]
                    stacked = jnp.concatenate(
                        [jnp.where(of_head[h], q, jnp.zeros_like(q)) for h in range(HEAD_GROUP)],
                        axis=0,
                    )
                    scores.append(mm(stacked, kx[g, :, pl.ds(start, length)]))
                for g in range(groups):
                    level = scores[g] * SCORE_SCALE
                    if exact:
                        level = level - jnp.max(level, axis=1, keepdims=True)
                    weights = jnp.exp2(level).astype(BF)
                    mixed = mm(weights, vx[g, pl.ds(start, length), :])
                    mixed = mixed.reshape(HEAD_GROUP, ROWS, 2 * cols)
                    own = mixed[0]
                    for h in range(1, HEAD_GROUP):
                        own = jnp.where(lane_out == h, mixed[h], own)
                    att[here, g * cols : (g + 1) * cols] = (own[:, :cols] / own[:, cols:]).astype(BF)

            for i in range(span // WINDOW):
                pl.when(safe & (steps == i + 1))(
                    functools.partial(run, low, (i + 1) * WINDOW, False)
                )
            pl.when(jnp.logical_not(safe))(functools.partial(run, 0, span, True))
            return 0

        lax.fori_loop(0, per_tile, block, 0)
        out_ref[at, :] = (tile_rows.astype(F32) + mm(att[...], wo_ref[...])).astype(BF)
        return 0

    lax.fori_loop(0, tiles, tile, 0)


def attend(index, low, count, ids, w_qkv, w_out, rows):
    tiles, span = ids.shape
    width = rows.shape[1]
    cols = HEAD_GROUP * HDIM
    groups = width // cols
    pairs = tiles * span * span * HEAD_GROUP
    return pl.pallas_call(
        attend_kernel,
        out_shape=jax.ShapeDtypeStruct((tiles * span, width), BF),
        in_specs=[SMEM, SMEM, SMEM, VMEM, VMEM, VMEM, HBM],
        out_specs=VMEM,
        scratch_shapes=[
            pltpu.VMEM((tiles * span, width), BF),
            pltpu.VMEM((groups, span, 2 * cols), BF),
            pltpu.VMEM((groups, 2 * cols, span), BF),
            pltpu.VMEM((groups, span, 2 * cols), BF),
            pltpu.VMEM((span, width), BF),
            pltpu.SemaphoreType.DMA((tiles,)),
        ],
        compiler_params=ROOM,
        cost_estimate=cost(pairs * 1024, 4 * rows.size, pairs),
    )(index, low, count, ids, w_qkv, w_out, rows)


def sum_kernel(round_ref, seat_ref, most_ref, rows_ref, out_ref):
    chunk = out_ref.shape[0]
    first = SEATS * round_ref[0].astype(F32)
    owner = seat_ref[0:1, :]
    seat = seat_ref[1:2, :] - first
    seated = (seat >= 0.0) & (seat < float(SEATS))
    code = jnp.where(seated, owner * float(SEAT) + seat, -1.0).astype(jnp.int32)
    mine = iota((chunk, 1), 0) + pl.program_id(0) * chunk
    member = jnp.where(mine == code, 1.0, 0.0).astype(BF)
    sums = mm(member, rows_ref[...])
    tags = mm(seat_ref[...].astype(BF), member, NT)
    rounds = jnp.floor((most_ref[0:1, :] + (SEATS - 1.0)) / float(SEATS))
    line = iota((SEAT - SEATS, SEAT), 0)
    for d in range(chunk // SEAT):
        low = d * SEAT
        out_ref[low : low + SEATS, :] = sums[low : low + SEATS].astype(BF)
        origin = jnp.where(line == 0, tags[2:3, low : low + SEAT], jnp.where(line == 1, rounds, 0.0))
        place = jnp.where(line == 0, tags[3:4, low : low + SEAT], 0.0)
        out_ref[low + SEATS : low + SEAT, :] = jnp.concatenate([origin, place], axis=1).astype(BF)


def sum_runs(step, seats, most, rows, devices):
    count, width = rows.shape
    total = devices * SEAT
    chunk = 512
    fixed = lambda i: (0, 0)
    return pl.pallas_call(
        sum_kernel,
        grid=(total // chunk,),
        out_shape=jax.ShapeDtypeStruct((total, width), BF),
        in_specs=[
            SMEM,
            pl.BlockSpec((8, count), fixed),
            pl.BlockSpec((8, 128), fixed),
            pl.BlockSpec((count, width), fixed),
        ],
        out_specs=pl.BlockSpec((chunk, width), lambda i: (i, 0)),
        compiler_params=ROOM,
        cost_estimate=cost(2 * total * count * width, 4 * count * width),
    )(step, seats, most, rows)


def fold_kernel(per_owner, pieces_ref, before_ref, out_ref, target):
    step = pl.program_id(0)
    parents = out_ref.shape[0]
    chunk = pieces_ref.shape[0]

    @pl.when(step == 0)
    def _():
        out_ref[...] = before_ref[...]

    valid = iota((1, SEAT), 1) < SEATS
    for h in range(chunk // SEAT):
        tag = pieces_ref[h * SEAT + SEATS : (h + 1) * SEAT, :].astype(F32)[0:1]
        where = tag[:, :SEAT] * float(per_owner) + tag[:, SEAT:]
        target[0:1, h * SEAT : (h + 1) * SEAT] = jnp.where(valid, where, -1.0).astype(jnp.int32)
    member = jnp.where(iota((parents, 1), 0) == target[0:1, :], 1.0, 0.0).astype(BF)
    out_ref[...] += mm(member, pieces_ref[...])


def fold_pieces(pieces, before, per_owner):
    parents, width = before.shape
    chunk = min(2048, pieces.shape[0])
    fixed = lambda i: (0, 0)
    return pl.pallas_call(
        functools.partial(fold_kernel, per_owner),
        grid=(pieces.shape[0] // chunk,),
        out_shape=jax.ShapeDtypeStruct((parents, width), F32),
        in_specs=[
            pl.BlockSpec((chunk, width), lambda i: (i, 0)),
            pl.BlockSpec((parents, width), fixed),
        ],
        out_specs=pl.BlockSpec((parents, width), fixed),
        scratch_shapes=[pltpu.VMEM((8, chunk), jnp.int32)],
        compiler_params=ROOM,
        cost_estimate=cost(2 * parents * pieces.size, 4 * pieces.size),
    )(pieces, before)


def pool_kernel(
    in_ref, length_ref, w_ref, gain_ref, shift_ref, cot_ref, pooled_ref, back_ref, weight_ref, norm_ref, acc, sums
):
    step = pl.program_id(0)

    @pl.when(step == 0)
    def _():
        acc[...] = jnp.zeros_like(acc)
        sums[...] = jnp.zeros_like(sums)

    lengths = jnp.concatenate([length_ref[...]] * (in_ref.shape[1] // 128), axis=1)
    parent_in = (in_ref[...] / lengths).astype(BF)
    w_pool = w_ref[...]
    gain = gain_ref[...]
    projected = mm(parent_in, w_pool)
    centred = projected - jnp.mean(projected, axis=-1, keepdims=True)
    variance = jnp.mean(centred * centred, axis=-1, keepdims=True)
    inv_std = lax.rsqrt(variance + norm_eps)
    normed = centred * inv_std
    shifted = normed * gain + shift_ref[...]
    normal_cdf = 0.5 * (1.0 + lax.erf(shifted * inv_sqrt_two))
    pooled_ref[...] = (shifted * normal_cdf).astype(BF)
    grad_act = cot_ref[...].astype(F32) * (
        normal_cdf + shifted * jnp.exp(-0.5 * shifted * shifted) * inv_sqrt_tau
    )
    sums[0:1, :] += jnp.sum(grad_act * normed, axis=0, keepdims=True)
    sums[1:2, :] += jnp.sum(grad_act, axis=0, keepdims=True)
    scaled = grad_act * gain
    grad_proj = (
        (
            scaled
            - jnp.mean(scaled, axis=-1, keepdims=True)
            - normed * jnp.mean(scaled * normed, axis=-1, keepdims=True)
        )
        * inv_std
    ).astype(BF)
    acc[...] += mm(parent_in, grad_proj, TN)
    back_ref[...] = mm(grad_proj, w_pool, NT).astype(BF)

    @pl.when(step == pl.num_programs(0) - 1)
    def _():
        weight_ref[...] = acc[...].astype(BF)
        norm_ref[...] = sums[...]


def pool(parent_sum, length, w_pool, gain, shift, cotangent):
    parents, width = parent_sum.shape
    wide = w_pool.shape[1]
    chunk = 256
    fixed = lambda i: (0, 0)
    along = lambda i: (i, 0)
    return pl.pallas_call(
        pool_kernel,
        grid=(parents // chunk,),
        out_shape=(
            jax.ShapeDtypeStruct((parents, wide), BF),
            jax.ShapeDtypeStruct((parents, width), BF),
            jax.ShapeDtypeStruct((width, wide), BF),
            jax.ShapeDtypeStruct((8, wide), F32),
        ),
        in_specs=[
            pl.BlockSpec((chunk, width), along),
            pl.BlockSpec((chunk, 128), along),
            pl.BlockSpec((width, wide), fixed),
            pl.BlockSpec((1, wide), fixed),
            pl.BlockSpec((1, wide), fixed),
            pl.BlockSpec((chunk, wide), along),
        ],
        out_specs=(
            pl.BlockSpec((chunk, wide), along),
            pl.BlockSpec((chunk, width), along),
            pl.BlockSpec((width, wide), fixed),
            pl.BlockSpec((8, wide), fixed),
        ),
        scratch_shapes=[pltpu.VMEM((width, wide), F32), pltpu.VMEM((8, wide), F32)],
        compiler_params=ROOM,
        cost_estimate=cost(6 * parents * width * wide, 8 * parents * wide, 2 * parents * wide),
    )(parent_sum, length, w_pool, gain, shift, cotangent)


def spread_kernel(span_ref, grad_ref, out_ref, share):
    step = pl.program_id(0)
    chunk = out_ref.shape[0]
    parents, width = share.shape

    @pl.when(step == 0)
    def _():
        pick = jnp.where(iota((8, width), 0) == 2, 1.0, 0.0).astype(BF)
        lengths = mm(jnp.minimum(span_ref[...], 64).astype(F32).astype(BF), pick, TN)
        share[...] = (grad_ref[...].astype(F32) / lengths).astype(BF)

    row = iota((chunk, parents), 0) + step * chunk
    inside = (row >= span_ref[0:1, :]) & (row < span_ref[1:2, :])
    out_ref[...] = mm(jnp.where(inside, 1.0, 0.0).astype(BF), share[...]).astype(BF)


def spread_grads(span, grad_back, rows):
    parents, width = grad_back.shape
    chunk = 512
    fixed = lambda i: (0, 0)
    return pl.pallas_call(
        spread_kernel,
        grid=(rows // chunk,),
        out_shape=jax.ShapeDtypeStruct((rows, width), BF),
        in_specs=[
            pl.BlockSpec((8, parents), fixed),
            pl.BlockSpec((parents, width), fixed),
        ],
        out_specs=pl.BlockSpec((chunk, width), lambda i: (i, 0)),
        scratch_shapes=[pltpu.VMEM((parents, width), BF)],
        compiler_params=ROOM,
        cost_estimate=cost(2 * rows * parents * width, 4 * rows * width),
    )(span, grad_back)


def swap(parts):
    return lax.all_to_all(parts, "pts", split_axis=0, concat_axis=0, tiled=True)


def exchange(rows, devices):
    return swap(rows.reshape(devices, rows.shape[0] // devices, rows.shape[1])).reshape(rows.shape)


def received_index(codes, blocks, capacity):
    devices = codes.shape[0]
    mine = codes // blocks == lax.axis_index("pts")
    slots = codes % blocks
    lane = jnp.arange(blocks)
    rank = jnp.sum(mine[:, None, :] & (lane[None, :] < lane[:, None])[None], axis=2)
    index = jnp.arange(devices)[:, None] * capacity + rank
    both = index * blocks + lane[None, :]
    hit = mine[:, :, None] & (slots[:, :, None] == lane[None, None, :])
    both = jnp.sum(jnp.where(hit, both[:, :, None], 0), axis=(0, 1)).astype(jnp.int32)
    return both // blocks, both % blocks


def key_windows(patch_ids):
    tiles, span = patch_ids.shape
    patch = jnp.arange(PATCHES + 1)
    starts = jnp.sum(patch_ids[:, None, :] < patch[None, :, None], axis=2)
    by_block = patch_ids.reshape(tiles, span // ROWS, ROWS)
    first, last = by_block[:, :, 0], by_block[:, :, -1]
    pick = lambda which: jnp.sum(
        jnp.where(which[:, :, None] == patch[None, None, :], starts[:, None, :], 0), axis=2
    )
    low = pick(first) // ROWS * ROWS
    count = (pick(last + 1) - low + WINDOW - 1) // WINDOW
    low = jnp.minimum(low, span - count * WINDOW)
    return low.reshape(-1).astype(jnp.int32), count.reshape(-1).astype(jnp.int32)


def local(
    points,
    hil_dest,
    hil_slot,
    patch_ids,
    child_counts,
    parent_order,
    w_qkv,
    w_out,
    w_pool,
    norm_gain,
    norm_shift,
    cotangent,
):
    devices = lax.axis_size("pts")
    blocks = hil_dest.shape[0]
    rows, width = points.shape
    wide = w_pool.shape[1]
    parents = child_counts.shape[1]
    per_owner = parents // devices
    capacity = (blocks + devices - 1) // devices

    info, span = order_tables(child_counts, parent_order, hil_dest, hil_slot, devices)
    info = swap(info)
    payload = pack_blocks(hil_dest, points, devices, capacity)
    received = exchange(payload, devices)
    index, block = received_index(info[:, parents // 128, :blocks], blocks, capacity)
    seats, most = seat_rows(
        index // capacity, block, info.reshape(devices * INFO, 128), per_owner
    )
    low, count = key_windows(patch_ids)
    lengths = lax.dynamic_slice_in_dim(
        info[:, : parents // 128].reshape(devices, parents),
        lax.axis_index("pts") * per_owner,
        per_owner,
        axis=1,
    ).reshape(parents, 1) % 16
    lengths = jnp.broadcast_to(lengths.astype(F32), (parents, 128))
    index, low, count, seats, most, lengths = lax.optimization_barrier(
        (index, low, count, seats, most, lengths)
    )
    mixed = attend(index, low, count, patch_ids, w_qkv, w_out, received)

    def turn(step, before):
        sent = sum_runs(step.reshape(1), seats, most, mixed, devices)
        pieces = exchange(sent, devices)
        needed = jnp.max(pieces.reshape(devices, SEAT, width)[:, SEATS + 1, 0].astype(F32))
        return needed.astype(jnp.int32), fold_pieces(pieces, before, per_owner)

    rounds, parent_sum = turn(jnp.int32(0), jnp.zeros((parents, width), F32))
    _, parent_sum = lax.while_loop(
        lambda carry: carry[0] < rounds,
        lambda carry: (carry[0] + 1, turn(carry[0], carry[1])[1]),
        (jnp.int32(1), parent_sum),
    )
    pooled, back, weight, norm = pool(
        parent_sum, lengths, w_pool, norm_gain[None], norm_shift[None], cotangent
    )
    norm_high = norm.astype(BF)
    norm_low = (norm - norm_high.astype(F32)).astype(BF)
    norm_parts = jnp.concatenate([norm_high[:2], norm_low[:2]], axis=0).reshape(1, -1, width)
    outgoing = jnp.concatenate(
        [
            back.reshape(devices, -1, width),
            weight.reshape(devices, -1, width),
            jnp.broadcast_to(norm_parts, (devices,) + norm_parts.shape[1:]),
        ],
        axis=1,
    )
    arrived = swap(outgoing)
    weight_rows = width * wide // width // devices
    grad_back = arrived[:, :per_owner].reshape(parents, width)
    weight_sum = jnp.sum(arrived[:, per_owner : per_owner + weight_rows].astype(F32), axis=0)
    norm_sum = jnp.sum(arrived[:, per_owner + weight_rows :].astype(F32), axis=0)
    norm_sum = norm_sum.reshape(4, wide)
    grad_norm = norm_sum[:2] + norm_sum[2:]
    shared = jnp.broadcast_to(weight_sum.astype(BF)[None], (devices,) + weight_sum.shape)
    grad_weight = swap(shared).reshape(width, wide).astype(F32)
    grad_points = spread_grads(span, grad_back, rows)
    return (pooled, grad_points, grad_weight, grad_norm)


def solution(mesh):
    in_specs = (
        P(("grp", "pts"), None),
        P(("grp", "pts")),
        P(("grp", "pts")),
        P(("grp", "pts"), None),
        P(("grp", "pts"), None),
        P(("grp", "pts"), None),
        P(),
        P(),
        P(),
        P(),
        P(),
        P(("grp", "pts"), None),
    )
    out_specs = (P(("grp", "pts"), None), P(("grp", "pts"), None), P("grp", None), P("grp", None))
    return jax.shard_map(local, mesh=mesh, in_specs=in_specs, out_specs=out_specs, check_vma=False)
```

```python
import functools
import math

import jax
import jax.numpy as jnp
from jax import lax
from jax.experimental import pallas as pl
from jax.experimental.pallas import tpu as pltpu
from jax.sharding import PartitionSpec as P

HDIM = 16
HEAD_GROUP = 8
ROWS = 128
SEAT = 128
SEATS = 112
INFO = 16
ALIGN = 16
CHUNK = 512
FIELDS = 6
WINDOW = 256
PATCHES = 4
FAR = 2.0**100
SCORE_SCALE = HDIM**-0.5 * math.log2(math.e)
SCORE_SAFE = 98.0

inv_sqrt_two = 0.7071067811865476
inv_sqrt_tau = 0.3989422804014327
norm_eps = 1e-05

BF = jnp.bfloat16
F32 = jnp.float32
NT = (((1,), (1,)), ((), ()))
TN = (((0,), (0,)), ((), ()))
VMEM = pl.BlockSpec(memory_space=pltpu.VMEM)
HBM = pl.BlockSpec(memory_space=pltpu.HBM)
SMEM = pl.BlockSpec(memory_space=pltpu.SMEM)
ANY = pl.BlockSpec(memory_space=pl.ANY)
ROOM = pltpu.CompilerParams(vmem_limit_bytes=48 << 20)
FULL = pltpu.CompilerParams(vmem_limit_bytes=60 << 20)


def iota(shape, dim):
    return lax.broadcasted_iota(jnp.int32, shape, dim)


def mm(a, b, dims=(((1,), (0,)), ((), ()))):
    return lax.dot_general(a, b, dims, preferred_element_type=F32)


def cost(flops, bytes_accessed, transcendentals=0):
    return pl.CostEstimate(
        flops=int(flops), bytes_accessed=int(bytes_accessed), transcendentals=int(transcendentals)
    )


def front_kernel(
    capacity,
    dest_ref,
    counts_ref,
    order_ref,
    dest_row_ref,
    slot_row_ref,
    points_ref,
    payload_ref,
    info_ref,
    span_ref,
    used,
    sem,
):
    blocks = dest_ref.shape[0]

    def clear(d, _):
        used[d] = 0
        return 0

    lax.fori_loop(0, used.shape[0], clear, 0)

    def send(b, _):
        d = dest_ref[b]
        place = d * capacity + used[d]
        used[d] = used[d] + 1
        pltpu.make_async_copy(
            points_ref.at[pl.ds(pl.multiple_of(b * ROWS, ROWS), ROWS)],
            payload_ref.at[pl.ds(pl.multiple_of(place * ROWS, ROWS), ROWS)],
            sem,
        ).start()
        return 0

    lax.fori_loop(0, blocks, send, 0)

    parents = counts_ref.shape[1]
    counts = jnp.broadcast_to(counts_ref[...], (8, parents)).astype(F32)
    upper = jnp.where(iota((parents, parents), 0) <= iota((parents, parents), 1), 1.0, 0.0)
    starts = mm(counts.astype(BF), upper.astype(BF)) - counts
    coarse = jnp.floor(starts * (1.0 / 64.0))
    which = iota((8, parents), 0)
    fields = jnp.where(which == 0, coarse, jnp.where(which == 1, starts - 64.0 * coarse, counts))
    pick = jnp.where(iota((parents, parents), 0) == order_ref[...], 1.0, 0.0).astype(BF)
    ordered = mm(fields.astype(BF), pick).astype(jnp.int32)
    first = 64 * ordered[0:1] + ordered[1:2]
    length = ordered[2:3]
    span_ref[...] = jnp.where(which == 0, first, jnp.where(which == 1, first + length, length))
    both = 16 * first + length
    lines = parents // 128
    for i in range(lines):
        info_ref[i : i + 1, :] = both[:, i * 128 : (i + 1) * 128]
    info_ref[lines:, :] = jnp.zeros((INFO - lines, 128), jnp.int32)
    info_ref[lines : lines + 1, :blocks] = dest_row_ref[...] * blocks + slot_row_ref[...]

    whole = pl.ds(0, blocks * ROWS)
    pltpu.make_async_copy(points_ref.at[whole], payload_ref.at[whole], sem).wait()


def front(child_counts, parent_order, hil_dest, hil_slot, points, devices, capacity):
    parents = child_counts.shape[1]
    return pl.pallas_call(
        functools.partial(front_kernel, capacity),
        out_shape=(
            jax.ShapeDtypeStruct((devices * capacity * ROWS, points.shape[1]), BF),
            jax.ShapeDtypeStruct((INFO, 128), jnp.int32),
            jax.ShapeDtypeStruct((8, parents), jnp.int32),
        ),
        in_specs=[SMEM, VMEM, VMEM, VMEM, VMEM, HBM],
        out_specs=(HBM, VMEM, VMEM),
        scratch_shapes=[pltpu.SMEM((devices,), jnp.int32), pltpu.SemaphoreType.DMA],
        compiler_params=FULL,
        cost_estimate=cost(32 * parents * parents, 4 * points.size),
    )(hil_dest, child_counts, parent_order, hil_dest[None], hil_slot[None], points)


def seat_kernel(
    per_owner,
    source_ref,
    entry_ref,
    block_ref,
    info_ref,
    table_ref,
    local_ref,
    base_ref,
    most_ref,
    owner,
    place,
    origin,
    seats,
):
    blocks = owner.shape[0]
    parents = 128 * 8
    devices = info_ref.shape[0] // INFO
    which = iota((16, parents), 0)
    rank = iota((16, parents), 1)
    fields = jnp.where(which == 0, rank // per_owner, jnp.where(which == 1, rank % per_owner, 0))
    fields = fields.astype(F32).astype(BF)

    def one(v, _):
        entry = entry_ref[v]
        packed = info_ref[pl.ds(pl.multiple_of(entry * INFO, INFO), 8), :]
        line = jnp.concatenate([packed[i : i + 1] for i in range(8)], axis=1)
        first = line // 16
        row = block_ref[v] * ROWS + iota((ROWS, parents), 0)
        inside = (row >= first) & (row < first + line % 16)
        found = mm(fields, jnp.where(inside, 1.0, 0.0).astype(BF), NT)
        owner[pl.ds(v, 1), :] = found[0:1]
        place[pl.ds(v, 1), :] = found[1:2]
        origin[pl.ds(v, 1), :] = jnp.full((1, ROWS), source_ref[v], jnp.int32).astype(F32)
        return 0

    lax.fori_loop(0, blocks, one, 0)
    own = owner[...]
    run = own * per_owner + place[...]
    opens = (iota((blocks, ROWS), 1) == 0) | (run != pltpu.roll(run, 1, 1))
    opened = jnp.where(opens, 1.0, 0.0)
    upper = jnp.where(iota((ROWS, ROWS), 0) <= iota((ROWS, ROWS), 1), 1.0, 0.0).astype(BF)
    every = jnp.ones((ROWS, ROWS), BF)
    before = jnp.where(iota((blocks, blocks), 1) < iota((blocks, blocks), 0), 1.0, 0.0).astype(BF)
    local_ref[...] = (mm(opened.astype(BF), upper) - 1.0).astype(jnp.int32)

    def count(e, carry):
        seat, most = carry
        here = own == e.astype(F32)
        marks = jnp.where(here, opened, 0.0).astype(BF)
        total = mm(marks, upper) + mm(before, mm(marks, every).astype(BF))
        return jnp.where(here, total - 1.0, seat), jnp.maximum(most, total)

    zero = jnp.zeros((blocks, ROWS), F32)
    seat, most = lax.fori_loop(0, devices, count, (zero, zero))
    seats[...] = seat
    most_ref[...] = jnp.full((8, 128), jnp.max(most), F32)
    table_ref[...] = jnp.zeros_like(table_ref)
    field = iota((ROWS, ROWS), 0)

    def lay(v, base):
        base = pl.multiple_of(base, ALIGN)
        base_ref[v] = base
        at = pl.ds(v, 1)
        local = local_ref[at, :]
        seat = seats[at, :]
        coarse = jnp.floor(seat * (1.0 / 64.0))
        lines = (owner[at, :], coarse, seat - 64.0 * coarse, origin[at, :], place[at, :])
        values = jnp.ones((ROWS, ROWS), F32)
        for i, line in enumerate(lines):
            values = jnp.where(field == i, line, values)
        previous = jnp.where(iota((1, ROWS), 1) == 0, -1, pltpu.roll(local, 1, 1))
        begins = (field == local) & (local != previous)
        found = mm(jnp.where(begins, 1.0, 0.0).astype(BF), values.astype(BF), NT)
        table_ref[pl.ds(base, ROWS), :] = found.astype(BF)
        return base + (jnp.max(local) + ALIGN) // ALIGN * ALIGN

    base_ref[blocks] = lax.fori_loop(0, blocks, lay, 0)


def seat_rows(source, entry, block, info, per_owner):
    blocks = source.shape[0]
    rows = blocks * ROWS
    return pl.pallas_call(
        functools.partial(seat_kernel, per_owner),
        out_shape=(
            jax.ShapeDtypeStruct((rows + CHUNK, 128), BF),
            jax.ShapeDtypeStruct((blocks, ROWS), jnp.int32),
            jax.ShapeDtypeStruct((blocks + 1,), jnp.int32),
            jax.ShapeDtypeStruct((8, 128), F32),
        ),
        in_specs=[SMEM, SMEM, SMEM, VMEM],
        out_specs=(VMEM, VMEM, SMEM, VMEM),
        scratch_shapes=[pltpu.VMEM((blocks, ROWS), F32)] * 4,
        compiler_params=ROOM,
        cost_estimate=cost(40 * rows * 1024, 8 * rows),
    )(source, entry, block, info)


def plan_kernel(round_ref, base_ref, most_ref, table_ref, code_ref, tags_ref, found):
    first = (SEATS * round_ref[0]).astype(F32)
    chunks = (base_ref[base_ref.shape[0] - 1] + CHUNK - 1) // CHUNK
    total = tags_ref.shape[1]
    pick = jnp.where(iota((16, 128), 0) == iota((16, 128), 1), 1.0, 0.0).astype(BF)
    base = pl.program_id(0) * total
    found[...] = jnp.zeros_like(found)

    def step(c, _):
        at = pl.ds(pl.multiple_of(c * CHUNK, CHUNK), CHUNK)
        lines = mm(pick, table_ref[at, :], NT)
        seat = 64.0 * lines[1:2] + lines[2:3] - first
        seated = (lines[5:6] > 0.5) & (seat >= 0.0) & (seat < float(SEATS))
        code = jnp.where(seated, lines[0:1] * float(SEAT) + seat, -1.0).astype(jnp.int32)
        code_ref[:, at] = jnp.broadcast_to(code, (8, CHUNK))
        member = jnp.where(iota((total, 1), 0) + base == code, 1.0, 0.0).astype(BF)
        found[...] += mm(lines.astype(BF), member, NT)
        return 0

    lax.fori_loop(0, chunks, step, 0)
    rounds = jnp.floor((jnp.max(most_ref[...]) + (SEATS - 1.0)) * (1.0 / SEATS) + 1e-3)
    line = iota((8, total), 0)
    tags_ref[...] = jnp.where(
        line == 0, found[3:4, :], jnp.where(line == 1, found[4:5, :], rounds)
    )


def plan_seats(step, base, most, table, devices):
    total = devices * SEAT
    part = min(2048, total)
    return pl.pallas_call(
        plan_kernel,
        grid=(total // part,),
        out_shape=(
            jax.ShapeDtypeStruct((8, table.shape[0]), jnp.int32),
            jax.ShapeDtypeStruct((8, total), F32),
        ),
        in_specs=[SMEM, SMEM, VMEM, VMEM],
        out_specs=(
            pl.BlockSpec((8, table.shape[0]), lambda i: (0, 0)),
            pl.BlockSpec((8, part), lambda i: (0, i)),
        ),
        scratch_shapes=[pltpu.VMEM((16, part), F32)],
        compiler_params=ROOM,
        cost_estimate=cost(64 * total * table.shape[0], 4 * table.size),
    )(step, base, most, table)


def attend_kernel(
    index_ref,
    low_ref,
    count_ref,
    base_ref,
    local_ref,
    ids_ref,
    w_ref,
    wo_ref,
    rows_ref,
    out_ref,
    x,
    qx,
    kx,
    vx,
    att,
    sems,
):
    tiles, span = ids_ref.shape
    width = w_ref.shape[0]
    cols = HEAD_GROUP * HDIM
    groups = width // cols
    heads = width // HDIM
    per_tile = span // ROWS

    for t in range(tiles):
        for b in range(per_tile):
            s = t * per_tile + b
            pltpu.make_async_copy(
                rows_ref.at[pl.ds(pl.multiple_of(index_ref[s] * ROWS, ROWS), ROWS)],
                x.at[pl.ds(s * ROWS, ROWS)],
                sems.at[t],
            ).start()

    out_ref[...] = jnp.zeros_like(out_ref)
    lane = iota((ROWS, 2 * cols), 1)
    of_head = [(lane // HDIM == h) | (lane >= cols) for h in range(HEAD_GROUP)]
    lane_out = lane % cols // HDIM
    for g in range(groups):
        vx[g, :, cols:] = jnp.ones((span, cols), BF)
    r_i = iota((cols, cols), 0)
    c_i = iota((cols, cols), 1)
    far = jnp.where((r_i != c_i) & (c_i < PATCHES), -FAR, 0.0).astype(BF)

    def tile(t, _):
        at = pl.ds(pl.multiple_of(t * span, span), span)
        pltpu.make_async_copy(rows_ref.at[pl.ds(0, span)], x.at[at], sems.at[t]).wait()
        tile_rows = x[at, :]
        same = ids_ref[pl.ds(t, 1), :] == iota((cols, span), 0)
        patch_hot = jnp.where(same, 1.0, 0.0).astype(BF)
        query = mm(tile_rows, w_ref[:, :width])
        keys = mm(w_ref[:, width : 2 * width], tile_rows, (((0,), (1,)), ((), ())))
        value = mm(tile_rows, w_ref[:, 2 * width :]).astype(BF)
        patch_far = mm(patch_hot, far, TN).astype(BF)
        for g in range(groups):
            some = slice(g * cols, (g + 1) * cols)
            qx[g, :, :cols] = query[:, some].astype(BF)
            qx[g, :, cols:] = patch_far
            kx[g, :cols, :] = keys[some].astype(BF)
            kx[g, cols:, :] = patch_hot
            vx[g, :, :cols] = value[:, some]
        query_most = jnp.max(jnp.abs(query), axis=0, keepdims=True)
        key_most = jnp.max(jnp.abs(keys), axis=1, keepdims=True)
        by_head = jnp.where(
            iota((heads, width), 1) // HDIM == iota((heads, width), 0), query_most, 0.0
        )
        bound = jnp.max(mm(by_head.astype(BF), jnp.broadcast_to(key_most, (width, 128)).astype(BF)))
        safe = bound * SCORE_SCALE < SCORE_SAFE

        def block(b, _):
            low = pl.multiple_of(low_ref[t * per_tile + b], ROWS)
            steps = count_ref[t * per_tile + b]
            here = pl.ds(pl.multiple_of(b * ROWS, ROWS), ROWS)

            def run(start, length, exact):
                scores = []
                for g in range(groups):
                    q = qx[g, here, :]
                    stacked = jnp.concatenate(
                        [jnp.where(of_head[h], q, jnp.zeros_like(q)) for h in range(HEAD_GROUP)],
                        axis=0,
                    )
                    scores.append(mm(stacked, kx[g, :, pl.ds(start, length)]))
                for g in range(groups):
                    level = scores[g] * SCORE_SCALE
                    if exact:
                        level = level - jnp.max(level, axis=1, keepdims=True)
                    weights = jnp.exp2(level).astype(BF)
                    mixed = mm(weights, vx[g, pl.ds(start, length), :])
                    mixed = mixed.reshape(HEAD_GROUP, ROWS, 2 * cols)
                    own = mixed[0]
                    for h in range(1, HEAD_GROUP):
                        own = jnp.where(lane_out == h, mixed[h], own)
                    att[here, g * cols : (g + 1) * cols] = (own[:, :cols] / own[:, cols:]).astype(BF)

            for i in range(span // WINDOW):
                pl.when(safe & (steps == i + 1))(
                    functools.partial(run, low, (i + 1) * WINDOW, False)
                )
            pl.when(jnp.logical_not(safe))(functools.partial(run, 0, span, True))
            return 0

        lax.fori_loop(0, per_tile, block, 0)
        mixed = (tile_rows.astype(F32) + mm(att[...], wo_ref[...])).astype(BF)
        for b in range(per_tile):
            s = t * per_tile + b
            run = jnp.where(iota((ROWS, ROWS), 0) == local_ref[pl.ds(s, 1), :], 1.0, 0.0)
            sums = mm(run.astype(BF), mixed[b * ROWS : (b + 1) * ROWS])
            out_ref[pl.ds(pl.multiple_of(base_ref[s], ALIGN), ROWS), :] = sums.astype(BF)
        return 0

    lax.fori_loop(0, tiles, tile, 0)


def attend(index, low, count, base, local, ids, w_qkv, w_out, rows):
    tiles, span = ids.shape
    width = rows.shape[1]
    cols = HEAD_GROUP * HDIM
    groups = width // cols
    pairs = tiles * span * span * HEAD_GROUP
    return pl.pallas_call(
        attend_kernel,
        out_shape=jax.ShapeDtypeStruct((tiles * span + CHUNK, width), BF),
        in_specs=[SMEM, SMEM, SMEM, SMEM, VMEM, VMEM, VMEM, VMEM, HBM],
        out_specs=VMEM,
        scratch_shapes=[
            pltpu.VMEM((tiles * span, width), BF),
            pltpu.VMEM((groups, span, 2 * cols), BF),
            pltpu.VMEM((groups, 2 * cols, span), BF),
            pltpu.VMEM((groups, span, 2 * cols), BF),
            pltpu.VMEM((span, width), BF),
            pltpu.SemaphoreType.DMA((tiles,)),
        ],
        compiler_params=ROOM,
        cost_estimate=cost(pairs * 1024, 4 * rows.size, pairs),
    )(index, low, count, base, local, ids, w_qkv, w_out, rows)


def route_kernel(base_ref, code_ref, tags_ref, sums_ref, out_ref, acc):
    total = out_ref.shape[0]
    chunks = (base_ref[base_ref.shape[0] - 1] + CHUNK - 1) // CHUNK
    seat = iota((total, 1), 0) + pl.program_id(0) * total
    acc[...] = jnp.zeros_like(acc)

    def step(c, _):
        at = pl.ds(pl.multiple_of(c * CHUNK, CHUNK), CHUNK)
        member = jnp.where(seat == code_ref[0:1, at], 1.0, 0.0).astype(BF)
        acc[...] += mm(member, sums_ref[at, :])
        return 0

    lax.fori_loop(0, chunks, step, 0)
    line = iota((SEAT - SEATS, SEAT), 0)
    for d in range(total // SEAT):
        low = d * SEAT
        here = slice(low, low + SEAT)
        out_ref[low : low + SEATS, :] = acc[low : low + SEATS, :].astype(BF)
        origin = jnp.where(
            line == 0, tags_ref[0:1, here], jnp.where(line == 1, tags_ref[2:3, here], 0.0)
        )
        place = jnp.where(line == 0, tags_ref[1:2, here], 0.0)
        out_ref[low + SEATS : low + SEAT, :] = jnp.concatenate([origin, place], axis=1).astype(BF)


def route_sums(base, code, tags, sums):
    count, width = sums.shape
    total = tags.shape[1]
    part = min(2048, total)
    return pl.pallas_call(
        route_kernel,
        grid=(total // part,),
        out_shape=jax.ShapeDtypeStruct((total, width), BF),
        in_specs=[
            SMEM,
            VMEM,
            pl.BlockSpec((8, part), lambda i: (0, i)),
            VMEM,
        ],
        out_specs=pl.BlockSpec((part, width), lambda i: (i, 0)),
        scratch_shapes=[pltpu.VMEM((part, width), F32)],
        compiler_params=ROOM,
        cost_estimate=cost(total * count * width, 4 * count * width),
    )(base, code, tags, sums)


def seat_targets(per_owner, pieces_ref, target):
    valid = iota((1, SEAT), 1) < SEATS
    for h in range(pieces_ref.shape[0] // SEAT):
        tag = pieces_ref[h * SEAT + SEATS : (h + 1) * SEAT, :].astype(F32)[0:1]
        where = tag[:, :SEAT] * float(per_owner) + tag[:, SEAT:]
        target[0:1, h * SEAT : (h + 1) * SEAT] = jnp.where(valid, where, -1.0).astype(jnp.int32)


def fold_kernel(per_owner, pieces_ref, before_ref, out_ref, target):
    step = pl.program_id(0)
    parents = out_ref.shape[0]
    chunk = pieces_ref.shape[0]

    @pl.when(step == 0)
    def _():
        out_ref[...] = before_ref[...]

    seat_targets(per_owner, pieces_ref, target)
    member = jnp.where(iota((parents, 1), 0) == target[0:1, :], 1.0, 0.0).astype(BF)
    out_ref[...] += mm(member, pieces_ref[...])


def fold_pieces(pieces, before, per_owner):
    parents, width = before.shape
    chunk = min(2048, pieces.shape[0])
    fixed = lambda i: (0, 0)
    return pl.pallas_call(
        functools.partial(fold_kernel, per_owner),
        grid=(pieces.shape[0] // chunk,),
        out_shape=jax.ShapeDtypeStruct((parents, width), F32),
        in_specs=[
            pl.BlockSpec((chunk, width), lambda i: (i, 0)),
            pl.BlockSpec((parents, width), fixed),
        ],
        out_specs=pl.BlockSpec((parents, width), fixed),
        scratch_shapes=[pltpu.VMEM((8, chunk), jnp.int32)],
        compiler_params=ROOM,
        cost_estimate=cost(2 * parents * pieces.size, 4 * pieces.size),
    )(pieces, before)


def pool_kernel(
    per_owner,
    pieces_ref,
    more_ref,
    length_ref,
    w_ref,
    gain_ref,
    shift_ref,
    cot_ref,
    pooled_ref,
    back_ref,
    weight_ref,
    norm_ref,
    acc,
    sums,
    target,
):
    step = pl.program_id(0)

    @pl.when(step == 0)
    def _():
        acc[...] = jnp.zeros_like(acc)
        sums[...] = jnp.zeros_like(sums)
        seat_targets(per_owner, pieces_ref, target)

    chunk, width = more_ref.shape
    total = more_ref[...]
    parent = iota((chunk, 1), 0) + step * chunk
    part = min(2048, pieces_ref.shape[0])
    for low in range(0, pieces_ref.shape[0], part):
        member = jnp.where(parent == target[0:1, low : low + part], 1.0, 0.0).astype(BF)
        total = total + mm(member, pieces_ref[low : low + part, :])
    lengths = jnp.concatenate([length_ref[...]] * (width // 128), axis=1)
    parent_in = (total / lengths).astype(BF)
    w_pool = w_ref[...]
    gain = gain_ref[...]
    projected = mm(parent_in, w_pool)
    centred = projected - jnp.mean(projected, axis=-1, keepdims=True)
    variance = jnp.mean(centred * centred, axis=-1, keepdims=True)
    inv_std = lax.rsqrt(variance + norm_eps)
    normed = centred * inv_std
    shifted = normed * gain + shift_ref[...]
    normal_cdf = 0.5 * (1.0 + lax.erf(shifted * inv_sqrt_two))
    pooled_ref[...] = (shifted * normal_cdf).astype(BF)
    grad_act = cot_ref[...].astype(F32) * (
        normal_cdf + shifted * jnp.exp(-0.5 * shifted * shifted) * inv_sqrt_tau
    )
    sums[0:1, :] += jnp.sum(grad_act * normed, axis=0, keepdims=True)
    sums[1:2, :] += jnp.sum(grad_act, axis=0, keepdims=True)
    scaled = grad_act * gain
    grad_proj = (
        (
            scaled
            - jnp.mean(scaled, axis=-1, keepdims=True)
            - normed * jnp.mean(scaled * normed, axis=-1, keepdims=True)
        )
        * inv_std
    ).astype(BF)
    acc[...] += mm(parent_in, grad_proj, TN)
    back_ref[...] = mm(grad_proj, w_pool, NT).astype(BF)

    @pl.when(step == pl.num_programs(0) - 1)
    def _():
        weight_ref[...] = acc[...].astype(BF)
        norm_ref[...] = sums[...]


def pool(pieces, more, length, w_pool, gain, shift, cotangent):
    parents, width = more.shape
    wide = w_pool.shape[1]
    chunk = 256
    fixed = lambda i: (0, 0)
    along = lambda i: (i, 0)
    return pl.pallas_call(
        functools.partial(pool_kernel, parents * SEAT // pieces.shape[0]),
        grid=(parents // chunk,),
        out_shape=(
            jax.ShapeDtypeStruct((parents, wide), BF),
            jax.ShapeDtypeStruct((parents, width), BF),
            jax.ShapeDtypeStruct((width, wide), BF),
            jax.ShapeDtypeStruct((8, wide), F32),
        ),
        in_specs=[
            pl.BlockSpec(pieces.shape, fixed),
            pl.BlockSpec((chunk, width), along),
            pl.BlockSpec((chunk, 128), along),
            pl.BlockSpec((width, wide), fixed),
            pl.BlockSpec((1, wide), fixed),
            pl.BlockSpec((1, wide), fixed),
            pl.BlockSpec((chunk, wide), along),
        ],
        out_specs=(
            pl.BlockSpec((chunk, wide), along),
            pl.BlockSpec((chunk, width), along),
            pl.BlockSpec((width, wide), fixed),
            pl.BlockSpec((8, wide), fixed),
        ),
        scratch_shapes=[
            pltpu.VMEM((width, wide), F32),
            pltpu.VMEM((8, wide), F32),
            pltpu.VMEM((8, pieces.shape[0]), jnp.int32),
        ],
        compiler_params=FULL,
        cost_estimate=cost(6 * parents * width * wide, 8 * parents * wide, 2 * parents * wide),
    )(pieces, more, length, w_pool, gain, shift, cotangent)


def spread_kernel(span_ref, grad_ref, out_ref, share):
    step = pl.program_id(0)
    chunk = out_ref.shape[0]
    parents, width = share.shape

    @pl.when(step == 0)
    def _():
        pick = jnp.where(iota((8, width), 0) == 2, 1.0, 0.0).astype(BF)
        lengths = mm(jnp.minimum(span_ref[...], 64).astype(F32).astype(BF), pick, TN)
        share[...] = (grad_ref[...].astype(F32) / lengths).astype(BF)

    row = iota((chunk, parents), 0) + step * chunk
    inside = (row >= span_ref[0:1, :]) & (row < span_ref[1:2, :])
    out_ref[...] = mm(jnp.where(inside, 1.0, 0.0).astype(BF), share[...]).astype(BF)


def spread_grads(span, grad_back, rows):
    parents, width = grad_back.shape
    chunk = 512
    fixed = lambda i: (0, 0)
    return pl.pallas_call(
        spread_kernel,
        grid=(rows // chunk,),
        out_shape=jax.ShapeDtypeStruct((rows, width), BF),
        in_specs=[
            pl.BlockSpec((8, parents), fixed),
            pl.BlockSpec((parents, width), fixed),
        ],
        out_specs=pl.BlockSpec((chunk, width), lambda i: (i, 0)),
        scratch_shapes=[pltpu.VMEM((parents, width), BF)],
        compiler_params=ROOM,
        cost_estimate=cost(2 * rows * parents * width, 4 * rows * width),
    )(span, grad_back)


def swap(parts):
    return lax.all_to_all(parts, "pts", split_axis=0, concat_axis=0, tiled=True)


def exchange(rows, devices):
    return swap(rows.reshape(devices, rows.shape[0] // devices, rows.shape[1])).reshape(rows.shape)


def gather_info(info, devices):
    known = info[None]
    bit = 1
    while bit < devices:
        pairs = [(d, d ^ bit) for d in range(devices)]
        known = jnp.concatenate([known, lax.ppermute(known, "pts", pairs)], axis=0)
        bit *= 2
    return known


def received_index(codes, blocks, capacity):
    devices = codes.shape[0]
    me = lax.axis_index("pts")
    mine = codes // blocks == me
    slots = codes % blocks
    lane = jnp.arange(blocks)
    rank = jnp.sum(mine[:, None, :] & (lane[None, :] < lane[:, None])[None], axis=2)
    index = (jnp.arange(devices) ^ me)[:, None] * capacity + rank
    both = index * blocks + lane[None, :]
    hit = mine[:, :, None] & (slots[:, :, None] == lane[None, None, :])
    both = jnp.sum(jnp.where(hit, both[:, :, None], 0), axis=(0, 1)).astype(jnp.int32)
    return both // blocks, both % blocks


def key_windows(patch_ids):
    tiles, span = patch_ids.shape
    patch = jnp.arange(PATCHES + 1)
    starts = jnp.sum(patch_ids[:, None, :] < patch[None, :, None], axis=2)
    by_block = patch_ids.reshape(tiles, span // ROWS, ROWS)
    first, last = by_block[:, :, 0], by_block[:, :, -1]
    pick = lambda which: jnp.sum(
        jnp.where(which[:, :, None] == patch[None, None, :], starts[:, None, :], 0), axis=2
    )
    low = pick(first) // ROWS * ROWS
    count = (pick(last + 1) - low + WINDOW - 1) // WINDOW
    low = jnp.minimum(low, span - count * WINDOW)
    return low.reshape(-1).astype(jnp.int32), count.reshape(-1).astype(jnp.int32)


def local(
    points,
    hil_dest,
    hil_slot,
    patch_ids,
    child_counts,
    parent_order,
    w_qkv,
    w_out,
    w_pool,
    norm_gain,
    norm_shift,
    cotangent,
):
    devices = lax.axis_size("pts")
    blocks = hil_dest.shape[0]
    rows, width = points.shape
    wide = w_pool.shape[1]
    parents = child_counts.shape[1]
    per_owner = parents // devices
    capacity = (blocks + devices - 1) // devices

    me = lax.axis_index("pts")
    payload, info, span = front(
        child_counts, parent_order, hil_dest, hil_slot, points, devices, capacity
    )
    received = exchange(payload, devices)
    info = gather_info(info, devices)
    index, block = received_index(info[:, parents // 128, :blocks], blocks, capacity)
    source = index // capacity
    table, local_run, base, most = seat_rows(
        source, source ^ me, block, info.reshape(devices * INFO, 128), per_owner
    )
    code, tags = plan_seats(jnp.zeros((1,), jnp.int32), base, most, table, devices)
    low, count = key_windows(patch_ids)
    lengths = lax.dynamic_slice_in_dim(
        info[:, : parents // 128].reshape(devices, parents), me * per_owner, per_owner, axis=1
    )
    lengths = lengths[jnp.arange(devices) ^ me].reshape(parents, 1) % 16
    lengths = jnp.broadcast_to(lengths.astype(F32), (parents, 128))
    more = jnp.zeros((parents, width), F32)
    index, low, count, base, local_run, code, tags, lengths = lax.optimization_barrier(
        (index, low, count, base, local_run, code, tags, lengths)
    )
    sums = attend(index, low, count, base, local_run, patch_ids, w_qkv, w_out, received)
    pieces = exchange(route_sums(base, code, tags, sums), devices)
    rounds = jnp.max(pieces.reshape(devices, SEAT, width)[:, SEATS + 1, 0].astype(F32))

    def turn(carry):
        step, before = carry
        code, tags = plan_seats(step.reshape(1), base, most, table, devices)
        late = exchange(route_sums(base, code, tags, sums), devices)
        return step + 1, fold_pieces(late, before, per_owner)

    _, more = lax.while_loop(
        lambda carry: carry[0] < rounds.astype(jnp.int32), turn, (jnp.int32(1), more)
    )
    pooled, back, weight, norm = pool(
        pieces, more, lengths, w_pool, norm_gain[None], norm_shift[None], cotangent
    )
    norm_high = norm.astype(BF)
    norm_low = (norm - norm_high.astype(F32)).astype(BF)
    norm_parts = jnp.concatenate([norm_high[:2], norm_low[:2]], axis=0).reshape(1, -1, width)
    outgoing = jnp.concatenate(
        [
            back.reshape(devices, -1, width),
            weight.reshape(devices, -1, width),
            jnp.broadcast_to(norm_parts, (devices,) + norm_parts.shape[1:]),
        ],
        axis=1,
    )
    arrived = swap(outgoing)
    weight_rows = width * wide // width // devices
    grad_back = arrived[:, :per_owner].reshape(parents, width)
    weight_sum = jnp.sum(arrived[:, per_owner : per_owner + weight_rows].astype(F32), axis=0)
    norm_sum = jnp.sum(arrived[:, per_owner + weight_rows :].astype(F32), axis=0)
    norm_sum = norm_sum.reshape(4, wide)
    grad_norm = norm_sum[:2] + norm_sum[2:]
    shared = jnp.broadcast_to(weight_sum.astype(BF)[None], (devices,) + weight_sum.shape)
    grad_weight = swap(shared).reshape(width, wide).astype(F32)
    grad_points = spread_grads(span, grad_back, rows)
    return (pooled, grad_points, grad_weight, grad_norm)


def solution(mesh):
    in_specs = (
        P(("grp", "pts"), None),
        P(("grp", "pts")),
        P(("grp", "pts")),
        P(("grp", "pts"), None),
        P(("grp", "pts"), None),
        P(("grp", "pts"), None),
        P(),
        P(),
        P(),
        P(),
        P(),
        P(("grp", "pts"), None),
    )
    out_specs = (P(("grp", "pts"), None), P(("grp", "pts"), None), P("grp", None), P("grp", None))
    return jax.shard_map(local, mesh=mesh, in_specs=in_specs, out_specs=out_specs, check_vma=False)
```

```python
import functools
import math

import jax
import jax.numpy as jnp
from jax import lax
from jax.experimental import pallas as pl
from jax.experimental.pallas import tpu as pltpu
from jax.sharding import PartitionSpec as P

HDIM = 16
HEAD_GROUP = 8
ROWS = 128
SEAT = 128
SEATS = 112
INFO = 16
ALIGN = 16
CHUNK = 512
FIELDS = 6
WINDOW = 256
PATCHES = 4
FAR = 2.0**100
SCORE_SCALE = HDIM**-0.5 * math.log2(math.e)
SCORE_SAFE = 98.0

inv_sqrt_two = 0.7071067811865476
inv_sqrt_tau = 0.3989422804014327
norm_eps = 1e-05

BF = jnp.bfloat16
F32 = jnp.float32
NT = (((1,), (1,)), ((), ()))
TN = (((0,), (0,)), ((), ()))
VMEM = pl.BlockSpec(memory_space=pltpu.VMEM)
HBM = pl.BlockSpec(memory_space=pltpu.HBM)
SMEM = pl.BlockSpec(memory_space=pltpu.SMEM)
ANY = pl.BlockSpec(memory_space=pl.ANY)
ROOM = pltpu.CompilerParams(vmem_limit_bytes=48 << 20)
FULL = pltpu.CompilerParams(vmem_limit_bytes=60 << 20)


def iota(shape, dim):
    return lax.broadcasted_iota(jnp.int32, shape, dim)


def mm(a, b, dims=(((1,), (0,)), ((), ()))):
    return lax.dot_general(a, b, dims, preferred_element_type=F32)


def cost(flops, bytes_accessed, transcendentals=0):
    return pl.CostEstimate(
        flops=int(flops), bytes_accessed=int(bytes_accessed), transcendentals=int(transcendentals)
    )


def order_kernel(counts_ref, order_ref, dest_ref, slot_ref, info_ref, span_ref):
    parents = counts_ref.shape[1]
    blocks = dest_ref.shape[1]
    counts = jnp.broadcast_to(counts_ref[...], (8, parents)).astype(F32)
    upper = jnp.where(iota((parents, parents), 0) <= iota((parents, parents), 1), 1.0, 0.0)
    starts = mm(counts.astype(BF), upper.astype(BF)) - counts
    coarse = jnp.floor(starts * (1.0 / 64.0))
    which = iota((8, parents), 0)
    fields = jnp.where(which == 0, coarse, jnp.where(which == 1, starts - 64.0 * coarse, counts))
    pick = jnp.where(iota((parents, parents), 0) == order_ref[...], 1.0, 0.0).astype(BF)
    ordered = mm(fields.astype(BF), pick).astype(jnp.int32)
    first = 64 * ordered[0:1] + ordered[1:2]
    length = ordered[2:3]
    span_ref[...] = jnp.where(which == 0, first, jnp.where(which == 1, first + length, length))
    both = 16 * first + length
    lines = parents // 128
    info_ref[0, lines:, :] = jnp.zeros((INFO - lines, 128), jnp.int32)
    info_ref[0, lines : lines + 1, :blocks] = dest_ref[...] * blocks + slot_ref[...]
    for i in range(lines):
        info_ref[0, i : i + 1, :] = both[:, i * 128 : (i + 1) * 128]
    tile = info_ref[0]
    for d in range(1, info_ref.shape[0]):
        info_ref[d] = tile


def order_tables(child_counts, parent_order, hil_dest, hil_slot, devices):
    parents = child_counts.shape[1]
    return pl.pallas_call(
        order_kernel,
        out_shape=(
            jax.ShapeDtypeStruct((devices, INFO, 128), jnp.int32),
            jax.ShapeDtypeStruct((8, parents), jnp.int32),
        ),
        in_specs=[VMEM] * 4,
        out_specs=(VMEM, VMEM),
        compiler_params=FULL,
        cost_estimate=cost(32 * parents * parents, 8 * parents),
    )(child_counts, parent_order, hil_dest[None], hil_slot[None])


def pack_kernel(capacity, dest_ref, points_ref, payload_ref, used, sem):
    blocks = dest_ref.shape[0]

    def clear(d, _):
        used[d] = 0
        return 0

    lax.fori_loop(0, used.shape[0], clear, 0)

    def send(b, _):
        d = dest_ref[b]
        place = d * capacity + used[d]
        used[d] = used[d] + 1
        pltpu.make_async_copy(
            points_ref.at[pl.ds(pl.multiple_of(b * ROWS, ROWS), ROWS)],
            payload_ref.at[pl.ds(pl.multiple_of(place * ROWS, ROWS), ROWS)],
            sem,
        ).start()
        return 0

    lax.fori_loop(0, blocks, send, 0)
    whole = pl.ds(0, blocks * ROWS)
    pltpu.make_async_copy(points_ref.at[whole], payload_ref.at[whole], sem).wait()


def pack_blocks(hil_dest, points, devices, capacity):
    return pl.pallas_call(
        functools.partial(pack_kernel, capacity),
        out_shape=jax.ShapeDtypeStruct((devices * capacity * ROWS, points.shape[1]), BF),
        in_specs=[SMEM, HBM],
        out_specs=VMEM,
        scratch_shapes=[pltpu.SMEM((devices,), jnp.int32), pltpu.SemaphoreType.DMA],
        compiler_params=FULL,
        cost_estimate=cost(0, 4 * points.size),
    )(hil_dest, points)


def seat_kernel(
    per_owner,
    source_ref,
    block_ref,
    info_ref,
    table_ref,
    local_ref,
    base_ref,
    most_ref,
    owner,
    place,
    origin,
    seats,
):
    blocks = owner.shape[0]
    parents = 128 * 8
    devices = info_ref.shape[0] // INFO
    which = iota((16, parents), 0)
    rank = iota((16, parents), 1)
    fields = jnp.where(which == 0, rank // per_owner, jnp.where(which == 1, rank % per_owner, 0))
    fields = fields.astype(F32).astype(BF)

    def one(v, _):
        source = source_ref[v]
        packed = info_ref[pl.ds(pl.multiple_of(source * INFO, INFO), 8), :]
        line = jnp.concatenate([packed[i : i + 1] for i in range(8)], axis=1)
        first = line // 16
        row = block_ref[v] * ROWS + iota((ROWS, parents), 0)
        inside = (row >= first) & (row < first + line % 16)
        found = mm(fields, jnp.where(inside, 1.0, 0.0).astype(BF), NT)
        owner[pl.ds(v, 1), :] = found[0:1]
        place[pl.ds(v, 1), :] = found[1:2]
        origin[pl.ds(v, 1), :] = jnp.full((1, ROWS), source, jnp.int32).astype(F32)
        return 0

    lax.fori_loop(0, blocks, one, 0)
    own = owner[...]
    run = own * per_owner + place[...]
    opens = (iota((blocks, ROWS), 1) == 0) | (run != pltpu.roll(run, 1, 1))
    opened = jnp.where(opens, 1.0, 0.0)
    upper = jnp.where(iota((ROWS, ROWS), 0) <= iota((ROWS, ROWS), 1), 1.0, 0.0).astype(BF)
    every = jnp.ones((ROWS, ROWS), BF)
    before = jnp.where(iota((blocks, blocks), 1) < iota((blocks, blocks), 0), 1.0, 0.0).astype(BF)
    local_ref[...] = (mm(opened.astype(BF), upper) - 1.0).astype(jnp.int32)

    def count(e, carry):
        seat, most = carry
        here = own == e.astype(F32)
        marks = jnp.where(here, opened, 0.0).astype(BF)
        total = mm(marks, upper) + mm(before, mm(marks, every).astype(BF))
        return jnp.where(here, total - 1.0, seat), jnp.maximum(most, total)

    zero = jnp.zeros((blocks, ROWS), F32)
    seat, most = lax.fori_loop(0, devices, count, (zero, zero))
    seats[...] = seat
    most_ref[...] = jnp.full((8, 128), jnp.max(most), F32)
    table_ref[...] = jnp.zeros_like(table_ref)
    field = iota((ROWS, ROWS), 0)

    def lay(v, base):
        base = pl.multiple_of(base, ALIGN)
        base_ref[v] = base
        at = pl.ds(v, 1)
        local = local_ref[at, :]
        seat = seats[at, :]
        coarse = jnp.floor(seat * (1.0 / 64.0))
        lines = (owner[at, :], coarse, seat - 64.0 * coarse, origin[at, :], place[at, :])
        values = jnp.ones((ROWS, ROWS), F32)
        for i, line in enumerate(lines):
            values = jnp.where(field == i, line, values)
        previous = jnp.where(iota((1, ROWS), 1) == 0, -1, pltpu.roll(local, 1, 1))
        begins = (field == local) & (local != previous)
        found = mm(jnp.where(begins, 1.0, 0.0).astype(BF), values.astype(BF), NT)
        table_ref[pl.ds(base, ROWS), :] = found.astype(BF)
        return base + (jnp.max(local) + ALIGN) // ALIGN * ALIGN

    base_ref[blocks] = lax.fori_loop(0, blocks, lay, 0)


def seat_rows(source, block, info, per_owner):
    blocks = source.shape[0]
    rows = blocks * ROWS
    return pl.pallas_call(
        functools.partial(seat_kernel, per_owner),
        out_shape=(
            jax.ShapeDtypeStruct((rows + CHUNK, 128), BF),
            jax.ShapeDtypeStruct((blocks, ROWS), jnp.int32),
            jax.ShapeDtypeStruct((blocks + 1,), jnp.int32),
            jax.ShapeDtypeStruct((8, 128), F32),
        ),
        in_specs=[SMEM, SMEM, VMEM],
        out_specs=(VMEM, VMEM, SMEM, VMEM),
        scratch_shapes=[pltpu.VMEM((blocks, ROWS), F32)] * 4,
        compiler_params=ROOM,
        cost_estimate=cost(40 * rows * 1024, 8 * rows),
    )(source, block, info)


def plan_kernel(round_ref, base_ref, most_ref, table_ref, code_ref, tags_ref, found):
    first = (SEATS * round_ref[0]).astype(F32)
    chunks = (base_ref[base_ref.shape[0] - 1] + CHUNK - 1) // CHUNK
    total = tags_ref.shape[1]
    pick = jnp.where(iota((16, 128), 0) == iota((16, 128), 1), 1.0, 0.0).astype(BF)
    base = pl.program_id(0) * total
    found[...] = jnp.zeros_like(found)

    def step(c, _):
        at = pl.ds(pl.multiple_of(c * CHUNK, CHUNK), CHUNK)
        lines = mm(pick, table_ref[at, :], NT)
        seat = 64.0 * lines[1:2] + lines[2:3] - first
        seated = (lines[5:6] > 0.5) & (seat >= 0.0) & (seat < float(SEATS))
        code = jnp.where(seated, lines[0:1] * float(SEAT) + seat, -1.0).astype(jnp.int32)
        code_ref[:, at] = jnp.broadcast_to(code, (8, CHUNK))
        member = jnp.where(iota((total, 1), 0) + base == code, 1.0, 0.0).astype(BF)
        found[...] += mm(lines.astype(BF), member, NT)
        return 0

    lax.fori_loop(0, chunks, step, 0)
    rounds = jnp.floor((jnp.max(most_ref[...]) + (SEATS - 1.0)) * (1.0 / SEATS) + 1e-3)
    line = iota((8, total), 0)
    tags_ref[...] = jnp.where(
        line == 0, found[3:4, :], jnp.where(line == 1, found[4:5, :], rounds)
    )


def plan_seats(step, base, most, table, devices):
    total = devices * SEAT
    part = min(2048, total)
    return pl.pallas_call(
        plan_kernel,
        grid=(total // part,),
        out_shape=(
            jax.ShapeDtypeStruct((8, table.shape[0]), jnp.int32),
            jax.ShapeDtypeStruct((8, total), F32),
        ),
        in_specs=[SMEM, SMEM, VMEM, VMEM],
        out_specs=(
            pl.BlockSpec((8, table.shape[0]), lambda i: (0, 0)),
            pl.BlockSpec((8, part), lambda i: (0, i)),
        ),
        scratch_shapes=[pltpu.VMEM((16, part), F32)],
        compiler_params=ROOM,
        cost_estimate=cost(64 * total * table.shape[0], 4 * table.size),
    )(step, base, most, table)


def attend_kernel(
    index_ref,
    low_ref,
    count_ref,
    base_ref,
    local_ref,
    ids_ref,
    w_ref,
    wo_ref,
    rows_ref,
    out_ref,
    x,
    qx,
    kx,
    vx,
    att,
    sems,
):
    tiles, span = ids_ref.shape
    width = w_ref.shape[0]
    cols = HEAD_GROUP * HDIM
    groups = width // cols
    heads = width // HDIM
    per_tile = span // ROWS

    for t in range(tiles):
        for b in range(per_tile):
            s = t * per_tile + b
            pltpu.make_async_copy(
                rows_ref.at[pl.ds(pl.multiple_of(index_ref[s] * ROWS, ROWS), ROWS)],
                x.at[pl.ds(s * ROWS, ROWS)],
                sems.at[t],
            ).start()

    out_ref[...] = jnp.zeros_like(out_ref)
    lane = iota((ROWS, 2 * cols), 1)
    of_head = [(lane // HDIM == h) | (lane >= cols) for h in range(HEAD_GROUP)]
    lane_out = lane % cols // HDIM
    for g in range(groups):
        vx[g, :, cols:] = jnp.ones((span, cols), BF)
    r_i = iota((cols, cols), 0)
    c_i = iota((cols, cols), 1)
    far = jnp.where((r_i != c_i) & (c_i < PATCHES), -FAR, 0.0).astype(BF)

    def tile(t, _):
        at = pl.ds(pl.multiple_of(t * span, span), span)
        pltpu.make_async_copy(rows_ref.at[pl.ds(0, span)], x.at[at], sems.at[t]).wait()
        tile_rows = x[at, :]
        same = ids_ref[pl.ds(t, 1), :] == iota((cols, span), 0)
        patch_hot = jnp.where(same, 1.0, 0.0).astype(BF)
        query = mm(tile_rows, w_ref[:, :width])
        keys = mm(w_ref[:, width : 2 * width], tile_rows, (((0,), (1,)), ((), ())))
        value = mm(tile_rows, w_ref[:, 2 * width :]).astype(BF)
        patch_far = mm(patch_hot, far, TN).astype(BF)
        for g in range(groups):
            some = slice(g * cols, (g + 1) * cols)
            qx[g, :, :cols] = query[:, some].astype(BF)
            qx[g, :, cols:] = patch_far
            kx[g, :cols, :] = keys[some].astype(BF)
            kx[g, cols:, :] = patch_hot
            vx[g, :, :cols] = value[:, some]
        query_most = jnp.max(jnp.abs(query), axis=0, keepdims=True)
        key_most = jnp.max(jnp.abs(keys), axis=1, keepdims=True)
        by_head = jnp.where(
            iota((heads, width), 1) // HDIM == iota((heads, width), 0), query_most, 0.0
        )
        bound = jnp.max(mm(by_head.astype(BF), jnp.broadcast_to(key_most, (width, 128)).astype(BF)))
        safe = bound * SCORE_SCALE < SCORE_SAFE

        def block(b, _):
            low = pl.multiple_of(low_ref[t * per_tile + b], ROWS)
            steps = count_ref[t * per_tile + b]
            here = pl.ds(pl.multiple_of(b * ROWS, ROWS), ROWS)

            def run(start, length, exact):
                scores = []
                for g in range(groups):
                    q = qx[g, here, :]
                    stacked = jnp.concatenate(
                        [jnp.where(of_head[h], q, jnp.zeros_like(q)) for h in range(HEAD_GROUP)],
                        axis=0,
                    )
                    scores.append(mm(stacked, kx[g, :, pl.ds(start, length)]))
                for g in range(groups):
                    level = scores[g] * SCORE_SCALE
                    if exact:
                        level = level - jnp.max(level, axis=1, keepdims=True)
                    weights = jnp.exp2(level).astype(BF)
                    mixed = mm(weights, vx[g, pl.ds(start, length), :])
                    mixed = mixed.reshape(HEAD_GROUP, ROWS, 2 * cols)
                    own = mixed[0]
                    for h in range(1, HEAD_GROUP):
                        own = jnp.where(lane_out == h, mixed[h], own)
                    att[here, g * cols : (g + 1) * cols] = (own[:, :cols] / own[:, cols:]).astype(BF)

            for i in range(span // WINDOW):
                pl.when(safe & (steps == i + 1))(
                    functools.partial(run, low, (i + 1) * WINDOW, False)
                )
            pl.when(jnp.logical_not(safe))(functools.partial(run, 0, span, True))
            return 0

        lax.fori_loop(0, per_tile, block, 0)
        mixed = (tile_rows.astype(F32) + mm(att[...], wo_ref[...])).astype(BF)
        for b in range(per_tile):
            s = t * per_tile + b
            run = jnp.where(iota((ROWS, ROWS), 0) == local_ref[pl.ds(s, 1), :], 1.0, 0.0)
            sums = mm(run.astype(BF), mixed[b * ROWS : (b + 1) * ROWS])
            out_ref[pl.ds(pl.multiple_of(base_ref[s], ALIGN), ROWS), :] = sums.astype(BF)
        return 0

    lax.fori_loop(0, tiles, tile, 0)


def attend(index, low, count, base, local, ids, w_qkv, w_out, rows):
    tiles, span = ids.shape
    width = rows.shape[1]
    cols = HEAD_GROUP * HDIM
    groups = width // cols
    pairs = tiles * span * span * HEAD_GROUP
    return pl.pallas_call(
        attend_kernel,
        out_shape=jax.ShapeDtypeStruct((tiles * span + CHUNK, width), BF),
        in_specs=[SMEM, SMEM, SMEM, SMEM, VMEM, VMEM, VMEM, VMEM, HBM],
        out_specs=VMEM,
        scratch_shapes=[
            pltpu.VMEM((tiles * span, width), BF),
            pltpu.VMEM((groups, span, 2 * cols), BF),
            pltpu.VMEM((groups, 2 * cols, span), BF),
            pltpu.VMEM((groups, span, 2 * cols), BF),
            pltpu.VMEM((span, width), BF),
            pltpu.SemaphoreType.DMA((tiles,)),
        ],
        compiler_params=ROOM,
        cost_estimate=cost(pairs * 1024, 4 * rows.size, pairs),
    )(index, low, count, base, local, ids, w_qkv, w_out, rows)


def route_kernel(base_ref, code_ref, tags_ref, sums_ref, out_ref, acc):
    total = out_ref.shape[0]
    chunks = (base_ref[base_ref.shape[0] - 1] + CHUNK - 1) // CHUNK
    seat = iota((total, 1), 0) + pl.program_id(0) * total
    acc[...] = jnp.zeros_like(acc)

    def step(c, _):
        at = pl.ds(pl.multiple_of(c * CHUNK, CHUNK), CHUNK)
        member = jnp.where(seat == code_ref[0:1, at], 1.0, 0.0).astype(BF)
        acc[...] += mm(member, sums_ref[at, :])
        return 0

    lax.fori_loop(0, chunks, step, 0)
    line = iota((SEAT - SEATS, SEAT), 0)
    for d in range(total // SEAT):
        low = d * SEAT
        here = slice(low, low + SEAT)
        out_ref[low : low + SEATS, :] = acc[low : low + SEATS, :].astype(BF)
        origin = jnp.where(
            line == 0, tags_ref[0:1, here], jnp.where(line == 1, tags_ref[2:3, here], 0.0)
        )
        place = jnp.where(line == 0, tags_ref[1:2, here], 0.0)
        out_ref[low + SEATS : low + SEAT, :] = jnp.concatenate([origin, place], axis=1).astype(BF)


def route_sums(base, code, tags, sums):
    count, width = sums.shape
    total = tags.shape[1]
    part = min(2048, total)
    return pl.pallas_call(
        route_kernel,
        grid=(total // part,),
        out_shape=jax.ShapeDtypeStruct((total, width), BF),
        in_specs=[
            SMEM,
            VMEM,
            pl.BlockSpec((8, part), lambda i: (0, i)),
            VMEM,
        ],
        out_specs=pl.BlockSpec((part, width), lambda i: (i, 0)),
        scratch_shapes=[pltpu.VMEM((part, width), F32)],
        compiler_params=ROOM,
        cost_estimate=cost(total * count * width, 4 * count * width),
    )(base, code, tags, sums)


def seat_targets(per_owner, pieces_ref, target):
    valid = iota((1, SEAT), 1) < SEATS
    for h in range(pieces_ref.shape[0] // SEAT):
        tag = pieces_ref[h * SEAT + SEATS : (h + 1) * SEAT, :].astype(F32)[0:1]
        where = tag[:, :SEAT] * float(per_owner) + tag[:, SEAT:]
        target[0:1, h * SEAT : (h + 1) * SEAT] = jnp.where(valid, where, -1.0).astype(jnp.int32)


def fold_kernel(per_owner, pieces_ref, before_ref, out_ref, target):
    step = pl.program_id(0)
    parents = out_ref.shape[0]
    chunk = pieces_ref.shape[0]

    @pl.when(step == 0)
    def _():
        out_ref[...] = before_ref[...]

    seat_targets(per_owner, pieces_ref, target)
    member = jnp.where(iota((parents, 1), 0) == target[0:1, :], 1.0, 0.0).astype(BF)
    out_ref[...] += mm(member, pieces_ref[...])


def fold_pieces(pieces, before, per_owner):
    parents, width = before.shape
    chunk = min(2048, pieces.shape[0])
    fixed = lambda i: (0, 0)
    return pl.pallas_call(
        functools.partial(fold_kernel, per_owner),
        grid=(pieces.shape[0] // chunk,),
        out_shape=jax.ShapeDtypeStruct((parents, width), F32),
        in_specs=[
            pl.BlockSpec((chunk, width), lambda i: (i, 0)),
            pl.BlockSpec((parents, width), fixed),
        ],
        out_specs=pl.BlockSpec((parents, width), fixed),
        scratch_shapes=[pltpu.VMEM((8, chunk), jnp.int32)],
        compiler_params=ROOM,
        cost_estimate=cost(2 * parents * pieces.size, 4 * pieces.size),
    )(pieces, before)


def whole_tiles(rows):
    return (rows + 15) // 16 * 16


def pad_rows(value):
    spare = whole_tiles(value.shape[0]) - value.shape[0]
    if spare == 0:
        return value
    return jnp.concatenate([value, jnp.zeros((spare, value.shape[1]), value.dtype)], axis=0)


def pool_kernel(
    per_owner,
    pieces_ref,
    more_ref,
    length_ref,
    w_ref,
    gain_ref,
    shift_ref,
    cot_ref,
    pooled_ref,
    sent_ref,
    acc,
    sums,
    target,
):
    step = pl.program_id(0)

    @pl.when(step == 0)
    def _():
        acc[...] = jnp.zeros_like(acc)
        sums[...] = jnp.zeros_like(sums)
        seat_targets(per_owner, pieces_ref, target)

    chunk, width = more_ref.shape
    total = more_ref[...]
    parent = iota((chunk, 1), 0) + step * chunk
    part = min(2048, pieces_ref.shape[0])
    for low in range(0, pieces_ref.shape[0], part):
        member = jnp.where(parent == target[0:1, low : low + part], 1.0, 0.0).astype(BF)
        total = total + mm(member, pieces_ref[low : low + part, :])
    lengths = jnp.concatenate([length_ref[...]] * (width // 128), axis=1)
    parent_in = (total / lengths).astype(BF)
    w_pool = w_ref[...]
    gain = gain_ref[...]
    projected = mm(parent_in, w_pool)
    centred = projected - jnp.mean(projected, axis=-1, keepdims=True)
    variance = jnp.mean(centred * centred, axis=-1, keepdims=True)
    inv_std = lax.rsqrt(variance + norm_eps)
    normed = centred * inv_std
    shifted = normed * gain + shift_ref[...]
    normal_cdf = 0.5 * (1.0 + lax.erf(shifted * inv_sqrt_two))
    pooled_ref[...] = (shifted * normal_cdf).astype(BF)
    grad_act = cot_ref[...].astype(F32) * (
        normal_cdf + shifted * jnp.exp(-0.5 * shifted * shifted) * inv_sqrt_tau
    )
    sums[0:1, :] += jnp.sum(grad_act * normed, axis=0, keepdims=True)
    sums[1:2, :] += jnp.sum(grad_act, axis=0, keepdims=True)
    scaled = grad_act * gain
    grad_proj = (
        (
            scaled
            - jnp.mean(scaled, axis=-1, keepdims=True)
            - normed * jnp.mean(scaled * normed, axis=-1, keepdims=True)
        )
        * inv_std
    ).astype(BF)
    acc[...] += mm(parent_in, grad_proj, TN)
    back = mm(grad_proj, w_pool, NT)
    devices, _, width = sent_ref.shape
    fits = chunk // per_owner
    for d in range(fits):
        part = back[d * per_owner : (d + 1) * per_owner]
        sent_ref[step * fits + d, : whole_tiles(per_owner), :] = pad_rows(part).astype(BF)

    @pl.when(step == pl.num_programs(0) - 1)
    def _():
        each = acc.shape[0] // devices
        tall = whole_tiles(each)
        exact = sums[0:2, :]
        high = exact.astype(BF).astype(F32)
        parts = []
        for value in (high, exact - high):
            for row in range(2):
                for low in range(0, acc.shape[1], width):
                    parts.append(value[row : row + 1, low : low + width])
        norm = pad_rows(jnp.concatenate(parts, axis=0)).astype(BF)
        for d in range(devices):
            low = whole_tiles(per_owner)
            for side in range(0, acc.shape[1], width):
                part = acc[d * each : (d + 1) * each, side : side + width]
                sent_ref[d, low : low + tall, :] = pad_rows(part).astype(BF)
                low += tall
            sent_ref[d, low:, :] = norm


def pool(pieces, more, length, w_pool, gain, shift, cotangent):
    parents, width = more.shape
    wide = w_pool.shape[1]
    chunk = 256
    devices = pieces.shape[0] // SEAT
    tall = whole_tiles(parents // devices) + wide // width * whole_tiles(width // devices)
    tall += whole_tiles(4 * wide // width)
    fixed = lambda i: (0, 0)
    along = lambda i: (i, 0)
    return pl.pallas_call(
        functools.partial(pool_kernel, parents * SEAT // pieces.shape[0]),
        grid=(parents // chunk,),
        out_shape=(
            jax.ShapeDtypeStruct((parents, wide), BF),
            jax.ShapeDtypeStruct((devices, tall, width), BF),
        ),
        in_specs=[
            pl.BlockSpec(pieces.shape, fixed),
            pl.BlockSpec((chunk, width), along),
            pl.BlockSpec((chunk, 128), along),
            pl.BlockSpec((width, wide), fixed),
            pl.BlockSpec((1, wide), fixed),
            pl.BlockSpec((1, wide), fixed),
            pl.BlockSpec((chunk, wide), along),
        ],
        out_specs=(
            pl.BlockSpec((chunk, wide), along),
            pl.BlockSpec((devices, tall, width), lambda i: (0, 0, 0)),
        ),
        scratch_shapes=[
            pltpu.VMEM((width, wide), F32),
            pltpu.VMEM((8, wide), F32),
            pltpu.VMEM((8, pieces.shape[0]), jnp.int32),
        ],
        compiler_params=FULL,
        cost_estimate=cost(6 * parents * width * wide, 8 * parents * wide, 2 * parents * wide),
    )(pieces, more, length, w_pool, gain, shift, cotangent)


def spread_kernel(span_ref, grad_ref, out_ref, share):
    step = pl.program_id(0)
    chunk = out_ref.shape[0]
    parents, width = share.shape

    @pl.when(step == 0)
    def _():
        pick = jnp.where(iota((8, width), 0) == 2, 1.0, 0.0).astype(BF)
        lengths = mm(jnp.minimum(span_ref[...], 64).astype(F32).astype(BF), pick, TN)
        per_owner = parents // grad_ref.shape[0]
        grads = [grad_ref[d, :per_owner, :].astype(F32) for d in range(grad_ref.shape[0])]
        share[...] = (jnp.concatenate(grads, axis=0) / lengths).astype(BF)

    row = iota((chunk, parents), 0) + step * chunk
    inside = (row >= span_ref[0:1, :]) & (row < span_ref[1:2, :])
    out_ref[...] = mm(jnp.where(inside, 1.0, 0.0).astype(BF), share[...]).astype(BF)


def spread_grads(span, arrived, rows):
    parents = span.shape[1]
    width = arrived.shape[2]
    chunk = 512
    fixed = lambda i: (0, 0)
    return pl.pallas_call(
        spread_kernel,
        grid=(rows // chunk,),
        out_shape=jax.ShapeDtypeStruct((rows, width), BF),
        in_specs=[
            pl.BlockSpec((8, parents), fixed),
            pl.BlockSpec(arrived.shape, lambda i: (0, 0, 0)),
        ],
        out_specs=pl.BlockSpec((chunk, width), lambda i: (i, 0)),
        scratch_shapes=[pltpu.VMEM((parents, width), BF)],
        compiler_params=ROOM,
        cost_estimate=cost(2 * rows * parents * width, 4 * rows * width),
    )(span, arrived)


def settle_kernel(per_owner, arrived_ref, shared_ref, norm_ref):
    devices, tall, width = arrived_ref.shape
    low = whole_tiles(per_owner)
    total = arrived_ref[0, low:, :].astype(F32)
    for d in range(1, devices):
        total = total + arrived_ref[d, low:, :].astype(F32)
    weight_rows = shared_ref.shape[1]
    weight = total[:weight_rows].astype(BF)
    for d in range(devices):
        shared_ref[d] = weight
    norm = total[weight_rows : weight_rows + 8]
    sides = norm_ref.shape[1] // width
    for row in range(2):
        for side in range(sides):
            i = row * sides + side
            value = norm[i : i + 1] + norm[2 * sides + i : 2 * sides + i + 1]
            norm_ref[row : row + 1, side * width : (side + 1) * width] = value


def settle(arrived, per_owner, weight_rows, wide):
    devices, tall, width = arrived.shape
    return pl.pallas_call(
        functools.partial(settle_kernel, per_owner),
        out_shape=(
            jax.ShapeDtypeStruct((devices, weight_rows, width), BF),
            jax.ShapeDtypeStruct((2, wide), F32),
        ),
        in_specs=[VMEM],
        out_specs=(VMEM, VMEM),
        compiler_params=ROOM,
        cost_estimate=cost(arrived.size, 2 * arrived.size),
    )(arrived)


def swap(parts):
    return lax.all_to_all(parts, "pts", split_axis=0, concat_axis=0, tiled=True)


def exchange(rows, devices):
    return swap(rows.reshape(devices, rows.shape[0] // devices, rows.shape[1])).reshape(rows.shape)


def received_index(codes, blocks, capacity):
    devices = codes.shape[0]
    me = lax.axis_index("pts")
    mine = codes // blocks == me
    slots = codes % blocks
    lane = jnp.arange(blocks)
    rank = jnp.sum(mine[:, None, :] & (lane[None, :] < lane[:, None])[None], axis=2)
    index = jnp.arange(devices)[:, None] * capacity + rank
    both = index * blocks + lane[None, :]
    hit = mine[:, :, None] & (slots[:, :, None] == lane[None, None, :])
    both = jnp.sum(jnp.where(hit, both[:, :, None], 0), axis=(0, 1)).astype(jnp.int32)
    return both // blocks, both % blocks


def key_windows(patch_ids):
    tiles, span = patch_ids.shape
    patch = jnp.arange(PATCHES + 1)
    starts = jnp.sum(patch_ids[:, None, :] < patch[None, :, None], axis=2)
    by_block = patch_ids.reshape(tiles, span // ROWS, ROWS)
    first, last = by_block[:, :, 0], by_block[:, :, -1]
    pick = lambda which: jnp.sum(
        jnp.where(which[:, :, None] == patch[None, None, :], starts[:, None, :], 0), axis=2
    )
    low = pick(first) // ROWS * ROWS
    count = (pick(last + 1) - low + WINDOW - 1) // WINDOW
    low = jnp.minimum(low, span - count * WINDOW)
    return low.reshape(-1).astype(jnp.int32), count.reshape(-1).astype(jnp.int32)


def local(
    points,
    hil_dest,
    hil_slot,
    patch_ids,
    child_counts,
    parent_order,
    w_qkv,
    w_out,
    w_pool,
    norm_gain,
    norm_shift,
    cotangent,
):
    devices = lax.axis_size("pts")
    blocks = hil_dest.shape[0]
    rows, width = points.shape
    wide = w_pool.shape[1]
    parents = child_counts.shape[1]
    per_owner = parents // devices
    capacity = (blocks + devices - 1) // devices

    me = lax.axis_index("pts")
    info, span = order_tables(child_counts, parent_order, hil_dest, hil_slot, devices)
    info = swap(info)
    payload = pack_blocks(hil_dest, points, devices, capacity)
    received = exchange(payload, devices)
    index, block = received_index(info[:, parents // 128, :blocks], blocks, capacity)
    source = index // capacity
    table, local_run, base, most = seat_rows(
        source, block, info.reshape(devices * INFO, 128), per_owner
    )
    code, tags = plan_seats(jnp.zeros((1,), jnp.int32), base, most, table, devices)
    low, count = key_windows(patch_ids)
    lengths = lax.dynamic_slice_in_dim(
        info[:, : parents // 128].reshape(devices, parents), me * per_owner, per_owner, axis=1
    )
    lengths = lengths.reshape(parents, 1) % 16
    lengths = jnp.broadcast_to(lengths.astype(F32), (parents, 128))
    more = jnp.zeros((parents, width), F32)
    index, low, count, base, local_run, code, tags, lengths = lax.optimization_barrier(
        (index, low, count, base, local_run, code, tags, lengths)
    )
    sums = attend(index, low, count, base, local_run, patch_ids, w_qkv, w_out, received)
    pieces = exchange(route_sums(base, code, tags, sums), devices)
    rounds = jnp.max(pieces.reshape(devices, SEAT, width)[:, SEATS + 1, 0].astype(F32))

    def turn(carry):
        step, before = carry
        code, tags = plan_seats(step.reshape(1), base, most, table, devices)
        late = exchange(route_sums(base, code, tags, sums), devices)
        return step + 1, fold_pieces(late, before, per_owner)

    _, more = lax.while_loop(
        lambda carry: carry[0] < rounds.astype(jnp.int32), turn, (jnp.int32(1), more)
    )
    pooled, outgoing = pool(
        pieces, more, lengths, w_pool, norm_gain[None], norm_shift[None], cotangent
    )
    arrived = swap(outgoing)
    each = width // devices
    tall = whole_tiles(each)
    sides = wide // width
    shared, grad_norm = settle(arrived, per_owner, sides * tall, wide)
    shared = swap(shared)
    grad_weight = jnp.concatenate(
        [shared[:, side * tall : side * tall + each] for side in range(sides)], axis=2
    )
    grad_weight = grad_weight.reshape(width, wide).astype(F32)
    grad_points = spread_grads(span, arrived, rows)
    return (pooled, grad_points, grad_weight, grad_norm)


def solution(mesh):
    in_specs = (
        P(("grp", "pts"), None),
        P(("grp", "pts")),
        P(("grp", "pts")),
        P(("grp", "pts"), None),
        P(("grp", "pts"), None),
        P(("grp", "pts"), None),
        P(),
        P(),
        P(),
        P(),
        P(),
        P(("grp", "pts"), None),
    )
    out_specs = (P(("grp", "pts"), None), P(("grp", "pts"), None), P("grp", None), P("grp", None))
    return jax.shard_map(local, mesh=mesh, in_specs=in_specs, out_specs=out_specs, check_vma=False)
```

```python
import functools
import math

import jax
import jax.numpy as jnp
from jax import lax
from jax.experimental import pallas as pl
from jax.experimental.pallas import tpu as pltpu
from jax.sharding import PartitionSpec as P

HDIM = 16
HEAD_GROUP = 8
ROWS = 128
SEAT = 128
SEATS = 112
INFO = 16
ALIGN = 16
CHUNK = 512
FIELDS = 6
WINDOW = 256
PATCHES = 4
FAR = 2.0**100
SCORE_SCALE = HDIM**-0.5 * math.log2(math.e)
SCORE_SAFE = 98.0

inv_sqrt_two = 0.7071067811865476
inv_sqrt_tau = 0.3989422804014327
norm_eps = 1e-05

BF = jnp.bfloat16
F32 = jnp.float32
NT = (((1,), (1,)), ((), ()))
TN = (((0,), (0,)), ((), ()))
VMEM = pl.BlockSpec(memory_space=pltpu.VMEM)
HBM = pl.BlockSpec(memory_space=pltpu.HBM)
SMEM = pl.BlockSpec(memory_space=pltpu.SMEM)
ANY = pl.BlockSpec(memory_space=pl.ANY)
ROOM = pltpu.CompilerParams(vmem_limit_bytes=48 << 20)
FULL = pltpu.CompilerParams(vmem_limit_bytes=60 << 20)


def iota(shape, dim):
    return lax.broadcasted_iota(jnp.int32, shape, dim)


def mm(a, b, dims=(((1,), (0,)), ((), ()))):
    return lax.dot_general(a, b, dims, preferred_element_type=F32)


def cost(flops, bytes_accessed, transcendentals=0):
    return pl.CostEstimate(
        flops=int(flops), bytes_accessed=int(bytes_accessed), transcendentals=int(transcendentals)
    )


def order_kernel(counts_ref, order_ref, dest_ref, slot_ref, info_ref, span_ref):
    parents = counts_ref.shape[1]
    blocks = dest_ref.shape[1]
    counts = jnp.broadcast_to(counts_ref[...], (8, parents)).astype(F32)
    upper = jnp.where(iota((parents, parents), 0) <= iota((parents, parents), 1), 1.0, 0.0)
    starts = mm(counts.astype(BF), upper.astype(BF)) - counts
    coarse = jnp.floor(starts * (1.0 / 64.0))
    which = iota((8, parents), 0)
    fields = jnp.where(which == 0, coarse, jnp.where(which == 1, starts - 64.0 * coarse, counts))
    pick = jnp.where(iota((parents, parents), 0) == order_ref[...], 1.0, 0.0).astype(BF)
    ordered = mm(fields.astype(BF), pick).astype(jnp.int32)
    first = 64 * ordered[0:1] + ordered[1:2]
    length = ordered[2:3]
    span_ref[...] = jnp.where(which == 0, first, jnp.where(which == 1, first + length, length))
    both = 16 * first + length
    lines = parents // 128
    info_ref[0, lines:, :] = jnp.zeros((INFO - lines, 128), jnp.int32)
    info_ref[0, lines : lines + 1, :blocks] = dest_ref[...] * blocks + slot_ref[...]
    for i in range(lines):
        info_ref[0, i : i + 1, :] = both[:, i * 128 : (i + 1) * 128]
    tile = info_ref[0]
    for d in range(1, info_ref.shape[0]):
        info_ref[d] = tile


def order_tables(child_counts, parent_order, hil_dest, hil_slot, devices):
    parents = child_counts.shape[1]
    return pl.pallas_call(
        order_kernel,
        out_shape=(
            jax.ShapeDtypeStruct((devices, INFO, 128), jnp.int32),
            jax.ShapeDtypeStruct((8, parents), jnp.int32),
        ),
        in_specs=[VMEM] * 4,
        out_specs=(VMEM, VMEM),
        compiler_params=FULL,
        cost_estimate=cost(32 * parents * parents, 8 * parents),
    )(child_counts, parent_order, hil_dest[None], hil_slot[None])


def pack_kernel(capacity, dest_ref, points_ref, payload_ref, used, sem):
    blocks = dest_ref.shape[0]

    def clear(d, _):
        used[d] = 0
        return 0

    lax.fori_loop(0, used.shape[0], clear, 0)

    def send(b, _):
        d = dest_ref[b]
        place = d * capacity + used[d]
        used[d] = used[d] + 1
        pltpu.make_async_copy(
            points_ref.at[pl.ds(pl.multiple_of(b * ROWS, ROWS), ROWS)],
            payload_ref.at[pl.ds(pl.multiple_of(place * ROWS, ROWS), ROWS)],
            sem,
        ).start()
        return 0

    lax.fori_loop(0, blocks, send, 0)
    whole = pl.ds(0, blocks * ROWS)
    pltpu.make_async_copy(points_ref.at[whole], payload_ref.at[whole], sem).wait()


def pack_blocks(hil_dest, points, devices, capacity):
    return pl.pallas_call(
        functools.partial(pack_kernel, capacity),
        out_shape=jax.ShapeDtypeStruct((devices * capacity * ROWS, points.shape[1]), BF),
        in_specs=[SMEM, HBM],
        out_specs=VMEM,
        scratch_shapes=[pltpu.SMEM((devices,), jnp.int32), pltpu.SemaphoreType.DMA],
        compiler_params=FULL,
        cost_estimate=cost(0, 4 * points.size),
    )(hil_dest, points)


def seat_kernel(
    per_owner,
    source_ref,
    block_ref,
    info_ref,
    table_ref,
    local_ref,
    base_ref,
    most_ref,
    owner,
    place,
    origin,
    seats,
):
    blocks = owner.shape[0]
    parents = 128 * 8
    devices = info_ref.shape[0] // INFO
    which = iota((16, parents), 0)
    rank = iota((16, parents), 1)
    fields = jnp.where(which == 0, rank // per_owner, jnp.where(which == 1, rank % per_owner, 0))
    fields = fields.astype(F32).astype(BF)

    def one(v, _):
        source = source_ref[v]
        packed = info_ref[pl.ds(pl.multiple_of(source * INFO, INFO), 8), :]
        line = jnp.concatenate([packed[i : i + 1] for i in range(8)], axis=1)
        first = line // 16
        row = block_ref[v] * ROWS + iota((ROWS, parents), 0)
        inside = (row >= first) & (row < first + line % 16)
        found = mm(fields, jnp.where(inside, 1.0, 0.0).astype(BF), NT)
        owner[pl.ds(v, 1), :] = found[0:1]
        place[pl.ds(v, 1), :] = found[1:2]
        origin[pl.ds(v, 1), :] = jnp.full((1, ROWS), source, jnp.int32).astype(F32)
        return 0

    lax.fori_loop(0, blocks, one, 0)
    own = owner[...]
    run = own * per_owner + place[...]
    opens = (iota((blocks, ROWS), 1) == 0) | (run != pltpu.roll(run, 1, 1))
    opened = jnp.where(opens, 1.0, 0.0)
    upper = jnp.where(iota((ROWS, ROWS), 0) <= iota((ROWS, ROWS), 1), 1.0, 0.0).astype(BF)
    every = jnp.ones((ROWS, ROWS), BF)
    before = jnp.where(iota((blocks, blocks), 1) < iota((blocks, blocks), 0), 1.0, 0.0).astype(BF)
    local_ref[...] = (mm(opened.astype(BF), upper) - 1.0).astype(jnp.int32)

    def count(e, carry):
        seat, most = carry
        here = own == e.astype(F32)
        marks = jnp.where(here, opened, 0.0).astype(BF)
        total = mm(marks, upper) + mm(before, mm(marks, every).astype(BF))
        return jnp.where(here, total - 1.0, seat), jnp.maximum(most, total)

    zero = jnp.zeros((blocks, ROWS), F32)
    seat, most = lax.fori_loop(0, devices, count, (zero, zero))
    seats[...] = seat
    most_ref[...] = jnp.full((8, 128), jnp.max(most), F32)
    table_ref[...] = jnp.zeros_like(table_ref)
    field = iota((ROWS, ROWS), 0)

    def lay(v, base):
        base = pl.multiple_of(base, ALIGN)
        base_ref[v] = base
        at = pl.ds(v, 1)
        local = local_ref[at, :]
        seat = seats[at, :]
        coarse = jnp.floor(seat * (1.0 / 64.0))
        lines = (owner[at, :], coarse, seat - 64.0 * coarse, origin[at, :], place[at, :])
        values = jnp.ones((ROWS, ROWS), F32)
        for i, line in enumerate(lines):
            values = jnp.where(field == i, line, values)
        previous = jnp.where(iota((1, ROWS), 1) == 0, -1, pltpu.roll(local, 1, 1))
        begins = (field == local) & (local != previous)
        found = mm(jnp.where(begins, 1.0, 0.0).astype(BF), values.astype(BF), NT)
        table_ref[pl.ds(base, ROWS), :] = found.astype(BF)
        return base + (jnp.max(local) + ALIGN) // ALIGN * ALIGN

    base_ref[blocks] = lax.fori_loop(0, blocks, lay, 0)


def seat_rows(source, block, info, per_owner):
    blocks = source.shape[0]
    rows = blocks * ROWS
    return pl.pallas_call(
        functools.partial(seat_kernel, per_owner),
        out_shape=(
            jax.ShapeDtypeStruct((rows + CHUNK, 128), BF),
            jax.ShapeDtypeStruct((blocks, ROWS), jnp.int32),
            jax.ShapeDtypeStruct((blocks + 1,), jnp.int32),
            jax.ShapeDtypeStruct((8, 128), F32),
        ),
        in_specs=[SMEM, SMEM, VMEM],
        out_specs=(VMEM, VMEM, SMEM, VMEM),
        scratch_shapes=[pltpu.VMEM((blocks, ROWS), F32)] * 4,
        compiler_params=ROOM,
        cost_estimate=cost(40 * rows * 1024, 8 * rows),
    )(source, block, info)


def plan_kernel(round_ref, base_ref, most_ref, table_ref, code_ref, tags_ref, found):
    first = (SEATS * round_ref[0]).astype(F32)
    chunks = (base_ref[base_ref.shape[0] - 1] + CHUNK - 1) // CHUNK
    total = tags_ref.shape[1]
    pick = jnp.where(iota((16, 128), 0) == iota((16, 128), 1), 1.0, 0.0).astype(BF)
    base = pl.program_id(0) * total
    found[...] = jnp.zeros_like(found)

    def step(c, _):
        at = pl.ds(pl.multiple_of(c * CHUNK, CHUNK), CHUNK)
        lines = mm(pick, table_ref[at, :], NT)
        seat = 64.0 * lines[1:2] + lines[2:3] - first
        seated = (lines[5:6] > 0.5) & (seat >= 0.0) & (seat < float(SEATS))
        code = jnp.where(seated, lines[0:1] * float(SEAT) + seat, -1.0).astype(jnp.int32)
        code_ref[:, at] = jnp.broadcast_to(code, (8, CHUNK))
        member = jnp.where(iota((total, 1), 0) + base == code, 1.0, 0.0).astype(BF)
        found[...] += mm(lines.astype(BF), member, NT)
        return 0

    lax.fori_loop(0, chunks, step, 0)
    rounds = jnp.floor((jnp.max(most_ref[...]) + (SEATS - 1.0)) * (1.0 / SEATS) + 1e-3)
    line = iota((8, total), 0)
    tags_ref[...] = jnp.where(
        line == 0, found[3:4, :], jnp.where(line == 1, found[4:5, :], rounds)
    )


def plan_seats(step, base, most, table, devices):
    total = devices * SEAT
    part = min(2048, total)
    return pl.pallas_call(
        plan_kernel,
        grid=(total // part,),
        out_shape=(
            jax.ShapeDtypeStruct((8, table.shape[0]), jnp.int32),
            jax.ShapeDtypeStruct((8, total), F32),
        ),
        in_specs=[SMEM, SMEM, VMEM, VMEM],
        out_specs=(
            pl.BlockSpec((8, table.shape[0]), lambda i: (0, 0)),
            pl.BlockSpec((8, part), lambda i: (0, i)),
        ),
        scratch_shapes=[pltpu.VMEM((16, part), F32)],
        compiler_params=ROOM,
        cost_estimate=cost(64 * total * table.shape[0], 4 * table.size),
    )(step, base, most, table)


def rotate_rows(doubled, turn, span):
    coarse = pl.multiple_of(turn // 8 * 8, 8)
    fine = turn % 8
    width = doubled.shape[1]
    rows = doubled[pl.ds(coarse, span + 8), :].reshape(span // 8 + 1, 8, width)
    rolled = pltpu.roll(rows, (8 - fine) % 8, 1)
    kept = iota((span // 8, 8, width), 1) < 8 - fine
    return jnp.where(kept, rolled[:-1], rolled[1:]).reshape(span, width)


def attend_kernel(
    index_ref,
    low_ref,
    count_ref,
    base_ref,
    turn_ref,
    local_ref,
    ids_ref,
    w_ref,
    wo_ref,
    rows_ref,
    out_ref,
    x,
    qx,
    kx,
    vx,
    att,
    doubled,
    wrapped,
    code,
    sems,
):
    tiles, span = ids_ref.shape
    width = w_ref.shape[0]
    cols = HEAD_GROUP * HDIM
    groups = width // cols
    heads = width // HDIM
    per_tile = span // ROWS

    def fetch(t):
        for s in range(t * per_tile, (t + 1) * per_tile):
            pltpu.make_async_copy(
                rows_ref.at[pl.ds(pl.multiple_of(index_ref[s] * ROWS, ROWS), ROWS)],
                x.at[pl.ds(s * ROWS, ROWS)],
                sems.at[t],
            ).start()

    fetch(0)
    out_ref[...] = jnp.zeros_like(out_ref)
    lane = iota((ROWS, 2 * cols), 1)
    of_head = [(lane // HDIM == h) | (lane >= cols) for h in range(HEAD_GROUP)]
    lane_out = lane % cols // HDIM
    for g in range(groups):
        vx[g, :, cols:] = jnp.ones((tiles * span, cols), BF)
    r_i = iota((cols, cols), 0)
    c_i = iota((cols, cols), 1)
    far = jnp.where((r_i != c_i) & (c_i < PATCHES), -FAR, 0.0).astype(BF)
    bounds = []

    for t in range(tiles):
        at = slice(t * span, (t + 1) * span)
        if t + 1 < tiles:
            fetch(t + 1)
        pltpu.make_async_copy(
            rows_ref.at[pl.ds(0, span)], x.at[pl.ds(t * span, span)], sems.at[t]
        ).wait()
        whole = x[at, :].astype(F32)
        doubled[:span, :] = whole
        doubled[span:, :] = whole
        tile_rows = rotate_rows(doubled, turn_ref[t], span).astype(BF)
        x[at, :] = tile_rows
        same = ids_ref[t : t + 1, :] == iota((cols, span), 0)
        patch_hot = jnp.where(same, 1.0, 0.0).astype(BF)
        query = mm(tile_rows, w_ref[:, :width])
        keys = mm(w_ref[:, width : 2 * width], tile_rows, (((0,), (1,)), ((), ())))
        value = mm(tile_rows, w_ref[:, 2 * width :]).astype(BF)
        patch_far = mm(patch_hot, far, TN).astype(BF)
        for g in range(groups):
            some = slice(g * cols, (g + 1) * cols)
            qx[g, at, :cols] = query[:, some].astype(BF)
            qx[g, at, cols:] = patch_far
            kx[g, :cols, at] = keys[some].astype(BF)
            kx[g, cols:, at] = patch_hot
            vx[g, at, :cols] = value[:, some]
        query_most = jnp.max(jnp.abs(query), axis=0, keepdims=True)
        key_most = jnp.max(jnp.abs(keys), axis=1, keepdims=True)
        by_head = jnp.where(
            iota((heads, width), 1) // HDIM == iota((heads, width), 0), query_most, 0.0
        )
        bounds.append(mm(by_head.astype(BF), jnp.broadcast_to(key_most, (width, 128)).astype(BF)))
    bound = bounds[0]
    for other in bounds[1:]:
        bound = jnp.maximum(bound, other)
    safe = jnp.max(bound) * SCORE_SCALE < SCORE_SAFE

    def block(s, _):
        start = pl.multiple_of(s // per_tile * span, span)
        steps = count_ref[s]
        here = pl.ds(pl.multiple_of(s * ROWS, ROWS), ROWS)

        def run(first, length, exact):
            at = pl.ds(pl.multiple_of(start + first, ROWS), length)
            scores = []
            for g in range(groups):
                q = qx[g, here, :]
                stacked = jnp.concatenate(
                    [jnp.where(of_head[h], q, jnp.zeros_like(q)) for h in range(HEAD_GROUP)],
                    axis=0,
                )
                scores.append(mm(stacked, kx[g, :, at]))
            for g in range(groups):
                level = scores[g] * SCORE_SCALE
                if exact:
                    level = level - jnp.max(level, axis=1, keepdims=True)
                weights = jnp.exp2(level).astype(BF)
                mixed = mm(weights, vx[g, at, :])
                mixed = mixed.reshape(HEAD_GROUP, ROWS, 2 * cols)
                own = mixed[0]
                for h in range(1, HEAD_GROUP):
                    own = jnp.where(lane_out == h, mixed[h], own)
                att[here, g * cols : (g + 1) * cols] = (own[:, :cols] / own[:, cols:]).astype(BF)

        for i in range(span // WINDOW):
            pl.when(safe & (steps == i + 1))(
                functools.partial(run, low_ref[s], (i + 1) * WINDOW, False)
            )
        pl.when(jnp.logical_not(safe))(functools.partial(run, 0, span, True))
        return 0

    lax.fori_loop(0, tiles * per_tile, block, 0)

    for t in range(tiles):
        at = slice(t * span, (t + 1) * span)
        turn = turn_ref[t]
        mixed = (x[at, :].astype(F32) + mm(att[at, :], wo_ref[...])).astype(BF)
        wrapped[t, :span, :] = mixed
        wrapped[t, span:, :] = mixed[:ROWS]
        runs = local_ref[t : t + 1, :] + iota((1, span), 1) // ROWS * ROWS
        runs = pltpu.roll(jnp.broadcast_to(runs, (8, span)), lax.rem(span - turn, span), 1)
        code[t, :, :span] = runs
        code[t, :, span:] = runs[:, :ROWS]
        for b in range(per_tile):
            first = lax.rem(b * ROWS + span - turn, span) // ROWS * ROWS
            window = pl.ds(pl.multiple_of(first, ROWS), 2 * ROWS)
            run = iota((ROWS, 2 * ROWS), 0) + b * ROWS == code[t, 0:1, window]
            sums = mm(jnp.where(run, 1.0, 0.0).astype(BF), wrapped[t, window, :])
            put = pl.multiple_of(base_ref[t * per_tile + b], ALIGN)
            out_ref[pl.ds(put, ROWS), :] = sums.astype(BF)


def attend(index, low, count, base, turn, local, ids, w_qkv, w_out, rows):
    tiles, span = ids.shape
    width = rows.shape[1]
    cols = HEAD_GROUP * HDIM
    groups = width // cols
    pairs = tiles * span * span * HEAD_GROUP
    return pl.pallas_call(
        attend_kernel,
        out_shape=jax.ShapeDtypeStruct((tiles * span + CHUNK, width), BF),
        in_specs=[SMEM, SMEM, SMEM, SMEM, SMEM, VMEM, VMEM, VMEM, VMEM, HBM],
        out_specs=VMEM,
        scratch_shapes=[
            pltpu.VMEM((tiles * span, width), BF),
            pltpu.VMEM((groups, tiles * span, 2 * cols), BF),
            pltpu.VMEM((groups, 2 * cols, tiles * span), BF),
            pltpu.VMEM((groups, tiles * span, 2 * cols), BF),
            pltpu.VMEM((tiles * span, width), BF),
            pltpu.VMEM((2 * span, width), F32),
            pltpu.VMEM((tiles, span + ROWS, width), BF),
            pltpu.VMEM((tiles, 8, span + ROWS), jnp.int32),
            pltpu.SemaphoreType.DMA((tiles,)),
        ],
        compiler_params=ROOM,
        cost_estimate=cost(pairs * 1024, 4 * rows.size, pairs),
    )(index, low, count, base, turn, local, ids, w_qkv, w_out, rows)


def route_kernel(base_ref, code_ref, tags_ref, sums_ref, out_ref, acc):
    total = out_ref.shape[0]
    chunks = (base_ref[base_ref.shape[0] - 1] + CHUNK - 1) // CHUNK
    seat = iota((total, 1), 0) + pl.program_id(0) * total
    acc[...] = jnp.zeros_like(acc)

    def step(c, _):
        at = pl.ds(pl.multiple_of(c * CHUNK, CHUNK), CHUNK)
        member = jnp.where(seat == code_ref[0:1, at], 1.0, 0.0).astype(BF)
        acc[...] += mm(member, sums_ref[at, :])
        return 0

    lax.fori_loop(0, chunks, step, 0)
    line = iota((SEAT - SEATS, SEAT), 0)
    for d in range(total // SEAT):
        low = d * SEAT
        here = slice(low, low + SEAT)
        out_ref[low : low + SEATS, :] = acc[low : low + SEATS, :].astype(BF)
        origin = jnp.where(
            line == 0, tags_ref[0:1, here], jnp.where(line == 1, tags_ref[2:3, here], 0.0)
        )
        place = jnp.where(line == 0, tags_ref[1:2, here], 0.0)
        out_ref[low + SEATS : low + SEAT, :] = jnp.concatenate([origin, place], axis=1).astype(BF)


def route_sums(base, code, tags, sums):
    count, width = sums.shape
    total = tags.shape[1]
    part = min(2048, total)
    return pl.pallas_call(
        route_kernel,
        grid=(total // part,),
        out_shape=jax.ShapeDtypeStruct((total, width), BF),
        in_specs=[
            SMEM,
            VMEM,
            pl.BlockSpec((8, part), lambda i: (0, i)),
            VMEM,
        ],
        out_specs=pl.BlockSpec((part, width), lambda i: (i, 0)),
        scratch_shapes=[pltpu.VMEM((part, width), F32)],
        compiler_params=ROOM,
        cost_estimate=cost(total * count * width, 4 * count * width),
    )(base, code, tags, sums)


def seat_targets(per_owner, pieces_ref, target):
    valid = iota((1, SEAT), 1) < SEATS
    for h in range(pieces_ref.shape[0] // SEAT):
        tag = pieces_ref[h * SEAT + SEATS : (h + 1) * SEAT, :].astype(F32)[0:1]
        where = tag[:, :SEAT] * float(per_owner) + tag[:, SEAT:]
        target[0:1, h * SEAT : (h + 1) * SEAT] = jnp.where(valid, where, -1.0).astype(jnp.int32)


def fold_kernel(per_owner, pieces_ref, before_ref, out_ref, target):
    step = pl.program_id(0)
    parents = out_ref.shape[0]
    chunk = pieces_ref.shape[0]

    @pl.when(step == 0)
    def _():
        out_ref[...] = before_ref[...]

    seat_targets(per_owner, pieces_ref, target)
    member = jnp.where(iota((parents, 1), 0) == target[0:1, :], 1.0, 0.0).astype(BF)
    out_ref[...] += mm(member, pieces_ref[...])


def fold_pieces(pieces, before, per_owner):
    parents, width = before.shape
    chunk = min(2048, pieces.shape[0])
    fixed = lambda i: (0, 0)
    return pl.pallas_call(
        functools.partial(fold_kernel, per_owner),
        grid=(pieces.shape[0] // chunk,),
        out_shape=jax.ShapeDtypeStruct((parents, width), F32),
        in_specs=[
            pl.BlockSpec((chunk, width), lambda i: (i, 0)),
            pl.BlockSpec((parents, width), fixed),
        ],
        out_specs=pl.BlockSpec((parents, width), fixed),
        scratch_shapes=[pltpu.VMEM((8, chunk), jnp.int32)],
        compiler_params=ROOM,
        cost_estimate=cost(2 * parents * pieces.size, 4 * pieces.size),
    )(pieces, before)


def whole_tiles(rows):
    return (rows + 15) // 16 * 16


def pad_rows(value):
    spare = whole_tiles(value.shape[0]) - value.shape[0]
    if spare == 0:
        return value
    return jnp.concatenate([value, jnp.zeros((spare, value.shape[1]), value.dtype)], axis=0)


def pool_kernel(
    per_owner,
    pieces_ref,
    more_ref,
    length_ref,
    w_ref,
    gain_ref,
    shift_ref,
    cot_ref,
    pooled_ref,
    sent_ref,
    acc,
    sums,
    target,
):
    step = pl.program_id(0)

    @pl.when(step == 0)
    def _():
        acc[...] = jnp.zeros_like(acc)
        sums[...] = jnp.zeros_like(sums)
        seat_targets(per_owner, pieces_ref, target)

    chunk, width = more_ref.shape
    total = more_ref[...]
    parent = iota((chunk, 1), 0) + step * chunk
    part = min(2048, pieces_ref.shape[0])
    for low in range(0, pieces_ref.shape[0], part):
        member = jnp.where(parent == target[0:1, low : low + part], 1.0, 0.0).astype(BF)
        total = total + mm(member, pieces_ref[low : low + part, :])
    lengths = jnp.concatenate([length_ref[...]] * (width // 128), axis=1)
    parent_in = (total / lengths).astype(BF)
    w_pool = w_ref[...]
    gain = gain_ref[...]
    projected = mm(parent_in, w_pool)
    centred = projected - jnp.mean(projected, axis=-1, keepdims=True)
    variance = jnp.mean(centred * centred, axis=-1, keepdims=True)
    inv_std = lax.rsqrt(variance + norm_eps)
    normed = centred * inv_std
    shifted = normed * gain + shift_ref[...]
    normal_cdf = 0.5 * (1.0 + lax.erf(shifted * inv_sqrt_two))
    pooled_ref[...] = (shifted * normal_cdf).astype(BF)
    grad_act = cot_ref[...].astype(F32) * (
        normal_cdf + shifted * jnp.exp(-0.5 * shifted * shifted) * inv_sqrt_tau
    )
    sums[0:1, :] += jnp.sum(grad_act * normed, axis=0, keepdims=True)
    sums[1:2, :] += jnp.sum(grad_act, axis=0, keepdims=True)
    scaled = grad_act * gain
    grad_proj = (
        (
            scaled
            - jnp.mean(scaled, axis=-1, keepdims=True)
            - normed * jnp.mean(scaled * normed, axis=-1, keepdims=True)
        )
        * inv_std
    ).astype(BF)
    acc[...] += mm(parent_in, grad_proj, TN)
    back = mm(grad_proj, w_pool, NT)
    devices, _, width = sent_ref.shape
    fits = chunk // per_owner
    for d in range(fits):
        part = back[d * per_owner : (d + 1) * per_owner]
        sent_ref[step * fits + d, : whole_tiles(per_owner), :] = pad_rows(part).astype(BF)

    @pl.when(step == pl.num_programs(0) - 1)
    def _():
        each = acc.shape[0] // devices
        tall = whole_tiles(each)
        exact = sums[0:2, :]
        high = exact.astype(BF).astype(F32)
        parts = []
        for value in (high, exact - high):
            for row in range(2):
                for low in range(0, acc.shape[1], width):
                    parts.append(value[row : row + 1, low : low + width])
        norm = pad_rows(jnp.concatenate(parts, axis=0)).astype(BF)
        for d in range(devices):
            low = whole_tiles(per_owner)
            for side in range(0, acc.shape[1], width):
                part = acc[d * each : (d + 1) * each, side : side + width]
                sent_ref[d, low : low + tall, :] = pad_rows(part).astype(BF)
                low += tall
            sent_ref[d, low:, :] = norm


def pool(pieces, more, length, w_pool, gain, shift, cotangent):
    parents, width = more.shape
    wide = w_pool.shape[1]
    chunk = 256
    devices = pieces.shape[0] // SEAT
    tall = whole_tiles(parents // devices) + wide // width * whole_tiles(width // devices)
    tall += whole_tiles(4 * wide // width)
    fixed = lambda i: (0, 0)
    along = lambda i: (i, 0)
    return pl.pallas_call(
        functools.partial(pool_kernel, parents * SEAT // pieces.shape[0]),
        grid=(parents // chunk,),
        out_shape=(
            jax.ShapeDtypeStruct((parents, wide), BF),
            jax.ShapeDtypeStruct((devices, tall, width), BF),
        ),
        in_specs=[
            pl.BlockSpec(pieces.shape, fixed),
            pl.BlockSpec((chunk, width), along),
            pl.BlockSpec((chunk, 128), along),
            pl.BlockSpec((width, wide), fixed),
            pl.BlockSpec((1, wide), fixed),
            pl.BlockSpec((1, wide), fixed),
            pl.BlockSpec((chunk, wide), along),
        ],
        out_specs=(
            pl.BlockSpec((chunk, wide), along),
            pl.BlockSpec((devices, tall, width), lambda i: (0, 0, 0)),
        ),
        scratch_shapes=[
            pltpu.VMEM((width, wide), F32),
            pltpu.VMEM((8, wide), F32),
            pltpu.VMEM((8, pieces.shape[0]), jnp.int32),
        ],
        compiler_params=FULL,
        cost_estimate=cost(6 * parents * width * wide, 8 * parents * wide, 2 * parents * wide),
    )(pieces, more, length, w_pool, gain, shift, cotangent)


def spread_kernel(span_ref, grad_ref, out_ref, share):
    step = pl.program_id(0)
    chunk = out_ref.shape[0]
    parents, width = share.shape

    @pl.when(step == 0)
    def _():
        pick = jnp.where(iota((8, width), 0) == 2, 1.0, 0.0).astype(BF)
        lengths = mm(jnp.minimum(span_ref[...], 64).astype(F32).astype(BF), pick, TN)
        per_owner = parents // grad_ref.shape[0]
        grads = [grad_ref[d, :per_owner, :].astype(F32) for d in range(grad_ref.shape[0])]
        share[...] = (jnp.concatenate(grads, axis=0) / lengths).astype(BF)

    row = iota((chunk, parents), 0) + step * chunk
    inside = (row >= span_ref[0:1, :]) & (row < span_ref[1:2, :])
    out_ref[...] = mm(jnp.where(inside, 1.0, 0.0).astype(BF), share[...]).astype(BF)


def spread_grads(span, arrived, rows):
    parents = span.shape[1]
    width = arrived.shape[2]
    chunk = 512
    fixed = lambda i: (0, 0)
    return pl.pallas_call(
        spread_kernel,
        grid=(rows // chunk,),
        out_shape=jax.ShapeDtypeStruct((rows, width), BF),
        in_specs=[
            pl.BlockSpec((8, parents), fixed),
            pl.BlockSpec(arrived.shape, lambda i: (0, 0, 0)),
        ],
        out_specs=pl.BlockSpec((chunk, width), lambda i: (i, 0)),
        scratch_shapes=[pltpu.VMEM((parents, width), BF)],
        compiler_params=ROOM,
        cost_estimate=cost(2 * rows * parents * width, 4 * rows * width),
    )(span, arrived)


def settle_kernel(per_owner, arrived_ref, shared_ref, norm_ref):
    devices, tall, width = arrived_ref.shape
    low = whole_tiles(per_owner)
    total = arrived_ref[0, low:, :].astype(F32)
    for d in range(1, devices):
        total = total + arrived_ref[d, low:, :].astype(F32)
    weight_rows = shared_ref.shape[1]
    weight = total[:weight_rows].astype(BF)
    for d in range(devices):
        shared_ref[d] = weight
    norm = total[weight_rows : weight_rows + 8]
    sides = norm_ref.shape[1] // width
    for row in range(2):
        for side in range(sides):
            i = row * sides + side
            value = norm[i : i + 1] + norm[2 * sides + i : 2 * sides + i + 1]
            norm_ref[row : row + 1, side * width : (side + 1) * width] = value


def settle(arrived, per_owner, weight_rows, wide):
    devices, tall, width = arrived.shape
    return pl.pallas_call(
        functools.partial(settle_kernel, per_owner),
        out_shape=(
            jax.ShapeDtypeStruct((devices, weight_rows, width), BF),
            jax.ShapeDtypeStruct((2, wide), F32),
        ),
        in_specs=[VMEM],
        out_specs=(VMEM, VMEM),
        compiler_params=ROOM,
        cost_estimate=cost(arrived.size, 2 * arrived.size),
    )(arrived)


def swap(parts):
    return lax.all_to_all(parts, "pts", split_axis=0, concat_axis=0, tiled=True)


def exchange(rows, devices):
    return swap(rows.reshape(devices, rows.shape[0] // devices, rows.shape[1])).reshape(rows.shape)


def received_index(codes, blocks, capacity):
    devices = codes.shape[0]
    me = lax.axis_index("pts")
    mine = codes // blocks == me
    slots = codes % blocks
    lane = jnp.arange(blocks)
    rank = jnp.sum(mine[:, None, :] & (lane[None, :] < lane[:, None])[None], axis=2)
    index = jnp.arange(devices)[:, None] * capacity + rank
    both = index * blocks + lane[None, :]
    hit = mine[:, :, None] & (slots[:, :, None] == lane[None, None, :])
    both = jnp.sum(jnp.where(hit, both[:, :, None], 0), axis=(0, 1)).astype(jnp.int32)
    return both // blocks, both % blocks


def key_windows(patch_ids):
    tiles, span = patch_ids.shape
    patch = jnp.arange(PATCHES)
    sizes = jnp.sum(patch_ids[:, None, :] == patch[None, :, None], axis=2)
    starts = jnp.sum(jnp.where(patch[None, :] < patch[:, None], sizes[:, None, :], 0), axis=2)
    longest = sizes == jnp.max(sizes, axis=1, keepdims=True)
    turn = jnp.min(jnp.where(longest, starts, span), axis=1)
    firsts = (starts - turn[:, None]) % span
    row = jnp.arange(span)[None, :, None]
    inside = (row >= firsts[:, None, :]) & (row < (firsts + sizes)[:, None, :])
    turned = jnp.sum(jnp.where(inside, patch, 0), axis=2)
    block = jnp.arange(0, span, ROWS)[None, :, None]
    starts_in = (block >= firsts[:, None, :]) & (block < (firsts + sizes)[:, None, :])
    ending = block + ROWS - 1
    ends_in = (ending >= firsts[:, None, :]) & (ending < (firsts + sizes)[:, None, :])
    low = jnp.sum(jnp.where(starts_in, firsts[:, None, :], 0), axis=2) // ROWS * ROWS
    high = jnp.sum(jnp.where(ends_in, (firsts + sizes)[:, None, :], 0), axis=2)
    count = (high - low + WINDOW - 1) // WINDOW
    low = jnp.minimum(low, span - count * WINDOW)
    as_int = lambda value: value.astype(jnp.int32)
    return as_int(low.reshape(-1)), as_int(count.reshape(-1)), as_int(turn), as_int(turned)


def local(
    points,
    hil_dest,
    hil_slot,
    patch_ids,
    child_counts,
    parent_order,
    w_qkv,
    w_out,
    w_pool,
    norm_gain,
    norm_shift,
    cotangent,
):
    devices = lax.axis_size("pts")
    blocks = hil_dest.shape[0]
    rows, width = points.shape
    wide = w_pool.shape[1]
    parents = child_counts.shape[1]
    per_owner = parents // devices
    capacity = (blocks + devices - 1) // devices

    me = lax.axis_index("pts")
    info, span = order_tables(child_counts, parent_order, hil_dest, hil_slot, devices)
    info = swap(info)
    payload = pack_blocks(hil_dest, points, devices, capacity)
    received = exchange(payload, devices)
    index, block = received_index(info[:, parents // 128, :blocks], blocks, capacity)
    source = index // capacity
    table, local_run, base, most = seat_rows(
        source, block, info.reshape(devices * INFO, 128), per_owner
    )
    code, tags = plan_seats(jnp.zeros((1,), jnp.int32), base, most, table, devices)
    low, count, turn, turned = key_windows(patch_ids)
    lengths = lax.dynamic_slice_in_dim(
        info[:, : parents // 128].reshape(devices, parents), me * per_owner, per_owner, axis=1
    )
    lengths = lengths.reshape(parents, 1) % 16
    lengths = jnp.broadcast_to(lengths.astype(F32), (parents, 128))
    more = jnp.zeros((parents, width), F32)
    index, low, count, turn, turned, base, local_run, code, tags, lengths = (
        lax.optimization_barrier(
            (index, low, count, turn, turned, base, local_run, code, tags, lengths)
        )
    )
    local_run = local_run.reshape(patch_ids.shape)
    sums = attend(index, low, count, base, turn, local_run, turned, w_qkv, w_out, received)
    pieces = exchange(route_sums(base, code, tags, sums), devices)
    rounds = jnp.max(pieces.reshape(devices, SEAT, width)[:, SEATS + 1, 0].astype(F32))

    def turn(carry):
        step, before = carry
        code, tags = plan_seats(step.reshape(1), base, most, table, devices)
        late = exchange(route_sums(base, code, tags, sums), devices)
        return step + 1, fold_pieces(late, before, per_owner)

    _, more = lax.while_loop(
        lambda carry: carry[0] < rounds.astype(jnp.int32), turn, (jnp.int32(1), more)
    )
    pooled, outgoing = pool(
        pieces, more, lengths, w_pool, norm_gain[None], norm_shift[None], cotangent
    )
    arrived = swap(outgoing)
    each = width // devices
    tall = whole_tiles(each)
    sides = wide // width
    shared, grad_norm = settle(arrived, per_owner, sides * tall, wide)
    shared = swap(shared)
    grad_weight = jnp.concatenate(
        [shared[:, side * tall : side * tall + each] for side in range(sides)], axis=2
    )
    grad_weight = grad_weight.reshape(width, wide).astype(F32)
    grad_points = spread_grads(span, arrived, rows)
    return (pooled, grad_points, grad_weight, grad_norm)


def solution(mesh):
    in_specs = (
        P(("grp", "pts"), None),
        P(("grp", "pts")),
        P(("grp", "pts")),
        P(("grp", "pts"), None),
        P(("grp", "pts"), None),
        P(("grp", "pts"), None),
        P(),
        P(),
        P(),
        P(),
        P(),
        P(("grp", "pts"), None),
    )
    out_specs = (P(("grp", "pts"), None), P(("grp", "pts"), None), P("grp", None), P("grp", None))
    return jax.shard_map(local, mesh=mesh, in_specs=in_specs, out_specs=out_specs, check_vma=False)
```

```python
import functools
import math

import jax
import jax.numpy as jnp
from jax import lax
from jax.experimental import pallas as pl
from jax.experimental.pallas import tpu as pltpu
from jax.sharding import PartitionSpec as P

HDIM = 16
HEAD_GROUP = 8
ROWS = 128
SEAT = 112
TURN = 16 * SEAT
INFO = 16
ALIGN = 16
CHUNK = 512
WINDOW = 256
PATCHES = 4
FAR = 2.0**100
SCORE_SCALE = HDIM**-0.5 * math.log2(math.e)
SCORE_SAFE = 98.0

inv_sqrt_two = 0.7071067811865476
inv_sqrt_tau = 0.3989422804014327
norm_eps = 1e-05

BF = jnp.bfloat16
F32 = jnp.float32
NT = (((1,), (1,)), ((), ()))
TN = (((0,), (0,)), ((), ()))
VMEM = pl.BlockSpec(memory_space=pltpu.VMEM)
HBM = pl.BlockSpec(memory_space=pltpu.HBM)
SMEM = pl.BlockSpec(memory_space=pltpu.SMEM)
ANY = pl.BlockSpec(memory_space=pl.ANY)
ROOM = pltpu.CompilerParams(vmem_limit_bytes=48 << 20)
FULL = pltpu.CompilerParams(vmem_limit_bytes=60 << 20)


def iota(shape, dim):
    return lax.broadcasted_iota(jnp.int32, shape, dim)


def mm(a, b, dims=(((1,), (0,)), ((), ()))):
    return lax.dot_general(a, b, dims, preferred_element_type=F32)


def cost(flops, bytes_accessed, transcendentals=0):
    return pl.CostEstimate(
        flops=int(flops), bytes_accessed=int(bytes_accessed), transcendentals=int(transcendentals)
    )


def order_kernel(counts_ref, order_ref, dest_ref, slot_ref, info_ref, span_ref):
    parents = counts_ref.shape[1]
    blocks = dest_ref.shape[1]
    counts = jnp.broadcast_to(counts_ref[...], (8, parents)).astype(F32)
    upper = jnp.where(iota((parents, parents), 0) <= iota((parents, parents), 1), 1.0, 0.0)
    starts = mm(counts.astype(BF), upper.astype(BF)) - counts
    coarse = jnp.floor(starts * (1.0 / 64.0))
    which = iota((8, parents), 0)
    fields = jnp.where(which == 0, coarse, jnp.where(which == 1, starts - 64.0 * coarse, counts))
    pick = jnp.where(iota((parents, parents), 0) == order_ref[...], 1.0, 0.0).astype(BF)
    ordered = mm(fields.astype(BF), pick).astype(jnp.int32)
    first = 64 * ordered[0:1] + ordered[1:2]
    length = ordered[2:3]
    span_ref[...] = jnp.where(which == 0, first, jnp.where(which == 1, first + length, length))
    both = 16 * first + length
    lines = parents // 128
    info_ref[0, lines:, :] = jnp.zeros((INFO - lines, 128), jnp.int32)
    info_ref[0, lines : lines + 1, :blocks] = dest_ref[...] * blocks + slot_ref[...]
    for i in range(lines):
        info_ref[0, i : i + 1, :] = both[:, i * 128 : (i + 1) * 128]
    tile = info_ref[0]
    for d in range(1, info_ref.shape[0]):
        info_ref[d] = tile


def order_tables(child_counts, parent_order, hil_dest, hil_slot, devices):
    parents = child_counts.shape[1]
    return pl.pallas_call(
        order_kernel,
        out_shape=(
            jax.ShapeDtypeStruct((devices, INFO, 128), jnp.int32),
            jax.ShapeDtypeStruct((8, parents), jnp.int32),
        ),
        in_specs=[VMEM] * 4,
        out_specs=(VMEM, VMEM),
        compiler_params=FULL,
        cost_estimate=cost(32 * parents * parents, 8 * parents),
    )(child_counts, parent_order, hil_dest[None], hil_slot[None])


def pack_kernel(capacity, dest_ref, points_ref, payload_ref, used, sem):
    blocks = dest_ref.shape[0]

    def clear(d, _):
        used[d] = 0
        return 0

    lax.fori_loop(0, used.shape[0], clear, 0)

    def send(b, _):
        d = dest_ref[b]
        place = d * capacity + used[d]
        used[d] = used[d] + 1
        pltpu.make_async_copy(
            points_ref.at[pl.ds(pl.multiple_of(b * ROWS, ROWS), ROWS)],
            payload_ref.at[pl.ds(pl.multiple_of(place * ROWS, ROWS), ROWS)],
            sem,
        ).start()
        return 0

    lax.fori_loop(0, blocks, send, 0)
    whole = pl.ds(0, blocks * ROWS)
    pltpu.make_async_copy(points_ref.at[whole], payload_ref.at[whole], sem).wait()


def pack_blocks(hil_dest, points, devices, capacity):
    return pl.pallas_call(
        functools.partial(pack_kernel, capacity),
        out_shape=jax.ShapeDtypeStruct((devices * capacity * ROWS, points.shape[1]), BF),
        in_specs=[SMEM, HBM],
        out_specs=VMEM,
        scratch_shapes=[pltpu.SMEM((devices,), jnp.int32), pltpu.SemaphoreType.DMA],
        compiler_params=FULL,
        cost_estimate=cost(0, 4 * points.size),
    )(hil_dest, points)


def seat_kernel(
    per_owner,
    source_ref,
    block_ref,
    info_ref,
    table_ref,
    local_ref,
    base_ref,
    owner,
    place,
    seats,
):
    blocks = owner.shape[0]
    parents = 128 * 8
    devices = info_ref.shape[0] // INFO
    which = iota((16, parents), 0)
    rank = iota((16, parents), 1)
    fields = jnp.where(which == 0, rank // per_owner, jnp.where(which == 1, rank % per_owner, 0))
    fields = fields.astype(F32).astype(BF)

    def one(v, _):
        source = source_ref[v]
        packed = info_ref[pl.ds(pl.multiple_of(source * INFO, INFO), 8), :]
        line = jnp.concatenate([packed[i : i + 1] for i in range(8)], axis=1)
        first = line // 16
        row = block_ref[v] * ROWS + iota((ROWS, parents), 0)
        inside = (row >= first) & (row < first + line % 16)
        found = mm(fields, jnp.where(inside, 1.0, 0.0).astype(BF), NT)
        owner[pl.ds(v, 1), :] = found[0:1]
        place[pl.ds(v, 1), :] = found[1:2]
        return 0

    lax.fori_loop(0, blocks, one, 0)
    own = owner[...]
    run = own * per_owner + place[...]
    opens = (iota((blocks, ROWS), 1) == 0) | (run != pltpu.roll(run, 1, 1))
    opened = jnp.where(opens, 1.0, 0.0)
    upper = jnp.where(iota((ROWS, ROWS), 0) <= iota((ROWS, ROWS), 1), 1.0, 0.0).astype(BF)
    every = jnp.ones((ROWS, ROWS), BF)
    before = jnp.where(iota((blocks, blocks), 1) < iota((blocks, blocks), 0), 1.0, 0.0).astype(BF)
    local_ref[...] = (mm(opened.astype(BF), upper) - 1.0).astype(jnp.int32)

    def count(e, seat):
        here = own == e.astype(F32)
        marks = jnp.where(here, opened, 0.0).astype(BF)
        total = mm(marks, upper) + mm(before, mm(marks, every).astype(BF))
        return jnp.where(here, total - 1.0, seat)

    seats[...] = lax.fori_loop(0, devices, count, jnp.zeros((blocks, ROWS), F32))
    table_ref[...] = jnp.zeros_like(table_ref)
    field = iota((ROWS, ROWS), 0)

    def lay(v, base):
        base = pl.multiple_of(base, ALIGN)
        base_ref[v] = base
        at = pl.ds(v, 1)
        local = local_ref[at, :]
        seat = seats[at, :]
        coarse = jnp.floor(seat * (1.0 / 64.0))
        lines = (owner[at, :], coarse, seat - 64.0 * coarse)
        values = jnp.ones((ROWS, ROWS), F32)
        for i, line in enumerate(lines):
            values = jnp.where(field == i, line, values)
        previous = jnp.where(iota((1, ROWS), 1) == 0, -1, pltpu.roll(local, 1, 1))
        begins = (field == local) & (local != previous)
        found = mm(jnp.where(begins, 1.0, 0.0).astype(BF), values.astype(BF), NT)
        table_ref[pl.ds(base, ROWS), :] = found.astype(BF)
        return base + (jnp.max(local) + ALIGN) // ALIGN * ALIGN

    base_ref[blocks] = lax.fori_loop(0, blocks, lay, 0)


def seat_rows(source, block, info, per_owner):
    blocks = source.shape[0]
    rows = blocks * ROWS
    return pl.pallas_call(
        functools.partial(seat_kernel, per_owner),
        out_shape=(
            jax.ShapeDtypeStruct((rows + CHUNK, 128), BF),
            jax.ShapeDtypeStruct((blocks, ROWS), jnp.int32),
            jax.ShapeDtypeStruct((blocks + 1,), jnp.int32),
        ),
        in_specs=[SMEM, SMEM, VMEM],
        out_specs=(VMEM, VMEM, SMEM),
        scratch_shapes=[pltpu.VMEM((blocks, ROWS), F32)] * 3,
        compiler_params=ROOM,
        cost_estimate=cost(40 * rows * 1024, 8 * rows),
    )(source, block, info)


def plan_kernel(round_ref, base_ref, table_ref, code_ref):
    first = (SEAT * round_ref[0]).astype(F32)
    chunks = (base_ref[base_ref.shape[0] - 1] + CHUNK - 1) // CHUNK
    pick = jnp.where(iota((16, 128), 0) == iota((16, 128), 1), 1.0, 0.0).astype(BF)

    def step(c, _):
        at = pl.ds(pl.multiple_of(c * CHUNK, CHUNK), CHUNK)
        lines = mm(pick, table_ref[at, :], NT)
        seat = 64.0 * lines[1:2] + lines[2:3] - first
        seated = (lines[3:4] > 0.5) & (seat >= 0.0) & (seat < float(SEAT))
        code = jnp.where(seated, lines[0:1] * float(SEAT) + seat, -1.0).astype(jnp.int32)
        code_ref[:, at] = jnp.broadcast_to(code, (8, CHUNK))
        return 0

    lax.fori_loop(0, chunks, step, 0)


def plan_seats(step, base, table):
    return pl.pallas_call(
        plan_kernel,
        out_shape=jax.ShapeDtypeStruct((8, table.shape[0]), jnp.int32),
        in_specs=[SMEM, SMEM, VMEM],
        out_specs=VMEM,
        compiler_params=ROOM,
        cost_estimate=cost(64 * table.size, 4 * table.size),
    )(step, base, table)


def rotate_rows(doubled, turn, span):
    coarse = pl.multiple_of(turn // 8 * 8, 8)
    fine = turn % 8
    width = doubled.shape[1]
    rows = doubled[pl.ds(coarse, span + 8), :].reshape(span // 8 + 1, 8, width)
    rolled = pltpu.roll(rows, (8 - fine) % 8, 1)
    kept = iota((span // 8, 8, width), 1) < 8 - fine
    return jnp.where(kept, rolled[:-1], rolled[1:]).reshape(span, width)


def attend_kernel(
    index_ref,
    low_ref,
    count_ref,
    base_ref,
    turn_ref,
    local_ref,
    ids_ref,
    w_ref,
    wo_ref,
    rows_ref,
    out_ref,
    x,
    qx,
    kx,
    vx,
    att,
    doubled,
    wrapped,
    code,
    sems,
):
    tiles, span = ids_ref.shape
    width = w_ref.shape[0]
    cols = HEAD_GROUP * HDIM
    groups = width // cols
    heads = width // HDIM
    per_tile = span // ROWS

    def fetch(t):
        for s in range(t * per_tile, (t + 1) * per_tile):
            pltpu.make_async_copy(
                rows_ref.at[pl.ds(pl.multiple_of(index_ref[s] * ROWS, ROWS), ROWS)],
                x.at[pl.ds(s * ROWS, ROWS)],
                sems.at[t],
            ).start()

    fetch(0)
    out_ref[...] = jnp.zeros_like(out_ref)
    lane = iota((ROWS, 2 * cols), 1)
    of_head = [(lane // HDIM == h) | (lane >= cols) for h in range(HEAD_GROUP)]
    lane_out = lane % cols // HDIM
    for g in range(groups):
        vx[g, :, cols:] = jnp.ones((tiles * span, cols), BF)
    r_i = iota((cols, cols), 0)
    c_i = iota((cols, cols), 1)
    far = jnp.where((r_i != c_i) & (c_i < PATCHES), -FAR, 0.0).astype(BF)
    bounds = []

    for t in range(tiles):
        at = slice(t * span, (t + 1) * span)
        if t + 1 < tiles:
            fetch(t + 1)
        pltpu.make_async_copy(
            rows_ref.at[pl.ds(0, span)], x.at[pl.ds(t * span, span)], sems.at[t]
        ).wait()
        whole = x[at, :].astype(F32)
        doubled[:span, :] = whole
        doubled[span:, :] = whole
        tile_rows = rotate_rows(doubled, turn_ref[t], span).astype(BF)
        x[at, :] = tile_rows
        same = ids_ref[t : t + 1, :] == iota((cols, span), 0)
        patch_hot = jnp.where(same, 1.0, 0.0).astype(BF)
        query = mm(tile_rows, w_ref[:, :width])
        keys = mm(w_ref[:, width : 2 * width], tile_rows, (((0,), (1,)), ((), ())))
        value = mm(tile_rows, w_ref[:, 2 * width :]).astype(BF)
        patch_far = mm(patch_hot, far, TN).astype(BF)
        for g in range(groups):
            some = slice(g * cols, (g + 1) * cols)
            qx[g, at, :cols] = query[:, some].astype(BF)
            qx[g, at, cols:] = patch_far
            kx[g, :cols, at] = keys[some].astype(BF)
            kx[g, cols:, at] = patch_hot
            vx[g, at, :cols] = value[:, some]
        query_most = jnp.max(jnp.abs(query), axis=0, keepdims=True)
        key_most = jnp.max(jnp.abs(keys), axis=1, keepdims=True)
        by_head = jnp.where(
            iota((heads, width), 1) // HDIM == iota((heads, width), 0), query_most, 0.0
        )
        bounds.append(mm(by_head.astype(BF), jnp.broadcast_to(key_most, (width, 128)).astype(BF)))
    bound = bounds[0]
    for other in bounds[1:]:
        bound = jnp.maximum(bound, other)
    safe = jnp.max(bound) * SCORE_SCALE < SCORE_SAFE

    def block(s, _):
        start = pl.multiple_of(s // per_tile * span, span)
        steps = count_ref[s]
        here = pl.ds(pl.multiple_of(s * ROWS, ROWS), ROWS)

        def run(first, length, exact):
            at = pl.ds(pl.multiple_of(start + first, ROWS), length)
            scores = []
            for g in range(groups):
                q = qx[g, here, :]
                stacked = jnp.concatenate(
                    [jnp.where(of_head[h], q, jnp.zeros_like(q)) for h in range(HEAD_GROUP)],
                    axis=0,
                )
                scores.append(mm(stacked, kx[g, :, at]))
            for g in range(groups):
                level = scores[g] * SCORE_SCALE
                if exact:
                    level = level - jnp.max(level, axis=1, keepdims=True)
                weights = jnp.exp2(level).astype(BF)
                mixed = mm(weights, vx[g, at, :])
                mixed = mixed.reshape(HEAD_GROUP, ROWS, 2 * cols)
                own = mixed[0]
                for h in range(1, HEAD_GROUP):
                    own = jnp.where(lane_out == h, mixed[h], own)
                att[here, g * cols : (g + 1) * cols] = (own[:, :cols] / own[:, cols:]).astype(BF)

        for i in range(span // WINDOW):
            pl.when(safe & (steps == i + 1))(
                functools.partial(run, low_ref[s], (i + 1) * WINDOW, False)
            )
        pl.when(jnp.logical_not(safe))(functools.partial(run, 0, span, True))
        return 0

    lax.fori_loop(0, tiles * per_tile, block, 0)

    for t in range(tiles):
        at = slice(t * span, (t + 1) * span)
        turn = turn_ref[t]
        mixed = (x[at, :].astype(F32) + mm(att[at, :], wo_ref[...])).astype(BF)
        wrapped[t, :span, :] = mixed
        wrapped[t, span:, :] = mixed[:ROWS]
        runs = local_ref[t : t + 1, :] + iota((1, span), 1) // ROWS * ROWS
        runs = pltpu.roll(jnp.broadcast_to(runs, (8, span)), lax.rem(span - turn, span), 1)
        code[t, :, :span] = runs
        code[t, :, span:] = runs[:, :ROWS]
        for b in range(per_tile):
            first = lax.rem(b * ROWS + span - turn, span) // ROWS * ROWS
            window = pl.ds(pl.multiple_of(first, ROWS), 2 * ROWS)
            run = iota((ROWS, 2 * ROWS), 0) + b * ROWS == code[t, 0:1, window]
            sums = mm(jnp.where(run, 1.0, 0.0).astype(BF), wrapped[t, window, :])
            put = pl.multiple_of(base_ref[t * per_tile + b], ALIGN)
            out_ref[pl.ds(put, ROWS), :] = sums.astype(BF)


def attend(index, low, count, base, turn, local, ids, w_qkv, w_out, rows):
    tiles, span = ids.shape
    width = rows.shape[1]
    cols = HEAD_GROUP * HDIM
    groups = width // cols
    pairs = tiles * span * span * HEAD_GROUP
    return pl.pallas_call(
        attend_kernel,
        out_shape=jax.ShapeDtypeStruct((tiles * span + CHUNK, width), BF),
        in_specs=[SMEM, SMEM, SMEM, SMEM, SMEM, VMEM, VMEM, VMEM, VMEM, HBM],
        out_specs=VMEM,
        scratch_shapes=[
            pltpu.VMEM((tiles * span, width), BF),
            pltpu.VMEM((groups, tiles * span, 2 * cols), BF),
            pltpu.VMEM((groups, 2 * cols, tiles * span), BF),
            pltpu.VMEM((groups, tiles * span, 2 * cols), BF),
            pltpu.VMEM((tiles * span, width), BF),
            pltpu.VMEM((2 * span, width), F32),
            pltpu.VMEM((tiles, span + ROWS, width), BF),
            pltpu.VMEM((tiles, 8, span + ROWS), jnp.int32),
            pltpu.SemaphoreType.DMA((tiles,)),
        ],
        compiler_params=ROOM,
        cost_estimate=cost(pairs * 1024, 4 * rows.size, pairs),
    )(index, low, count, base, turn, local, ids, w_qkv, w_out, rows)


def route_kernel(base_ref, code_ref, sums_ref, out_ref, acc):
    total = out_ref.shape[0]
    chunks = (base_ref[base_ref.shape[0] - 1] + CHUNK - 1) // CHUNK
    seat = iota((total, 1), 0) + pl.program_id(0) * total
    acc[...] = jnp.zeros_like(acc)

    def step(c, _):
        at = pl.ds(pl.multiple_of(c * CHUNK, CHUNK), CHUNK)
        member = jnp.where(seat == code_ref[0:1, at], 1.0, 0.0).astype(BF)
        acc[...] += mm(member, sums_ref[at, :])
        return 0

    lax.fori_loop(0, chunks, step, 0)
    out_ref[...] = acc[...].astype(BF)


def route_sums(base, code, sums, devices):
    count, width = sums.shape
    total = devices * SEAT
    part = min(TURN, total)
    return pl.pallas_call(
        route_kernel,
        grid=(total // part,),
        out_shape=jax.ShapeDtypeStruct((total, width), BF),
        in_specs=[SMEM, VMEM, VMEM],
        out_specs=pl.BlockSpec((part, width), lambda i: (i, 0)),
        scratch_shapes=[pltpu.VMEM((part, width), F32)],
        compiler_params=ROOM,
        cost_estimate=cost(total * count * width, 4 * count * width),
    )(base, code, sums)


def fold_rows(step, pieces_ref, about):
    total = 0.0
    part = min(TURN, pieces_ref.shape[0])
    first = step * SEAT
    seats = []
    for i in (1, 3):
        seat = about[:, i + 1 : i + 2].astype(jnp.int32) - first
        seated = (seat >= 0) & (seat < SEAT)
        seats.append(jnp.where(seated, about[:, i : i + 1].astype(jnp.int32) * SEAT + seat, -1))
    for low in range(0, pieces_ref.shape[0], part):
        column = iota((1, part), 1) + low
        member = (column == seats[0]) | (column == seats[1])
        member = jnp.where(member, 1.0, 0.0).astype(BF)
        total = total + mm(member, pieces_ref[low : low + part, :])
    return total


def fold_kernel(step_ref, pieces_ref, about_ref, before_ref, out_ref):
    out_ref[...] = before_ref[...] + fold_rows(step_ref[0], pieces_ref, about_ref[...])


def fold_pieces(step, pieces, about, before):
    parents, width = before.shape
    chunk = 256
    along = lambda i: (i, 0)
    return pl.pallas_call(
        fold_kernel,
        grid=(parents // chunk,),
        out_shape=jax.ShapeDtypeStruct((parents, width), F32),
        in_specs=[
            SMEM,
            pl.BlockSpec(pieces.shape, lambda i: (0, 0)),
            pl.BlockSpec((chunk, 128), along),
            pl.BlockSpec((chunk, width), along),
        ],
        out_specs=pl.BlockSpec((chunk, width), along),
        compiler_params=ROOM,
        cost_estimate=cost(2 * parents * pieces.size, 4 * pieces.size),
    )(step, pieces, about, before)


def whole_tiles(rows):
    return (rows + 15) // 16 * 16


def pad_rows(value):
    spare = whole_tiles(value.shape[0]) - value.shape[0]
    if spare == 0:
        return value
    return jnp.concatenate([value, jnp.zeros((spare, value.shape[1]), value.dtype)], axis=0)


def pool_kernel(
    per_owner,
    pieces_ref,
    more_ref,
    about_ref,
    w_ref,
    gain_ref,
    shift_ref,
    cot_ref,
    pooled_ref,
    sent_ref,
    acc,
    sums,
):
    step = pl.program_id(0)

    @pl.when(step == 0)
    def _():
        acc[...] = jnp.zeros_like(acc)
        sums[...] = jnp.zeros_like(sums)

    chunk, width = more_ref.shape
    about = about_ref[...]
    total = more_ref[...] + fold_rows(0, pieces_ref, about)
    lengths = about[:, 0:1]
    parent_in = (total / lengths).astype(BF)
    w_pool = w_ref[...]
    gain = gain_ref[...]
    projected = mm(parent_in, w_pool)
    centred = projected - jnp.mean(projected, axis=-1, keepdims=True)
    variance = jnp.mean(centred * centred, axis=-1, keepdims=True)
    inv_std = lax.rsqrt(variance + norm_eps)
    normed = centred * inv_std
    shifted = normed * gain + shift_ref[...]
    normal_cdf = 0.5 * (1.0 + lax.erf(shifted * inv_sqrt_two))
    pooled_ref[...] = (shifted * normal_cdf).astype(BF)
    grad_act = cot_ref[...].astype(F32) * (
        normal_cdf + shifted * jnp.exp(-0.5 * shifted * shifted) * inv_sqrt_tau
    )
    sums[0:1, :] += jnp.sum(grad_act * normed, axis=0, keepdims=True)
    sums[1:2, :] += jnp.sum(grad_act, axis=0, keepdims=True)
    scaled = grad_act * gain
    grad_proj = (
        (
            scaled
            - jnp.mean(scaled, axis=-1, keepdims=True)
            - normed * jnp.mean(scaled * normed, axis=-1, keepdims=True)
        )
        * inv_std
    ).astype(BF)
    acc[...] += mm(parent_in, grad_proj, TN)
    back = mm(grad_proj, w_pool, NT)
    devices, _, width = sent_ref.shape
    fits = chunk // per_owner
    for d in range(fits):
        part = back[d * per_owner : (d + 1) * per_owner]
        sent_ref[step * fits + d, : whole_tiles(per_owner), :] = pad_rows(part).astype(BF)

    @pl.when(step == pl.num_programs(0) - 1)
    def _():
        each = acc.shape[0] // devices
        tall = whole_tiles(each)
        exact = sums[0:2, :]
        high = exact.astype(BF).astype(F32)
        parts = []
        for value in (high, exact - high):
            for row in range(2):
                for low in range(0, acc.shape[1], width):
                    parts.append(value[row : row + 1, low : low + width])
        norm = pad_rows(jnp.concatenate(parts, axis=0)).astype(BF)
        for d in range(devices):
            low = whole_tiles(per_owner)
            for side in range(0, acc.shape[1], width):
                part = acc[d * each : (d + 1) * each, side : side + width]
                sent_ref[d, low : low + tall, :] = pad_rows(part).astype(BF)
                low += tall
            sent_ref[d, low:, :] = norm


def pool(pieces, more, about, w_pool, gain, shift, cotangent):
    parents, width = more.shape
    wide = w_pool.shape[1]
    chunk = 512
    devices = pieces.shape[0] // SEAT
    tall = whole_tiles(parents // devices) + wide // width * whole_tiles(width // devices)
    tall += whole_tiles(4 * wide // width)
    fixed = lambda i: (0, 0)
    along = lambda i: (i, 0)
    return pl.pallas_call(
        functools.partial(pool_kernel, parents * SEAT // pieces.shape[0]),
        grid=(parents // chunk,),
        out_shape=(
            jax.ShapeDtypeStruct((parents, wide), BF),
            jax.ShapeDtypeStruct((devices, tall, width), BF),
        ),
        in_specs=[
            pl.BlockSpec(pieces.shape, fixed),
            pl.BlockSpec((chunk, width), along),
            pl.BlockSpec((chunk, 128), along),
            pl.BlockSpec((width, wide), fixed),
            pl.BlockSpec((1, wide), fixed),
            pl.BlockSpec((1, wide), fixed),
            pl.BlockSpec((chunk, wide), along),
        ],
        out_specs=(
            pl.BlockSpec((chunk, wide), along),
            pl.BlockSpec((devices, tall, width), lambda i: (0, 0, 0)),
        ),
        scratch_shapes=[
            pltpu.VMEM((width, wide), F32),
            pltpu.VMEM((8, wide), F32),
        ],
        compiler_params=FULL,
        cost_estimate=cost(6 * parents * width * wide, 8 * parents * wide, 2 * parents * wide),
    )(pieces, more, about, w_pool, gain, shift, cotangent)


def spread_kernel(span_ref, grad_ref, out_ref, share):
    step = pl.program_id(0)
    chunk = out_ref.shape[0]
    parents, width = share.shape

    @pl.when(step == 0)
    def _():
        pick = jnp.where(iota((8, width), 0) == 2, 1.0, 0.0).astype(BF)
        lengths = mm(jnp.minimum(span_ref[...], 64).astype(F32).astype(BF), pick, TN)
        per_owner = parents // grad_ref.shape[0]
        grads = [grad_ref[d, :per_owner, :].astype(F32) for d in range(grad_ref.shape[0])]
        share[...] = (jnp.concatenate(grads, axis=0) / lengths).astype(BF)

    row = iota((chunk, parents), 0) + step * chunk
    inside = (row >= span_ref[0:1, :]) & (row < span_ref[1:2, :])
    out_ref[...] = mm(jnp.where(inside, 1.0, 0.0).astype(BF), share[...]).astype(BF)


def spread_grads(span, arrived, rows):
    parents = span.shape[1]
    width = arrived.shape[2]
    chunk = 512
    fixed = lambda i: (0, 0)
    return pl.pallas_call(
        spread_kernel,
        grid=(rows // chunk,),
        out_shape=jax.ShapeDtypeStruct((rows, width), BF),
        in_specs=[
            pl.BlockSpec((8, parents), fixed),
            pl.BlockSpec(arrived.shape, lambda i: (0, 0, 0)),
        ],
        out_specs=pl.BlockSpec((chunk, width), lambda i: (i, 0)),
        scratch_shapes=[pltpu.VMEM((parents, width), BF)],
        compiler_params=ROOM,
        cost_estimate=cost(2 * rows * parents * width, 4 * rows * width),
    )(span, arrived)


def settle_kernel(per_owner, arrived_ref, shared_ref, norm_ref):
    devices, tall, width = arrived_ref.shape
    low = whole_tiles(per_owner)
    total = arrived_ref[0, low:, :].astype(F32)
    for d in range(1, devices):
        total = total + arrived_ref[d, low:, :].astype(F32)
    weight_rows = shared_ref.shape[1]
    weight = total[:weight_rows].astype(BF)
    for d in range(devices):
        shared_ref[d] = weight
    norm = total[weight_rows : weight_rows + 8]
    sides = norm_ref.shape[1] // width
    for row in range(2):
        for side in range(sides):
            i = row * sides + side
            value = norm[i : i + 1] + norm[2 * sides + i : 2 * sides + i + 1]
            norm_ref[row : row + 1, side * width : (side + 1) * width] = value


def settle(arrived, per_owner, weight_rows, wide):
    devices, tall, width = arrived.shape
    return pl.pallas_call(
        functools.partial(settle_kernel, per_owner),
        out_shape=(
            jax.ShapeDtypeStruct((devices, weight_rows, width), BF),
            jax.ShapeDtypeStruct((2, wide), F32),
        ),
        in_specs=[VMEM],
        out_specs=(VMEM, VMEM),
        compiler_params=ROOM,
        cost_estimate=cost(arrived.size, 2 * arrived.size),
    )(arrived)


def piece_seats(info, codes, blocks, per_owner):
    devices = codes.shape[0]
    parents = devices * per_owner
    me = lax.axis_index("pts")
    packed = info.reshape(devices, parents)
    span = blocks * ROWS
    lane = jnp.arange(blocks)

    def at_block(block):
        found = jnp.where(block[:, :, None] == lane, codes[:, None, :], 0)
        return jnp.sum(found, axis=2)

    first = packed // 16
    end = first + packed % 16 - 1
    near = at_block(first // ROWS)
    far = at_block(end // ROWS)
    split = first // ROWS != end // ROWS
    holders = jnp.arange(devices)
    by_owner = lambda value: value.reshape(devices, devices, per_owner, 1)
    filled = (by_owner(near // blocks) == holders).astype(jnp.int32)
    filled += (by_owner(jnp.where(split, far // blocks, -1)) == holders).astype(jnp.int32)
    rounds = (jnp.max(jnp.sum(filled, axis=(0, 2))) + SEAT - 1) // SEAT

    mine = lambda value: lax.dynamic_slice_in_dim(value, me * per_owner, per_owner, axis=1)
    near, far, split, first, packed = map(mine, (near, far, split, first, packed))
    near_key = near * ROWS + first % ROWS
    far_key = jnp.where(split, far * ROWS, devices * span)
    near_key, far_key = near_key.reshape(parents, 1), far_key.reshape(parents, 1)
    every = jnp.concatenate([near_key, far_key], axis=0).reshape(1, 2 * parents)

    def place(key):
        holder = key // span
        rank = jnp.sum((every < key) & (every >= holder * span), axis=1, keepdims=True)
        return holder, jnp.where(holder < devices, rank, -1)

    length = (packed % 16).reshape(parents, 1)
    columns = (length,) + place(near_key) + place(far_key)
    wide = iota((parents, 128), 1)
    about = jnp.zeros((parents, 128), jnp.int32)
    for i, column in enumerate(columns):
        about = jnp.where(wide == i, column, about)
    return about.astype(F32), rounds.astype(jnp.int32)


def swap(parts):
    return lax.all_to_all(parts, "pts", split_axis=0, concat_axis=0, tiled=True)


def exchange(rows, devices):
    return swap(rows.reshape(devices, rows.shape[0] // devices, rows.shape[1])).reshape(rows.shape)


def received_index(codes, blocks, capacity):
    devices = codes.shape[0]
    me = lax.axis_index("pts")
    mine = codes // blocks == me
    slots = codes % blocks
    lane = jnp.arange(blocks)
    rank = jnp.sum(mine[:, None, :] & (lane[None, :] < lane[:, None])[None], axis=2)
    index = jnp.arange(devices)[:, None] * capacity + rank
    both = index * blocks + lane[None, :]
    hit = mine[:, :, None] & (slots[:, :, None] == lane[None, None, :])
    both = jnp.sum(jnp.where(hit, both[:, :, None], 0), axis=(0, 1)).astype(jnp.int32)
    return both // blocks, both % blocks


def key_windows(patch_ids):
    tiles, span = patch_ids.shape
    patch = jnp.arange(PATCHES)
    sizes = jnp.sum(patch_ids[:, None, :] == patch[None, :, None], axis=2)
    starts = jnp.sum(jnp.where(patch[None, :] < patch[:, None], sizes[:, None, :], 0), axis=2)
    longest = sizes == jnp.max(sizes, axis=1, keepdims=True)
    turn = jnp.min(jnp.where(longest, starts, span), axis=1)
    firsts = (starts - turn[:, None]) % span
    row = jnp.arange(span)[None, :, None]
    inside = (row >= firsts[:, None, :]) & (row < (firsts + sizes)[:, None, :])
    turned = jnp.sum(jnp.where(inside, patch, 0), axis=2)
    block = jnp.arange(0, span, ROWS)[None, :, None]
    starts_in = (block >= firsts[:, None, :]) & (block < (firsts + sizes)[:, None, :])
    ending = block + ROWS - 1
    ends_in = (ending >= firsts[:, None, :]) & (ending < (firsts + sizes)[:, None, :])
    low = jnp.sum(jnp.where(starts_in, firsts[:, None, :], 0), axis=2) // ROWS * ROWS
    high = jnp.sum(jnp.where(ends_in, (firsts + sizes)[:, None, :], 0), axis=2)
    count = (high - low + WINDOW - 1) // WINDOW
    low = jnp.minimum(low, span - count * WINDOW)
    as_int = lambda value: value.astype(jnp.int32)
    return as_int(low.reshape(-1)), as_int(count.reshape(-1)), as_int(turn), as_int(turned)


def local(
    points,
    hil_dest,
    hil_slot,
    patch_ids,
    child_counts,
    parent_order,
    w_qkv,
    w_out,
    w_pool,
    norm_gain,
    norm_shift,
    cotangent,
):
    devices = lax.axis_size("pts")
    blocks = hil_dest.shape[0]
    rows, width = points.shape
    wide = w_pool.shape[1]
    parents = child_counts.shape[1]
    per_owner = parents // devices
    capacity = (blocks + devices - 1) // devices

    me = lax.axis_index("pts")
    info, span = order_tables(child_counts, parent_order, hil_dest, hil_slot, devices)
    info, patch_ids = lax.optimization_barrier((info, patch_ids))
    info = swap(info)
    payload = pack_blocks(hil_dest, points, devices, capacity)
    received = exchange(payload, devices)
    index, block = received_index(info[:, parents // 128, :blocks], blocks, capacity)
    source = index // capacity
    table, local_run, base = seat_rows(
        source, block, info.reshape(devices * INFO, 128), per_owner
    )
    code = plan_seats(jnp.zeros((1,), jnp.int32), base, table)
    low, count, turn, turned = key_windows(patch_ids)
    codes = info[:, parents // 128, :blocks]
    about, rounds = piece_seats(info[:, : parents // 128], codes, blocks, per_owner)
    more = jnp.broadcast_to(about[:, 127:], (parents, width))
    index, low, count, turn, turned, base, local_run, code, about, rounds, more = (
        lax.optimization_barrier(
            (index, low, count, turn, turned, base, local_run, code, about, rounds, more)
        )
    )
    local_run = local_run.reshape(patch_ids.shape)
    sums = attend(index, low, count, base, turn, local_run, turned, w_qkv, w_out, received)
    pieces = exchange(route_sums(base, code, sums, devices), devices)

    def turn_again(carry):
        step, before = carry
        step = step.reshape(1)
        late = exchange(route_sums(base, plan_seats(step, base, table), sums, devices), devices)
        return step[0] + 1, fold_pieces(step, late, about, before)

    _, more = lax.while_loop(
        lambda carry: carry[0] < rounds, turn_again, (jnp.int32(1), more)
    )
    pooled, outgoing = pool(
        pieces, more, about, w_pool, norm_gain[None], norm_shift[None], cotangent
    )
    arrived = swap(outgoing)
    each = width // devices
    tall = whole_tiles(each)
    sides = wide // width
    shared, grad_norm = settle(arrived, per_owner, sides * tall, wide)
    shared = swap(shared)
    grad_weight = jnp.concatenate(
        [shared[:, side * tall : side * tall + each] for side in range(sides)], axis=2
    )
    grad_weight = grad_weight.reshape(width, wide).astype(F32)
    grad_points = spread_grads(span, arrived, rows)
    return (pooled, grad_points, grad_weight, grad_norm)


def solution(mesh):
    in_specs = (
        P(("grp", "pts"), None),
        P(("grp", "pts")),
        P(("grp", "pts")),
        P(("grp", "pts"), None),
        P(("grp", "pts"), None),
        P(("grp", "pts"), None),
        P(),
        P(),
        P(),
        P(),
        P(),
        P(("grp", "pts"), None),
    )
    out_specs = (P(("grp", "pts"), None), P(("grp", "pts"), None), P("grp", None), P("grp", None))
    return jax.shard_map(local, mesh=mesh, in_specs=in_specs, out_specs=out_specs, check_vma=False)
```

```python
import functools
import math

import jax
import jax.numpy as jnp
from jax import lax
from jax.experimental import pallas as pl
from jax.experimental.pallas import tpu as pltpu
from jax.sharding import PartitionSpec as P

HDIM = 16
HEAD_GROUP = 8
ROWS = 128
SEAT = 104
TURN = 16 * SEAT
INFO = 8
ALIGN = 16
CHUNK = 512
WINDOW = 256
PATCHES = 4
FAR = 2.0**100
SCORE_SCALE = HDIM**-0.5 * math.log2(math.e)
SCORE_SAFE = 98.0

inv_sqrt_two = 0.7071067811865476
inv_sqrt_tau = 0.3989422804014327
norm_eps = 1e-05

BF = jnp.bfloat16
F32 = jnp.float32
NT = (((1,), (1,)), ((), ()))
TN = (((0,), (0,)), ((), ()))
VMEM = pl.BlockSpec(memory_space=pltpu.VMEM)
HBM = pl.BlockSpec(memory_space=pltpu.HBM)
SMEM = pl.BlockSpec(memory_space=pltpu.SMEM)
ANY = pl.BlockSpec(memory_space=pl.ANY)
ROOM = pltpu.CompilerParams(vmem_limit_bytes=48 << 20)
FULL = pltpu.CompilerParams(vmem_limit_bytes=60 << 20)


def iota(shape, dim):
    return lax.broadcasted_iota(jnp.int32, shape, dim)


def mm(a, b, dims=(((1,), (0,)), ((), ()))):
    return lax.dot_general(a, b, dims, preferred_element_type=F32)


def cost(flops, bytes_accessed, transcendentals=0):
    return pl.CostEstimate(
        flops=int(flops), bytes_accessed=int(bytes_accessed), transcendentals=int(transcendentals)
    )


def order_kernel(counts_ref, order_ref, dest_ref, slot_ref, info_ref, span_ref):
    parents = counts_ref.shape[1]
    blocks = dest_ref.shape[1]
    counts = jnp.broadcast_to(counts_ref[...], (8, parents)).astype(F32)
    upper = jnp.where(iota((parents, parents), 0) <= iota((parents, parents), 1), 1.0, 0.0)
    starts = mm(counts.astype(BF), upper.astype(BF)) - counts
    coarse = jnp.floor(starts * (1.0 / 64.0))
    which = iota((8, parents), 0)
    fields = jnp.where(which == 0, coarse, jnp.where(which == 1, starts - 64.0 * coarse, counts))
    pick = jnp.where(iota((parents, parents), 0) == order_ref[...], 1.0, 0.0).astype(BF)
    ordered = mm(fields.astype(BF), pick).astype(jnp.int32)
    first = 64 * ordered[0:1] + ordered[1:2]
    length = ordered[2:3]
    span_ref[...] = jnp.where(which == 0, first, jnp.where(which == 1, first + length, length))
    both = 16 * first + length
    both = both[:, : parents // 2] | (both[:, parents // 2 :] << 16)
    lines = parents // 256
    info_ref[0, lines:, :] = jnp.zeros((INFO - lines, 128), jnp.int32)
    info_ref[0, lines : lines + 1, :blocks] = dest_ref[...] * blocks + slot_ref[...]
    for i in range(lines):
        info_ref[0, i : i + 1, :] = both[:, i * 128 : (i + 1) * 128]
    tile = info_ref[0]
    for d in range(1, info_ref.shape[0]):
        info_ref[d] = tile


def order_tables(child_counts, parent_order, hil_dest, hil_slot, devices):
    parents = child_counts.shape[1]
    return pl.pallas_call(
        order_kernel,
        out_shape=(
            jax.ShapeDtypeStruct((devices, INFO, 128), jnp.int32),
            jax.ShapeDtypeStruct((8, parents), jnp.int32),
        ),
        in_specs=[VMEM] * 4,
        out_specs=(VMEM, VMEM),
        compiler_params=FULL,
        cost_estimate=cost(32 * parents * parents, 8 * parents),
    )(child_counts, parent_order, hil_dest[None], hil_slot[None])


def pack_kernel(capacity, dest_ref, points_ref, payload_ref, used, sem):
    blocks = dest_ref.shape[0]

    def clear(d, _):
        used[d] = 0
        return 0

    lax.fori_loop(0, used.shape[0], clear, 0)

    def send(b, _):
        d = dest_ref[b]
        place = d * capacity + used[d]
        used[d] = used[d] + 1
        pltpu.make_async_copy(
            points_ref.at[pl.ds(pl.multiple_of(b * ROWS, ROWS), ROWS)],
            payload_ref.at[pl.ds(pl.multiple_of(place * ROWS, ROWS), ROWS)],
            sem,
        ).start()
        return 0

    lax.fori_loop(0, blocks, send, 0)
    whole = pl.ds(0, blocks * ROWS)
    pltpu.make_async_copy(points_ref.at[whole], payload_ref.at[whole], sem).wait()


def pack_blocks(hil_dest, points, devices, capacity):
    return pl.pallas_call(
        functools.partial(pack_kernel, capacity),
        out_shape=jax.ShapeDtypeStruct((devices * capacity * ROWS, points.shape[1]), BF),
        in_specs=[SMEM, HBM],
        out_specs=VMEM,
        scratch_shapes=[pltpu.SMEM((devices,), jnp.int32), pltpu.SemaphoreType.DMA],
        compiler_params=FULL,
        cost_estimate=cost(0, 4 * points.size),
    )(hil_dest, points)


def key_windows(ids_ref, low_ref, count_ref, turn_ref, turned_ref):
    tiles, span = ids_ref.shape
    lane = iota((1, span), 1)
    for t in range(tiles):
        ids = ids_ref[t : t + 1, :]
        sizes = [
            jnp.sum(jnp.where(ids == c, 1.0, 0.0)).astype(jnp.int32) for c in range(PATCHES)
        ]
        starts = [jnp.int32(0)]
        for c in range(1, PATCHES):
            starts.append(starts[-1] + sizes[c - 1])
        most, turn = sizes[0], starts[0]
        for c in range(1, PATCHES):
            turn = jnp.where(sizes[c] > most, starts[c], turn)
            most = jnp.maximum(most, sizes[c])
        firsts = [lax.rem(start - turn + span, span) for start in starts]
        ends = [first + size for first, size in zip(firsts, sizes)]
        turned = jnp.zeros((1, span), jnp.int32)
        for c in range(1, PATCHES):
            turned = jnp.where((lane >= firsts[c]) & (lane < ends[c]), c, turned)
        turned_ref[t : t + 1, :] = turned
        turn_ref[t] = turn
        for b in range(span // ROWS):
            top, bottom = b * ROWS, (b + 1) * ROWS - 1
            low, high = jnp.int32(0), jnp.int32(span)
            for c in range(PATCHES):
                low = jnp.where((firsts[c] <= top) & (top < ends[c]), firsts[c], low)
                high = jnp.where((firsts[c] <= bottom) & (bottom < ends[c]), ends[c], high)
            low = low // ROWS * ROWS
            count = (high - low + WINDOW - 1) // WINDOW
            low_ref[t * (span // ROWS) + b] = jnp.minimum(low, span - count * WINDOW)
            count_ref[t * (span // ROWS) + b] = count


def seat_kernel(
    per_owner,
    source_ref,
    block_ref,
    info_ref,
    ids_ref,
    table_ref,
    local_ref,
    base_ref,
    low_ref,
    count_ref,
    turn_ref,
    turned_ref,
    owner,
    place,
    seats,
):
    blocks = owner.shape[0]
    parents = 128 * 8
    devices = info_ref.shape[0] // 8
    which = iota((16, parents), 0)
    rank = iota((16, parents), 1)
    fields = jnp.where(which == 0, rank // per_owner, jnp.where(which == 1, rank % per_owner, 0))
    fields = fields.astype(F32).astype(BF)

    def one(v, _):
        source = source_ref[v]
        packed = info_ref[pl.ds(pl.multiple_of(source * 8, 8), 8), :]
        line = jnp.concatenate([packed[i : i + 1] for i in range(8)], axis=1)
        first = line // 16
        row = block_ref[v] * ROWS + iota((ROWS, parents), 0)
        inside = (row >= first) & (row < first + line % 16)
        found = mm(fields, jnp.where(inside, 1.0, 0.0).astype(BF), NT)
        owner[pl.ds(v, 1), :] = found[0:1]
        place[pl.ds(v, 1), :] = found[1:2]
        return 0

    lax.fori_loop(0, blocks, one, 0)
    own = owner[...]
    run = own * per_owner + place[...]
    opens = (iota((blocks, ROWS), 1) == 0) | (run != pltpu.roll(run, 1, 1))
    opened = jnp.where(opens, 1.0, 0.0)
    upper = jnp.where(iota((ROWS, ROWS), 0) <= iota((ROWS, ROWS), 1), 1.0, 0.0).astype(BF)
    every = jnp.ones((ROWS, ROWS), BF)
    before = jnp.where(iota((blocks, blocks), 1) < iota((blocks, blocks), 0), 1.0, 0.0).astype(BF)
    local_ref[...] = (mm(opened.astype(BF), upper) - 1.0).astype(jnp.int32)

    def count(e, seat):
        here = own == e.astype(F32)
        marks = jnp.where(here, opened, 0.0).astype(BF)
        total = mm(marks, upper) + mm(before, mm(marks, every).astype(BF))
        return jnp.where(here, total - 1.0, seat)

    seats[...] = lax.fori_loop(0, devices, count, jnp.zeros((blocks, ROWS), F32))
    table_ref[...] = jnp.zeros_like(table_ref)
    field = iota((ROWS, ROWS), 0)

    def lay(v, base):
        base = pl.multiple_of(base, ALIGN)
        base_ref[v] = base
        at = pl.ds(v, 1)
        local = local_ref[at, :]
        seat = seats[at, :]
        coarse = jnp.floor(seat * (1.0 / 64.0))
        lines = (owner[at, :], coarse, seat - 64.0 * coarse)
        values = jnp.ones((ROWS, ROWS), F32)
        for i, line in enumerate(lines):
            values = jnp.where(field == i, line, values)
        previous = jnp.where(iota((1, ROWS), 1) == 0, -1, pltpu.roll(local, 1, 1))
        begins = (field == local) & (local != previous)
        found = mm(jnp.where(begins, 1.0, 0.0).astype(BF), values.astype(BF), NT)
        table_ref[pl.ds(base, ROWS), :] = found.astype(BF)
        return base + (jnp.max(local) + ALIGN) // ALIGN * ALIGN

    base_ref[blocks] = lax.fori_loop(0, blocks, lay, 0)
    key_windows(ids_ref, low_ref, count_ref, turn_ref, turned_ref)


def seat_rows(source, block, info, ids, per_owner):
    blocks = source.shape[0]
    rows = blocks * ROWS
    return pl.pallas_call(
        functools.partial(seat_kernel, per_owner),
        out_shape=(
            jax.ShapeDtypeStruct((rows + CHUNK, 128), BF),
            jax.ShapeDtypeStruct((blocks, ROWS), jnp.int32),
            jax.ShapeDtypeStruct((blocks + 1,), jnp.int32),
            jax.ShapeDtypeStruct((blocks,), jnp.int32),
            jax.ShapeDtypeStruct((blocks,), jnp.int32),
            jax.ShapeDtypeStruct((ids.shape[0],), jnp.int32),
            jax.ShapeDtypeStruct(ids.shape, jnp.int32),
        ),
        in_specs=[SMEM, SMEM, VMEM, VMEM],
        out_specs=(VMEM, VMEM, SMEM, SMEM, SMEM, SMEM, VMEM),
        scratch_shapes=[pltpu.VMEM((blocks, ROWS), F32)] * 3,
        compiler_params=ROOM,
        cost_estimate=cost(40 * rows * 1024, 8 * rows),
    )(source, block, info, ids)


def plan_kernel(round_ref, base_ref, table_ref, code_ref):
    first = (SEAT * round_ref[0]).astype(F32)
    chunks = (base_ref[base_ref.shape[0] - 1] + CHUNK - 1) // CHUNK
    pick = jnp.where(iota((16, 128), 0) == iota((16, 128), 1), 1.0, 0.0).astype(BF)

    def step(c, _):
        at = pl.ds(pl.multiple_of(c * CHUNK, CHUNK), CHUNK)
        lines = mm(pick, table_ref[at, :], NT)
        seat = 64.0 * lines[1:2] + lines[2:3] - first
        seated = (lines[3:4] > 0.5) & (seat >= 0.0) & (seat < float(SEAT))
        code = jnp.where(seated, lines[0:1] * float(SEAT) + seat, -1.0).astype(jnp.int32)
        code_ref[:, at] = jnp.broadcast_to(code, (8, CHUNK))
        return 0

    lax.fori_loop(0, chunks, step, 0)


def plan_seats(step, base, table):
    return pl.pallas_call(
        plan_kernel,
        out_shape=jax.ShapeDtypeStruct((8, table.shape[0]), jnp.int32),
        in_specs=[SMEM, SMEM, VMEM],
        out_specs=VMEM,
        compiler_params=ROOM,
        cost_estimate=cost(64 * table.size, 4 * table.size),
    )(step, base, table)


def rotate_rows(doubled, turn, span):
    coarse = pl.multiple_of(turn // 8 * 8, 8)
    fine = turn % 8
    width = doubled.shape[1]
    rows = doubled[pl.ds(coarse, span + 8), :].reshape(span // 8 + 1, 8, width)
    rolled = pltpu.roll(rows, (8 - fine) % 8, 1)
    kept = iota((span // 8, 8, width), 1) < 8 - fine
    return jnp.where(kept, rolled[:-1], rolled[1:]).reshape(span, width)


def attend_kernel(
    index_ref,
    low_ref,
    count_ref,
    base_ref,
    turn_ref,
    local_ref,
    ids_ref,
    w_ref,
    wo_ref,
    rows_ref,
    out_ref,
    x,
    qx,
    kx,
    vx,
    att,
    doubled,
    wrapped,
    code,
    sems,
):
    tiles, span = ids_ref.shape
    width = w_ref.shape[0]
    cols = HEAD_GROUP * HDIM
    groups = width // cols
    heads = width // HDIM
    per_tile = span // ROWS

    def fetch(t):
        for s in range(t * per_tile, (t + 1) * per_tile):
            pltpu.make_async_copy(
                rows_ref.at[pl.ds(pl.multiple_of(index_ref[s] * ROWS, ROWS), ROWS)],
                x.at[pl.ds(s * ROWS, ROWS)],
                sems.at[t],
            ).start()

    fetch(0)
    out_ref[...] = jnp.zeros_like(out_ref)
    lane = iota((ROWS, 2 * cols), 1)
    of_head = [(lane // HDIM == h) | (lane >= cols) for h in range(HEAD_GROUP)]
    lane_out = lane % cols // HDIM
    for g in range(groups):
        vx[g, :, cols:] = jnp.ones((tiles * span, cols), BF)
    r_i = iota((cols, cols), 0)
    c_i = iota((cols, cols), 1)
    far = jnp.where((r_i != c_i) & (c_i < PATCHES), -FAR, 0.0).astype(BF)
    bounds = []

    for t in range(tiles):
        at = slice(t * span, (t + 1) * span)
        if t + 1 < tiles:
            fetch(t + 1)
        pltpu.make_async_copy(
            rows_ref.at[pl.ds(0, span)], x.at[pl.ds(t * span, span)], sems.at[t]
        ).wait()
        whole = x[at, :].astype(F32)
        doubled[:span, :] = whole
        doubled[span:, :] = whole
        tile_rows = rotate_rows(doubled, turn_ref[t], span).astype(BF)
        x[at, :] = tile_rows
        same = ids_ref[t : t + 1, :] == iota((cols, span), 0)
        patch_hot = jnp.where(same, 1.0, 0.0).astype(BF)
        query = mm(tile_rows, w_ref[:, :width])
        keys = mm(w_ref[:, width : 2 * width], tile_rows, (((0,), (1,)), ((), ())))
        value = mm(tile_rows, w_ref[:, 2 * width :]).astype(BF)
        patch_far = mm(patch_hot, far, TN).astype(BF)
        for g in range(groups):
            some = slice(g * cols, (g + 1) * cols)
            qx[g, at, :cols] = query[:, some].astype(BF)
            qx[g, at, cols:] = patch_far
            kx[g, :cols, at] = keys[some].astype(BF)
            kx[g, cols:, at] = patch_hot
            vx[g, at, :cols] = value[:, some]
        query_most = jnp.max(jnp.abs(query), axis=0, keepdims=True)
        key_most = jnp.max(jnp.abs(keys), axis=1, keepdims=True)
        by_head = jnp.where(
            iota((heads, width), 1) // HDIM == iota((heads, width), 0), query_most, 0.0
        )
        bounds.append(mm(by_head.astype(BF), jnp.broadcast_to(key_most, (width, 128)).astype(BF)))
    bound = bounds[0]
    for other in bounds[1:]:
        bound = jnp.maximum(bound, other)
    safe = jnp.max(bound) * SCORE_SCALE < SCORE_SAFE

    def block(s, _):
        start = pl.multiple_of(s // per_tile * span, span)
        steps = count_ref[s]
        here = pl.ds(pl.multiple_of(s * ROWS, ROWS), ROWS)

        def run(first, length, exact):
            at = pl.ds(pl.multiple_of(start + first, ROWS), length)
            scores = []
            for g in range(groups):
                q = qx[g, here, :]
                stacked = jnp.concatenate(
                    [jnp.where(of_head[h], q, jnp.zeros_like(q)) for h in range(HEAD_GROUP)],
                    axis=0,
                )
                scores.append(mm(stacked, kx[g, :, at]))
            for g in range(groups):
                level = scores[g] * SCORE_SCALE
                if exact:
                    level = level - jnp.max(level, axis=1, keepdims=True)
                weights = jnp.exp2(level).astype(BF)
                mixed = mm(weights, vx[g, at, :])
                mixed = mixed.reshape(HEAD_GROUP, ROWS, 2 * cols)
                own = mixed[0]
                for h in range(1, HEAD_GROUP):
                    own = jnp.where(lane_out == h, mixed[h], own)
                att[here, g * cols : (g + 1) * cols] = (own[:, :cols] / own[:, cols:]).astype(BF)

        for i in range(span // WINDOW):
            pl.when(safe & (steps == i + 1))(
                functools.partial(run, low_ref[s], (i + 1) * WINDOW, False)
            )
        pl.when(jnp.logical_not(safe))(functools.partial(run, 0, span, True))
        return 0

    lax.fori_loop(0, tiles * per_tile, block, 0)

    for t in range(tiles):
        at = slice(t * span, (t + 1) * span)
        turn = turn_ref[t]
        mixed = (x[at, :].astype(F32) + mm(att[at, :], wo_ref[...])).astype(BF)
        wrapped[t, :span, :] = mixed
        wrapped[t, span:, :] = mixed[:ROWS]
        runs = local_ref[t : t + 1, :] + iota((1, span), 1) // ROWS * ROWS
        runs = pltpu.roll(jnp.broadcast_to(runs, (8, span)), lax.rem(span - turn, span), 1)
        code[t, :, :span] = runs
        code[t, :, span:] = runs[:, :ROWS]
        for b in range(per_tile):
            first = lax.rem(b * ROWS + span - turn, span) // ROWS * ROWS
            window = pl.ds(pl.multiple_of(first, ROWS), 2 * ROWS)
            run = iota((ROWS, 2 * ROWS), 0) + b * ROWS == code[t, 0:1, window]
            sums = mm(jnp.where(run, 1.0, 0.0).astype(BF), wrapped[t, window, :])
            put = pl.multiple_of(base_ref[t * per_tile + b], ALIGN)
            out_ref[pl.ds(put, ROWS), :] = sums.astype(BF)


def attend(index, low, count, base, turn, local, ids, w_qkv, w_out, rows):
    tiles, span = ids.shape
    width = rows.shape[1]
    cols = HEAD_GROUP * HDIM
    groups = width // cols
    pairs = tiles * span * span * HEAD_GROUP
    return pl.pallas_call(
        attend_kernel,
        out_shape=jax.ShapeDtypeStruct((tiles * span + CHUNK, width), BF),
        in_specs=[SMEM, SMEM, SMEM, SMEM, SMEM, VMEM, VMEM, VMEM, VMEM, HBM],
        out_specs=VMEM,
        scratch_shapes=[
            pltpu.VMEM((tiles * span, width), BF),
            pltpu.VMEM((groups, tiles * span, 2 * cols), BF),
            pltpu.VMEM((groups, 2 * cols, tiles * span), BF),
            pltpu.VMEM((groups, tiles * span, 2 * cols), BF),
            pltpu.VMEM((tiles * span, width), BF),
            pltpu.VMEM((2 * span, width), F32),
            pltpu.VMEM((tiles, span + ROWS, width), BF),
            pltpu.VMEM((tiles, 8, span + ROWS), jnp.int32),
            pltpu.SemaphoreType.DMA((tiles,)),
        ],
        compiler_params=ROOM,
        cost_estimate=cost(pairs * 1024, 4 * rows.size, pairs),
    )(index, low, count, base, turn, local, ids, w_qkv, w_out, rows)


def route_kernel(base_ref, code_ref, sums_ref, out_ref, acc):
    total = out_ref.shape[0]
    chunks = (base_ref[base_ref.shape[0] - 1] + CHUNK - 1) // CHUNK
    seat = iota((total, 1), 0) + pl.program_id(0) * total
    acc[...] = jnp.zeros_like(acc)

    def step(c, _):
        at = pl.ds(pl.multiple_of(c * CHUNK, CHUNK), CHUNK)
        member = jnp.where(seat == code_ref[0:1, at], 1.0, 0.0).astype(BF)
        acc[...] += mm(member, sums_ref[at, :])
        return 0

    lax.fori_loop(0, chunks, step, 0)
    out_ref[...] = acc[...].astype(BF)


def route_sums(base, code, sums, devices):
    count, width = sums.shape
    total = devices * SEAT
    part = min(TURN, total)
    return pl.pallas_call(
        route_kernel,
        grid=(total // part,),
        out_shape=jax.ShapeDtypeStruct((total, width), BF),
        in_specs=[SMEM, VMEM, VMEM],
        out_specs=pl.BlockSpec((part, width), lambda i: (i, 0)),
        scratch_shapes=[pltpu.VMEM((part, width), F32)],
        compiler_params=ROOM,
        cost_estimate=cost(total * count * width, 4 * count * width),
    )(base, code, sums)


def fold_rows(step, pieces_ref, about):
    total = 0.0
    part = min(TURN, pieces_ref.shape[0])
    first = step * SEAT
    seats = []
    for i in (1, 3):
        seat = about[:, i + 1 : i + 2].astype(jnp.int32) - first
        seated = (seat >= 0) & (seat < SEAT)
        seats.append(jnp.where(seated, about[:, i : i + 1].astype(jnp.int32) * SEAT + seat, -1))
    for low in range(0, pieces_ref.shape[0], part):
        column = iota((1, part), 1) + low
        member = (column == seats[0]) | (column == seats[1])
        member = jnp.where(member, 1.0, 0.0).astype(BF)
        total = total + mm(member, pieces_ref[low : low + part, :])
    return total


def fold_kernel(step_ref, pieces_ref, about_ref, before_ref, out_ref):
    out_ref[...] = before_ref[...] + fold_rows(step_ref[0], pieces_ref, about_ref[...])


def fold_pieces(step, pieces, about, before):
    parents, width = before.shape
    chunk = 256
    along = lambda i: (i, 0)
    return pl.pallas_call(
        fold_kernel,
        grid=(parents // chunk,),
        out_shape=jax.ShapeDtypeStruct((parents, width), F32),
        in_specs=[
            SMEM,
            pl.BlockSpec(pieces.shape, lambda i: (0, 0)),
            pl.BlockSpec((chunk, 128), along),
            pl.BlockSpec((chunk, width), along),
        ],
        out_specs=pl.BlockSpec((chunk, width), along),
        compiler_params=ROOM,
        cost_estimate=cost(2 * parents * pieces.size, 4 * pieces.size),
    )(step, pieces, about, before)


def whole_tiles(rows):
    return (rows + 15) // 16 * 16


def pad_rows(value):
    spare = whole_tiles(value.shape[0]) - value.shape[0]
    if spare == 0:
        return value
    return jnp.concatenate([value, jnp.zeros((spare, value.shape[1]), value.dtype)], axis=0)


def pool_kernel(
    per_owner,
    pieces_ref,
    more_ref,
    about_ref,
    w_ref,
    gain_ref,
    shift_ref,
    cot_ref,
    pooled_ref,
    sent_ref,
    acc,
    sums,
):
    step = pl.program_id(0)

    @pl.when(step == 0)
    def _():
        acc[...] = jnp.zeros_like(acc)
        sums[...] = jnp.zeros_like(sums)

    chunk, width = more_ref.shape
    about = about_ref[...]
    total = more_ref[...] + fold_rows(0, pieces_ref, about)
    lengths = about[:, 0:1]
    parent_in = (total / lengths).astype(BF)
    w_pool = w_ref[...]
    gain = gain_ref[...]
    projected = mm(parent_in, w_pool)
    centred = projected - jnp.mean(projected, axis=-1, keepdims=True)
    variance = jnp.mean(centred * centred, axis=-1, keepdims=True)
    inv_std = lax.rsqrt(variance + norm_eps)
    normed = centred * inv_std
    shifted = normed * gain + shift_ref[...]
    normal_cdf = 0.5 * (1.0 + lax.erf(shifted * inv_sqrt_two))
    pooled_ref[...] = (shifted * normal_cdf).astype(BF)
    grad_act = cot_ref[...].astype(F32) * (
        normal_cdf + shifted * jnp.exp(-0.5 * shifted * shifted) * inv_sqrt_tau
    )
    sums[0:1, :] += jnp.sum(grad_act * normed, axis=0, keepdims=True)
    sums[1:2, :] += jnp.sum(grad_act, axis=0, keepdims=True)
    scaled = grad_act * gain
    grad_proj = (
        (
            scaled
            - jnp.mean(scaled, axis=-1, keepdims=True)
            - normed * jnp.mean(scaled * normed, axis=-1, keepdims=True)
        )
        * inv_std
    ).astype(BF)
    acc[...] += mm(parent_in, grad_proj, TN)
    back = mm(grad_proj, w_pool, NT)
    devices, _, width = sent_ref.shape
    fits = chunk // per_owner
    for d in range(fits):
        part = back[d * per_owner : (d + 1) * per_owner]
        sent_ref[step * fits + d, : whole_tiles(per_owner), :] = pad_rows(part).astype(BF)

    @pl.when(step == pl.num_programs(0) - 1)
    def _():
        each = acc.shape[0] // devices
        tall = whole_tiles(each)
        exact = sums[0:2, :]
        high = exact.astype(BF).astype(F32)
        parts = []
        for value in (high, exact - high):
            for row in range(2):
                for low in range(0, acc.shape[1], width):
                    parts.append(value[row : row + 1, low : low + width])
        norm = pad_rows(jnp.concatenate(parts, axis=0)).astype(BF)
        for d in range(devices):
            low = whole_tiles(per_owner)
            for side in range(0, acc.shape[1], width):
                part = acc[d * each : (d + 1) * each, side : side + width]
                sent_ref[d, low : low + tall, :] = pad_rows(part).astype(BF)
                low += tall
            sent_ref[d, low:, :] = norm


def pool(pieces, more, about, w_pool, gain, shift, cotangent):
    parents, width = more.shape
    wide = w_pool.shape[1]
    chunk = 512
    devices = pieces.shape[0] // SEAT
    tall = whole_tiles(parents // devices) + wide // width * whole_tiles(width // devices)
    tall += whole_tiles(4 * wide // width)
    fixed = lambda i: (0, 0)
    along = lambda i: (i, 0)
    return pl.pallas_call(
        functools.partial(pool_kernel, parents * SEAT // pieces.shape[0]),
        grid=(parents // chunk,),
        out_shape=(
            jax.ShapeDtypeStruct((parents, wide), BF),
            jax.ShapeDtypeStruct((devices, tall, width), BF),
        ),
        in_specs=[
            pl.BlockSpec(pieces.shape, fixed),
            pl.BlockSpec((chunk, width), along),
            pl.BlockSpec((chunk, 128), along),
            pl.BlockSpec((width, wide), fixed),
            pl.BlockSpec((1, wide), fixed),
            pl.BlockSpec((1, wide), fixed),
            pl.BlockSpec((chunk, wide), along),
        ],
        out_specs=(
            pl.BlockSpec((chunk, wide), along),
            pl.BlockSpec((devices, tall, width), lambda i: (0, 0, 0)),
        ),
        scratch_shapes=[
            pltpu.VMEM((width, wide), F32),
            pltpu.VMEM((8, wide), F32),
        ],
        compiler_params=FULL,
        cost_estimate=cost(6 * parents * width * wide, 8 * parents * wide, 2 * parents * wide),
    )(pieces, more, about, w_pool, gain, shift, cotangent)


def spread_kernel(span_ref, grad_ref, out_ref, share):
    step = pl.program_id(0)
    chunk = out_ref.shape[0]
    parents, width = share.shape

    @pl.when(step == 0)
    def _():
        pick = jnp.where(iota((8, width), 0) == 2, 1.0, 0.0).astype(BF)
        lengths = mm(jnp.minimum(span_ref[...], 64).astype(F32).astype(BF), pick, TN)
        per_owner = parents // grad_ref.shape[0]
        grads = [grad_ref[d, :per_owner, :].astype(F32) for d in range(grad_ref.shape[0])]
        share[...] = (jnp.concatenate(grads, axis=0) / lengths).astype(BF)

    row = iota((chunk, parents), 0) + step * chunk
    inside = (row >= span_ref[0:1, :]) & (row < span_ref[1:2, :])
    out_ref[...] = mm(jnp.where(inside, 1.0, 0.0).astype(BF), share[...]).astype(BF)


def spread_grads(span, arrived, rows):
    parents = span.shape[1]
    width = arrived.shape[2]
    chunk = 512
    fixed = lambda i: (0, 0)
    return pl.pallas_call(
        spread_kernel,
        grid=(rows // chunk,),
        out_shape=jax.ShapeDtypeStruct((rows, width), BF),
        in_specs=[
            pl.BlockSpec((8, parents), fixed),
            pl.BlockSpec(arrived.shape, lambda i: (0, 0, 0)),
        ],
        out_specs=pl.BlockSpec((chunk, width), lambda i: (i, 0)),
        scratch_shapes=[pltpu.VMEM((parents, width), BF)],
        compiler_params=ROOM,
        cost_estimate=cost(2 * rows * parents * width, 4 * rows * width),
    )(span, arrived)


def settle_kernel(per_owner, arrived_ref, shared_ref, norm_ref):
    devices, tall, width = arrived_ref.shape
    low = whole_tiles(per_owner)
    total = arrived_ref[0, low:, :].astype(F32)
    for d in range(1, devices):
        total = total + arrived_ref[d, low:, :].astype(F32)
    weight_rows = shared_ref.shape[1]
    weight = total[:weight_rows].astype(BF)
    for d in range(devices):
        shared_ref[d] = weight
    norm = total[weight_rows : weight_rows + 8]
    sides = norm_ref.shape[1] // width
    for row in range(2):
        for side in range(sides):
            i = row * sides + side
            value = norm[i : i + 1] + norm[2 * sides + i : 2 * sides + i + 1]
            norm_ref[row : row + 1, side * width : (side + 1) * width] = value


def settle(arrived, per_owner, weight_rows, wide):
    devices, tall, width = arrived.shape
    return pl.pallas_call(
        functools.partial(settle_kernel, per_owner),
        out_shape=(
            jax.ShapeDtypeStruct((devices, weight_rows, width), BF),
            jax.ShapeDtypeStruct((2, wide), F32),
        ),
        in_specs=[VMEM],
        out_specs=(VMEM, VMEM),
        compiler_params=ROOM,
        cost_estimate=cost(arrived.size, 2 * arrived.size),
    )(arrived)


def piece_seats(info, codes, blocks, per_owner):
    devices = codes.shape[0]
    parents = devices * per_owner
    me = lax.axis_index("pts")
    packed = info.reshape(devices, parents)
    span = blocks * ROWS
    lane = jnp.arange(blocks)

    def at_block(block):
        found = jnp.where(block[:, :, None] == lane, codes[:, None, :], 0)
        return jnp.sum(found, axis=2)

    first = packed // 16
    end = first + packed % 16 - 1
    near = at_block(first // ROWS)
    far = at_block(end // ROWS)
    split = first // ROWS != end // ROWS
    holders = jnp.arange(devices)
    by_owner = lambda value: value.reshape(devices, devices, per_owner, 1)
    filled = (by_owner(near // blocks) == holders).astype(jnp.int32)
    filled += (by_owner(jnp.where(split, far // blocks, -1)) == holders).astype(jnp.int32)
    rounds = (jnp.max(jnp.sum(filled, axis=(0, 2))) + SEAT - 1) // SEAT

    mine = lambda value: lax.dynamic_slice_in_dim(value, me * per_owner, per_owner, axis=1)
    near, far, split, first, packed = map(mine, (near, far, split, first, packed))
    near_key = near * ROWS + first % ROWS
    far_key = jnp.where(split, far * ROWS, devices * span)
    near_key, far_key = near_key.reshape(parents, 1), far_key.reshape(parents, 1)
    every = jnp.concatenate([near_key, far_key], axis=0).reshape(1, 2 * parents)

    def place(key):
        holder = key // span
        rank = jnp.sum((every < key) & (every >= holder * span), axis=1, keepdims=True)
        return holder, jnp.where(holder < devices, rank, -1)

    length = (packed % 16).reshape(parents, 1)
    columns = (length,) + place(near_key) + place(far_key)
    wide = iota((parents, 128), 1)
    about = jnp.zeros((parents, 128), jnp.int32)
    for i, column in enumerate(columns):
        about = jnp.where(wide == i, column, about)
    return about.astype(F32), rounds.astype(jnp.int32)


def swap(parts):
    return lax.all_to_all(parts, "pts", split_axis=0, concat_axis=0, tiled=True)


def exchange(rows, devices):
    return swap(rows.reshape(devices, rows.shape[0] // devices, rows.shape[1])).reshape(rows.shape)


def received_index(codes, blocks, capacity):
    devices = codes.shape[0]
    me = lax.axis_index("pts")
    mine = codes // blocks == me
    slots = codes % blocks
    lane = jnp.arange(blocks)
    rank = jnp.sum(mine[:, None, :] & (lane[None, :] < lane[:, None])[None], axis=2)
    index = jnp.arange(devices)[:, None] * capacity + rank
    both = index * blocks + lane[None, :]
    hit = mine[:, :, None] & (slots[:, :, None] == lane[None, None, :])
    both = jnp.sum(jnp.where(hit, both[:, :, None], 0), axis=(0, 1)).astype(jnp.int32)
    return both // blocks, both % blocks


def local(
    points,
    hil_dest,
    hil_slot,
    patch_ids,
    child_counts,
    parent_order,
    w_qkv,
    w_out,
    w_pool,
    norm_gain,
    norm_shift,
    cotangent,
):
    devices = lax.axis_size("pts")
    blocks = hil_dest.shape[0]
    rows, width = points.shape
    wide = w_pool.shape[1]
    parents = child_counts.shape[1]
    per_owner = parents // devices
    capacity = (blocks + devices - 1) // devices

    me = lax.axis_index("pts")
    info, span = order_tables(child_counts, parent_order, hil_dest, hil_slot, devices)
    info = swap(info)
    payload = pack_blocks(hil_dest, points, devices, capacity)
    received = exchange(payload, devices)
    lines = parents // 256
    codes = info[:, lines, :blocks]
    packed = info[:, :lines]
    info = jnp.concatenate(
        [packed & 65535, lax.shift_right_logical(packed, jnp.int32(16))], axis=1
    )
    index, block = received_index(codes, blocks, capacity)
    source = index // capacity
    table, local_run, base, low, count, turn, turned = seat_rows(
        source, block, info.reshape(-1, 128), patch_ids, per_owner
    )
    code = plan_seats(jnp.zeros((1,), jnp.int32), base, table)
    about, rounds = piece_seats(info, codes, blocks, per_owner)
    more = jnp.broadcast_to(about[:, 127:], (parents, width))
    index, low, count, turn, turned, base, local_run, code, about, rounds, more = (
        lax.optimization_barrier(
            (index, low, count, turn, turned, base, local_run, code, about, rounds, more)
        )
    )
    local_run = local_run.reshape(patch_ids.shape)
    sums = attend(index, low, count, base, turn, local_run, turned, w_qkv, w_out, received)
    pieces = exchange(route_sums(base, code, sums, devices), devices)

    def turn_again(carry):
        step, before = carry
        step = step.reshape(1)
        late = exchange(route_sums(base, plan_seats(step, base, table), sums, devices), devices)
        return step[0] + 1, fold_pieces(step, late, about, before)

    _, more = lax.while_loop(
        lambda carry: carry[0] < rounds, turn_again, (jnp.int32(1), more)
    )
    pooled, outgoing = pool(
        pieces, more, about, w_pool, norm_gain[None], norm_shift[None], cotangent
    )
    arrived = swap(outgoing)
    each = width // devices
    tall = whole_tiles(each)
    sides = wide // width
    shared, grad_norm = settle(arrived, per_owner, sides * tall, wide)
    shared = swap(shared)
    grad_weight = jnp.concatenate(
        [shared[:, side * tall : side * tall + each] for side in range(sides)], axis=2
    )
    grad_weight = grad_weight.reshape(width, wide).astype(F32)
    grad_points = spread_grads(span, arrived, rows)
    return (pooled, grad_points, grad_weight, grad_norm)


def solution(mesh):
    in_specs = (
        P(("grp", "pts"), None),
        P(("grp", "pts")),
        P(("grp", "pts")),
        P(("grp", "pts"), None),
        P(("grp", "pts"), None),
        P(("grp", "pts"), None),
        P(),
        P(),
        P(),
        P(),
        P(),
        P(("grp", "pts"), None),
    )
    out_specs = (P(("grp", "pts"), None), P(("grp", "pts"), None), P("grp", None), P("grp", None))
    return jax.shard_map(local, mesh=mesh, in_specs=in_specs, out_specs=out_specs, check_vma=False)
```

```python
import functools
import math

import jax
import jax.numpy as jnp
from jax import lax
from jax.experimental import pallas as pl
from jax.experimental.pallas import tpu as pltpu
from jax.sharding import PartitionSpec as P

HDIM = 16
HEAD_GROUP = 8
ROWS = 128
SEAT = 104
TURN = 16 * SEAT
INFO = 8
ALIGN = 16
CHUNK = 512
WINDOW = 256
PATCHES = 4
FAR = 2.0**100
SCORE_SCALE = HDIM**-0.5 * math.log2(math.e)
SCORE_SAFE = 98.0

inv_sqrt_two = 0.7071067811865476
inv_sqrt_tau = 0.3989422804014327
norm_eps = 1e-05

BF = jnp.bfloat16
F32 = jnp.float32
NT = (((1,), (1,)), ((), ()))
TN = (((0,), (0,)), ((), ()))
VMEM = pl.BlockSpec(memory_space=pltpu.VMEM)
HBM = pl.BlockSpec(memory_space=pltpu.HBM)
SMEM = pl.BlockSpec(memory_space=pltpu.SMEM)
ANY = pl.BlockSpec(memory_space=pl.ANY)
ROOM = pltpu.CompilerParams(vmem_limit_bytes=48 << 20)
FULL = pltpu.CompilerParams(vmem_limit_bytes=60 << 20)


def iota(shape, dim):
    return lax.broadcasted_iota(jnp.int32, shape, dim)


def mm(a, b, dims=(((1,), (0,)), ((), ()))):
    return lax.dot_general(a, b, dims, preferred_element_type=F32)


def cost(flops, bytes_accessed, transcendentals=0):
    return pl.CostEstimate(
        flops=int(flops), bytes_accessed=int(bytes_accessed), transcendentals=int(transcendentals)
    )


def order_kernel(counts_ref, order_ref, dest_ref, slot_ref, info_ref, span_ref):
    parents = counts_ref.shape[1]
    blocks = dest_ref.shape[1]
    counts = jnp.broadcast_to(counts_ref[...], (8, parents)).astype(F32)
    upper = jnp.where(iota((parents, parents), 0) <= iota((parents, parents), 1), 1.0, 0.0)
    starts = mm(counts.astype(BF), upper.astype(BF)) - counts
    coarse = jnp.floor(starts * (1.0 / 64.0))
    which = iota((8, parents), 0)
    fields = jnp.where(which == 0, coarse, jnp.where(which == 1, starts - 64.0 * coarse, counts))
    pick = jnp.where(iota((parents, parents), 0) == order_ref[...], 1.0, 0.0).astype(BF)
    ordered = mm(fields.astype(BF), pick).astype(jnp.int32)
    first = 64 * ordered[0:1] + ordered[1:2]
    length = ordered[2:3]
    span_ref[...] = jnp.where(which == 0, first, jnp.where(which == 1, first + length, length))
    both = 16 * first + length
    both = both[:, : parents // 2] | (both[:, parents // 2 :] << 16)
    lines = parents // 256
    info_ref[0, lines:, :] = jnp.zeros((INFO - lines, 128), jnp.int32)
    info_ref[0, lines : lines + 1, :blocks] = dest_ref[...] * blocks + slot_ref[...]
    for i in range(lines):
        info_ref[0, i : i + 1, :] = both[:, i * 128 : (i + 1) * 128]
    tile = info_ref[0]
    for d in range(1, info_ref.shape[0]):
        info_ref[d] = tile


def order_tables(child_counts, parent_order, hil_dest, hil_slot, devices):
    parents = child_counts.shape[1]
    return pl.pallas_call(
        order_kernel,
        out_shape=(
            jax.ShapeDtypeStruct((devices, INFO, 128), jnp.int32),
            jax.ShapeDtypeStruct((8, parents), jnp.int32),
        ),
        in_specs=[VMEM] * 4,
        out_specs=(VMEM, VMEM),
        compiler_params=FULL,
        cost_estimate=cost(32 * parents * parents, 8 * parents),
    )(child_counts, parent_order, hil_dest[None], hil_slot[None])


def pack_kernel(capacity, dest_ref, points_ref, payload_ref, used, sem):
    blocks = dest_ref.shape[0]

    def clear(d, _):
        used[d] = 0
        return 0

    lax.fori_loop(0, used.shape[0], clear, 0)

    def send(b, _):
        d = dest_ref[b]
        place = d * capacity + used[d]
        used[d] = used[d] + 1
        pltpu.make_async_copy(
            points_ref.at[pl.ds(pl.multiple_of(b * ROWS, ROWS), ROWS)],
            payload_ref.at[pl.ds(pl.multiple_of(place * ROWS, ROWS), ROWS)],
            sem,
        ).start()
        return 0

    lax.fori_loop(0, blocks, send, 0)
    whole = pl.ds(0, blocks * ROWS)
    pltpu.make_async_copy(points_ref.at[whole], payload_ref.at[whole], sem).wait()


def pack_blocks(hil_dest, points, devices, capacity):
    return pl.pallas_call(
        functools.partial(pack_kernel, capacity),
        out_shape=jax.ShapeDtypeStruct((devices * capacity * ROWS, points.shape[1]), BF),
        in_specs=[SMEM, HBM],
        out_specs=VMEM,
        scratch_shapes=[pltpu.SMEM((devices,), jnp.int32), pltpu.SemaphoreType.DMA],
        compiler_params=FULL,
        cost_estimate=cost(0, 4 * points.size),
    )(hil_dest, points)


def key_windows(ids_ref, low_ref, count_ref, turn_ref, turned_ref):
    tiles, span = ids_ref.shape
    lane = iota((1, span), 1)
    for t in range(tiles):
        ids = ids_ref[t : t + 1, :]
        sizes = [
            jnp.sum(jnp.where(ids == c, 1.0, 0.0)).astype(jnp.int32) for c in range(PATCHES)
        ]
        starts = [jnp.int32(0)]
        for c in range(1, PATCHES):
            starts.append(starts[-1] + sizes[c - 1])
        most, turn = sizes[0], starts[0]
        for c in range(1, PATCHES):
            turn = jnp.where(sizes[c] > most, starts[c], turn)
            most = jnp.maximum(most, sizes[c])
        firsts = [lax.rem(start - turn + span, span) for start in starts]
        ends = [first + size for first, size in zip(firsts, sizes)]
        turned = jnp.zeros((1, span), jnp.int32)
        for c in range(1, PATCHES):
            turned = jnp.where((lane >= firsts[c]) & (lane < ends[c]), c, turned)
        turned_ref[t : t + 1, :] = turned
        turn_ref[t] = turn
        for b in range(span // ROWS):
            top, bottom = b * ROWS, (b + 1) * ROWS - 1
            low, high = jnp.int32(0), jnp.int32(span)
            for c in range(PATCHES):
                low = jnp.where((firsts[c] <= top) & (top < ends[c]), firsts[c], low)
                high = jnp.where((firsts[c] <= bottom) & (bottom < ends[c]), ends[c], high)
            low = low // ROWS * ROWS
            count = (high - low + WINDOW - 1) // WINDOW
            low_ref[t * (span // ROWS) + b] = jnp.minimum(low, span - count * WINDOW)
            count_ref[t * (span // ROWS) + b] = count


def seat_kernel(
    per_owner,
    source_ref,
    block_ref,
    info_ref,
    ids_ref,
    table_ref,
    local_ref,
    base_ref,
    low_ref,
    count_ref,
    turn_ref,
    turned_ref,
    owner,
    place,
    seats,
):
    blocks = owner.shape[0]
    parents = 128 * 8
    devices = info_ref.shape[0] // 8
    which = iota((16, parents), 0)
    rank = iota((16, parents), 1)
    fields = jnp.where(which == 0, rank // per_owner, jnp.where(which == 1, rank % per_owner, 0))
    fields = fields.astype(F32).astype(BF)

    def one(v, _):
        source = source_ref[v]
        packed = info_ref[pl.ds(pl.multiple_of(source * 8, 8), 8), :]
        line = jnp.concatenate([packed[i : i + 1] for i in range(8)], axis=1)
        first = line // 16
        row = block_ref[v] * ROWS + iota((ROWS, parents), 0)
        inside = (row >= first) & (row < first + line % 16)
        found = mm(fields, jnp.where(inside, 1.0, 0.0).astype(BF), NT)
        owner[pl.ds(v, 1), :] = found[0:1]
        place[pl.ds(v, 1), :] = found[1:2]
        return 0

    lax.fori_loop(0, blocks, one, 0)
    own = owner[...]
    run = own * per_owner + place[...]
    opens = (iota((blocks, ROWS), 1) == 0) | (run != pltpu.roll(run, 1, 1))
    opened = jnp.where(opens, 1.0, 0.0)
    upper = jnp.where(iota((ROWS, ROWS), 0) <= iota((ROWS, ROWS), 1), 1.0, 0.0).astype(BF)
    every = jnp.ones((ROWS, ROWS), BF)
    before = jnp.where(iota((blocks, blocks), 1) < iota((blocks, blocks), 0), 1.0, 0.0).astype(BF)
    local_ref[...] = (mm(opened.astype(BF), upper) - 1.0).astype(jnp.int32)

    def count(e, seat):
        here = own == e.astype(F32)
        marks = jnp.where(here, opened, 0.0).astype(BF)
        total = mm(marks, upper) + mm(before, mm(marks, every).astype(BF))
        return jnp.where(here, total - 1.0, seat)

    seats[...] = lax.fori_loop(0, devices, count, jnp.zeros((blocks, ROWS), F32))
    table_ref[...] = jnp.zeros_like(table_ref)
    field = iota((ROWS, ROWS), 0)

    def lay(v, base):
        base = pl.multiple_of(base, ALIGN)
        base_ref[v] = base
        at = pl.ds(v, 1)
        local = local_ref[at, :]
        seat = seats[at, :]
        coarse = jnp.floor(seat * (1.0 / 64.0))
        lines = (owner[at, :], coarse, seat - 64.0 * coarse)
        values = jnp.ones((ROWS, ROWS), F32)
        for i, line in enumerate(lines):
            values = jnp.where(field == i, line, values)
        previous = jnp.where(iota((1, ROWS), 1) == 0, -1, pltpu.roll(local, 1, 1))
        begins = (field == local) & (local != previous)
        found = mm(jnp.where(begins, 1.0, 0.0).astype(BF), values.astype(BF), NT)
        table_ref[pl.ds(base, ROWS), :] = found.astype(BF)
        return base + (jnp.max(local) + ALIGN) // ALIGN * ALIGN

    base_ref[blocks] = lax.fori_loop(0, blocks, lay, 0)
    key_windows(ids_ref, low_ref, count_ref, turn_ref, turned_ref)


def seat_rows(source, block, info, ids, per_owner):
    blocks = source.shape[0]
    rows = blocks * ROWS
    return pl.pallas_call(
        functools.partial(seat_kernel, per_owner),
        out_shape=(
            jax.ShapeDtypeStruct((rows + CHUNK, 128), BF),
            jax.ShapeDtypeStruct((blocks, ROWS), jnp.int32),
            jax.ShapeDtypeStruct((blocks + 1,), jnp.int32),
            jax.ShapeDtypeStruct((blocks,), jnp.int32),
            jax.ShapeDtypeStruct((blocks,), jnp.int32),
            jax.ShapeDtypeStruct((ids.shape[0],), jnp.int32),
            jax.ShapeDtypeStruct(ids.shape, jnp.int32),
        ),
        in_specs=[SMEM, SMEM, VMEM, VMEM],
        out_specs=(VMEM, VMEM, SMEM, SMEM, SMEM, SMEM, VMEM),
        scratch_shapes=[pltpu.VMEM((blocks, ROWS), F32)] * 3,
        compiler_params=ROOM,
        cost_estimate=cost(40 * rows * 1024, 8 * rows),
    )(source, block, info, ids)


def plan_kernel(round_ref, base_ref, table_ref, code_ref):
    first = (SEAT * round_ref[0]).astype(F32)
    chunks = (base_ref[base_ref.shape[0] - 1] + CHUNK - 1) // CHUNK
    pick = jnp.where(iota((16, 128), 0) == iota((16, 128), 1), 1.0, 0.0).astype(BF)

    def step(c, _):
        at = pl.ds(pl.multiple_of(c * CHUNK, CHUNK), CHUNK)
        lines = mm(pick, table_ref[at, :], NT)
        seat = 64.0 * lines[1:2] + lines[2:3] - first
        seated = (lines[3:4] > 0.5) & (seat >= 0.0) & (seat < float(SEAT))
        code = jnp.where(seated, lines[0:1] * float(SEAT) + seat, -1.0).astype(jnp.int32)
        code_ref[:, at] = jnp.broadcast_to(code, (8, CHUNK))
        return 0

    lax.fori_loop(0, chunks, step, 0)


def plan_seats(step, base, table):
    return pl.pallas_call(
        plan_kernel,
        out_shape=jax.ShapeDtypeStruct((8, table.shape[0]), jnp.int32),
        in_specs=[SMEM, SMEM, VMEM],
        out_specs=VMEM,
        compiler_params=ROOM,
        cost_estimate=cost(64 * table.size, 4 * table.size),
    )(step, base, table)


def rotate_rows(doubled, turn, span):
    coarse = pl.multiple_of(turn // 8 * 8, 8)
    fine = turn % 8
    width = doubled.shape[1]
    rows = doubled[pl.ds(coarse, span + 8), :].reshape(span // 8 + 1, 8, width)
    rolled = pltpu.roll(rows, (8 - fine) % 8, 1)
    kept = iota((span // 8, 8, width), 1) < 8 - fine
    return jnp.where(kept, rolled[:-1], rolled[1:]).reshape(span, width)


def attend_kernel(
    index_ref,
    low_ref,
    count_ref,
    base_ref,
    turn_ref,
    local_ref,
    ids_ref,
    w_ref,
    wo_ref,
    rows_ref,
    out_ref,
    x,
    qx,
    kx,
    vx,
    att,
    doubled,
    wrapped,
    code,
    sems,
):
    tiles, span = ids_ref.shape
    width = w_ref.shape[0]
    cols = HEAD_GROUP * HDIM
    groups = width // cols
    heads = width // HDIM
    per_tile = span // ROWS

    def fetch(t):
        for s in range(t * per_tile, (t + 1) * per_tile):
            pltpu.make_async_copy(
                rows_ref.at[pl.ds(pl.multiple_of(index_ref[s] * ROWS, ROWS), ROWS)],
                x.at[pl.ds(s * ROWS, ROWS)],
                sems.at[t],
            ).start()

    fetch(0)
    out_ref[...] = jnp.zeros_like(out_ref)
    lane = iota((ROWS, 2 * cols), 1)
    of_head = [(lane // HDIM == h) | (lane >= cols) for h in range(HEAD_GROUP)]
    lane_out = lane % cols // HDIM
    for g in range(groups):
        vx[g, :, cols:] = jnp.ones((tiles * span, cols), BF)
    r_i = iota((cols, cols), 0)
    c_i = iota((cols, cols), 1)
    far = jnp.where((r_i != c_i) & (c_i < PATCHES), -FAR, 0.0).astype(BF)
    bounds = []

    for t in range(tiles):
        at = slice(t * span, (t + 1) * span)
        if t + 1 < tiles:
            fetch(t + 1)
        pltpu.make_async_copy(
            rows_ref.at[pl.ds(0, span)], x.at[pl.ds(t * span, span)], sems.at[t]
        ).wait()
        whole = x[at, :].astype(F32)
        doubled[:span, :] = whole
        doubled[span:, :] = whole
        tile_rows = rotate_rows(doubled, turn_ref[t], span).astype(BF)
        x[at, :] = tile_rows
        same = ids_ref[t : t + 1, :] == iota((cols, span), 0)
        patch_hot = jnp.where(same, 1.0, 0.0).astype(BF)
        query = mm(tile_rows, w_ref[:, :width])
        keys = mm(w_ref[:, width : 2 * width], tile_rows, (((0,), (1,)), ((), ())))
        value = mm(tile_rows, w_ref[:, 2 * width :]).astype(BF)
        patch_far = mm(patch_hot, far, TN).astype(BF)
        for g in range(groups):
            some = slice(g * cols, (g + 1) * cols)
            qx[g, at, :cols] = query[:, some].astype(BF)
            qx[g, at, cols:] = patch_far
            kx[g, :cols, at] = keys[some].astype(BF)
            kx[g, cols:, at] = patch_hot
            vx[g, at, :cols] = value[:, some]
        query_most = jnp.max(jnp.abs(query), axis=0, keepdims=True)
        key_most = jnp.max(jnp.abs(keys), axis=1, keepdims=True)
        by_head = jnp.where(
            iota((heads, width), 1) // HDIM == iota((heads, width), 0), query_most, 0.0
        )
        bounds.append(mm(by_head.astype(BF), jnp.broadcast_to(key_most, (width, 128)).astype(BF)))
    bound = bounds[0]
    for other in bounds[1:]:
        bound = jnp.maximum(bound, other)
    safe = jnp.max(bound) * SCORE_SCALE < SCORE_SAFE

    def block(s, _):
        start = pl.multiple_of(s // per_tile * span, span)
        steps = count_ref[s]
        here = pl.ds(pl.multiple_of(s * ROWS, ROWS), ROWS)

        def run(first, length, exact):
            at = pl.ds(pl.multiple_of(start + first, ROWS), length)
            scores = []
            for g in range(groups):
                q = qx[g, here, :]
                stacked = jnp.concatenate(
                    [jnp.where(of_head[h], q, jnp.zeros_like(q)) for h in range(HEAD_GROUP)],
                    axis=0,
                )
                scores.append(mm(stacked, kx[g, :, at]))
            for g in range(groups):
                level = scores[g] * SCORE_SCALE
                if exact:
                    level = level - jnp.max(level, axis=1, keepdims=True)
                weights = jnp.exp2(level).astype(BF)
                mixed = mm(weights, vx[g, at, :])
                mixed = mixed.reshape(HEAD_GROUP, ROWS, 2 * cols)
                own = mixed[0]
                for h in range(1, HEAD_GROUP):
                    own = jnp.where(lane_out == h, mixed[h], own)
                att[here, g * cols : (g + 1) * cols] = (own[:, :cols] / own[:, cols:]).astype(BF)

        for i in range(span // WINDOW):
            pl.when(safe & (steps == i + 1))(
                functools.partial(run, low_ref[s], (i + 1) * WINDOW, False)
            )
        pl.when(jnp.logical_not(safe))(functools.partial(run, 0, span, True))
        return 0

    lax.fori_loop(0, tiles * per_tile, block, 0)

    for t in range(tiles):
        at = slice(t * span, (t + 1) * span)
        turn = turn_ref[t]
        mixed = (x[at, :].astype(F32) + mm(att[at, :], wo_ref[...])).astype(BF)
        wrapped[t, :span, :] = mixed
        wrapped[t, span:, :] = mixed[:ROWS]
        runs = local_ref[t : t + 1, :] + iota((1, span), 1) // ROWS * ROWS
        runs = pltpu.roll(jnp.broadcast_to(runs, (8, span)), lax.rem(span - turn, span), 1)
        code[t, :, :span] = runs
        code[t, :, span:] = runs[:, :ROWS]
        for b in range(per_tile):
            first = lax.rem(b * ROWS + span - turn, span) // ROWS * ROWS
            window = pl.ds(pl.multiple_of(first, ROWS), 2 * ROWS)
            run = iota((ROWS, 2 * ROWS), 0) + b * ROWS == code[t, 0:1, window]
            sums = mm(jnp.where(run, 1.0, 0.0).astype(BF), wrapped[t, window, :])
            put = pl.multiple_of(base_ref[t * per_tile + b], ALIGN)
            out_ref[pl.ds(put, ROWS), :] = sums.astype(BF)


def attend(index, low, count, base, turn, local, ids, w_qkv, w_out, rows):
    tiles, span = ids.shape
    width = rows.shape[1]
    cols = HEAD_GROUP * HDIM
    groups = width // cols
    pairs = tiles * span * span * HEAD_GROUP
    return pl.pallas_call(
        attend_kernel,
        out_shape=jax.ShapeDtypeStruct((tiles * span + CHUNK, width), BF),
        in_specs=[SMEM, SMEM, SMEM, SMEM, SMEM, VMEM, VMEM, VMEM, VMEM, HBM],
        out_specs=VMEM,
        scratch_shapes=[
            pltpu.VMEM((tiles * span, width), BF),
            pltpu.VMEM((groups, tiles * span, 2 * cols), BF),
            pltpu.VMEM((groups, 2 * cols, tiles * span), BF),
            pltpu.VMEM((groups, tiles * span, 2 * cols), BF),
            pltpu.VMEM((tiles * span, width), BF),
            pltpu.VMEM((2 * span, width), F32),
            pltpu.VMEM((tiles, span + ROWS, width), BF),
            pltpu.VMEM((tiles, 8, span + ROWS), jnp.int32),
            pltpu.SemaphoreType.DMA((tiles,)),
        ],
        compiler_params=ROOM,
        cost_estimate=cost(pairs * 1024, 4 * rows.size, pairs),
    )(index, low, count, base, turn, local, ids, w_qkv, w_out, rows)


def route_kernel(base_ref, code_ref, sums_ref, out_ref, acc):
    total = out_ref.shape[0]
    chunks = (base_ref[base_ref.shape[0] - 1] + CHUNK - 1) // CHUNK
    seat = iota((total, 1), 0) + pl.program_id(0) * total
    acc[...] = jnp.zeros_like(acc)

    def step(c, _):
        at = pl.ds(pl.multiple_of(c * CHUNK, CHUNK), CHUNK)
        member = jnp.where(seat == code_ref[0:1, at], 1.0, 0.0).astype(BF)
        acc[...] += mm(member, sums_ref[at, :])
        return 0

    lax.fori_loop(0, chunks, step, 0)
    out_ref[...] = acc[...].astype(BF)


def route_sums(base, code, sums, devices):
    count, width = sums.shape
    total = devices * SEAT
    part = min(TURN, total)
    return pl.pallas_call(
        route_kernel,
        grid=(total // part,),
        out_shape=jax.ShapeDtypeStruct((total, width), BF),
        in_specs=[SMEM, VMEM, VMEM],
        out_specs=pl.BlockSpec((part, width), lambda i: (i, 0)),
        scratch_shapes=[pltpu.VMEM((part, width), F32)],
        compiler_params=ROOM,
        cost_estimate=cost(total * count * width, 4 * count * width),
    )(base, code, sums)


def fold_rows(step, pieces_ref, about):
    total = 0.0
    part = min(TURN, pieces_ref.shape[0])
    first = step * SEAT
    seats = []
    for i in (1, 3):
        seat = about[:, i + 1 : i + 2].astype(jnp.int32) - first
        seated = (seat >= 0) & (seat < SEAT)
        seats.append(jnp.where(seated, about[:, i : i + 1].astype(jnp.int32) * SEAT + seat, -1))
    for low in range(0, pieces_ref.shape[0], part):
        column = iota((1, part), 1) + low
        member = (column == seats[0]) | (column == seats[1])
        member = jnp.where(member, 1.0, 0.0).astype(BF)
        total = total + mm(member, pieces_ref[low : low + part, :])
    return total


def fold_kernel(step_ref, pieces_ref, about_ref, before_ref, out_ref):
    out_ref[...] = before_ref[...] + fold_rows(step_ref[0], pieces_ref, about_ref[...])


def fold_pieces(step, pieces, about, before):
    parents, width = before.shape
    chunk = 256
    along = lambda i: (i, 0)
    return pl.pallas_call(
        fold_kernel,
        grid=(parents // chunk,),
        out_shape=jax.ShapeDtypeStruct((parents, width), F32),
        in_specs=[
            SMEM,
            pl.BlockSpec(pieces.shape, lambda i: (0, 0)),
            pl.BlockSpec((chunk, 128), along),
            pl.BlockSpec((chunk, width), along),
        ],
        out_specs=pl.BlockSpec((chunk, width), along),
        compiler_params=ROOM,
        cost_estimate=cost(2 * parents * pieces.size, 4 * pieces.size),
    )(step, pieces, about, before)


def whole_tiles(rows):
    return (rows + 15) // 16 * 16


def pad_rows(value):
    spare = whole_tiles(value.shape[0]) - value.shape[0]
    if spare == 0:
        return value
    return jnp.concatenate([value, jnp.zeros((spare, value.shape[1]), value.dtype)], axis=0)


def pool_kernel(
    per_owner,
    pieces_ref,
    more_ref,
    about_ref,
    w_ref,
    gain_ref,
    shift_ref,
    cot_ref,
    pooled_ref,
    sent_ref,
    acc,
    sums,
):
    step = pl.program_id(0)

    @pl.when(step == 0)
    def _():
        acc[...] = jnp.zeros_like(acc)
        sums[...] = jnp.zeros_like(sums)

    chunk, width = more_ref.shape
    about = about_ref[...]
    total = more_ref[...] + fold_rows(0, pieces_ref, about)
    lengths = about[:, 0:1]
    parent_in = (total / lengths).astype(BF)
    w_pool = w_ref[...]
    gain = gain_ref[...]
    projected = mm(parent_in, w_pool)
    centred = projected - jnp.mean(projected, axis=-1, keepdims=True)
    variance = jnp.mean(centred * centred, axis=-1, keepdims=True)
    inv_std = lax.rsqrt(variance + norm_eps)
    normed = centred * inv_std
    shifted = normed * gain + shift_ref[...]
    normal_cdf = 0.5 * (1.0 + lax.erf(shifted * inv_sqrt_two))
    pooled_ref[...] = (shifted * normal_cdf).astype(BF)
    grad_act = cot_ref[...].astype(F32) * (
        normal_cdf + shifted * jnp.exp(-0.5 * shifted * shifted) * inv_sqrt_tau
    )
    sums[0:1, :] += jnp.sum(grad_act * normed, axis=0, keepdims=True)
    sums[1:2, :] += jnp.sum(grad_act, axis=0, keepdims=True)
    scaled = grad_act * gain
    grad_proj = (
        (
            scaled
            - jnp.mean(scaled, axis=-1, keepdims=True)
            - normed * jnp.mean(scaled * normed, axis=-1, keepdims=True)
        )
        * inv_std
    ).astype(BF)
    acc[...] += mm(parent_in, grad_proj, TN)
    back = mm(grad_proj, w_pool, NT)
    devices, _, width = sent_ref.shape
    fits = chunk // per_owner
    for d in range(fits):
        part = back[d * per_owner : (d + 1) * per_owner]
        sent_ref[step * fits + d, : whole_tiles(per_owner), :] = pad_rows(part).astype(BF)

    @pl.when(step == pl.num_programs(0) - 1)
    def _():
        each = acc.shape[0] // devices
        exact = sums[0:2, :]
        high = exact.astype(BF).astype(F32)
        parts = []
        for value in (high, exact - high):
            for row in range(2):
                for low in range(0, acc.shape[1], width):
                    parts.append(value[row : row + 1, low : low + width])
        norm = jnp.concatenate(parts, axis=0)
        for d in range(devices):
            parts = []
            for side in range(0, acc.shape[1], width):
                parts.append(pad_rows(acc[d * each : (d + 1) * each, side : side + width]))
            rest = jnp.concatenate(parts + [norm], axis=0)
            sent_ref[d, whole_tiles(per_owner) :, :] = rest.astype(BF)


def pool(pieces, more, about, w_pool, gain, shift, cotangent):
    parents, width = more.shape
    wide = w_pool.shape[1]
    chunk = parents
    devices = pieces.shape[0] // SEAT
    tall = whole_tiles(parents // devices) + wide // width * whole_tiles(width // devices)
    tall += 4 * wide // width
    fixed = lambda i: (0, 0)
    along = lambda i: (i, 0)
    return pl.pallas_call(
        functools.partial(pool_kernel, parents * SEAT // pieces.shape[0]),
        grid=(parents // chunk,),
        out_shape=(
            jax.ShapeDtypeStruct((parents, wide), BF),
            jax.ShapeDtypeStruct((devices, tall, width), BF),
        ),
        in_specs=[
            pl.BlockSpec(pieces.shape, fixed),
            pl.BlockSpec((chunk, width), along),
            pl.BlockSpec((chunk, 128), along),
            pl.BlockSpec((width, wide), fixed),
            pl.BlockSpec((1, wide), fixed),
            pl.BlockSpec((1, wide), fixed),
            pl.BlockSpec((chunk, wide), along),
        ],
        out_specs=(
            pl.BlockSpec((chunk, wide), along),
            pl.BlockSpec((devices, tall, width), lambda i: (0, 0, 0)),
        ),
        scratch_shapes=[
            pltpu.VMEM((width, wide), F32),
            pltpu.VMEM((8, wide), F32),
        ],
        compiler_params=FULL,
        cost_estimate=cost(6 * parents * width * wide, 8 * parents * wide, 2 * parents * wide),
    )(pieces, more, about, w_pool, gain, shift, cotangent)


def spread_kernel(span_ref, grad_ref, out_ref, share):
    step = pl.program_id(0)
    chunk = out_ref.shape[0]
    parents, width = share.shape

    @pl.when(step == 0)
    def _():
        pick = jnp.where(iota((8, width), 0) == 2, 1.0, 0.0).astype(BF)
        lengths = mm(jnp.minimum(span_ref[...], 64).astype(F32).astype(BF), pick, TN)
        per_owner = parents // grad_ref.shape[0]
        grads = [grad_ref[d, :per_owner, :].astype(F32) for d in range(grad_ref.shape[0])]
        share[...] = (jnp.concatenate(grads, axis=0) / lengths).astype(BF)

    row = iota((chunk, parents), 0) + step * chunk
    inside = (row >= span_ref[0:1, :]) & (row < span_ref[1:2, :])
    out_ref[...] = mm(jnp.where(inside, 1.0, 0.0).astype(BF), share[...]).astype(BF)


def spread_grads(span, arrived, rows):
    parents = span.shape[1]
    width = arrived.shape[2]
    chunk = 512
    fixed = lambda i: (0, 0)
    return pl.pallas_call(
        spread_kernel,
        grid=(rows // chunk,),
        out_shape=jax.ShapeDtypeStruct((rows, width), BF),
        in_specs=[
            pl.BlockSpec((8, parents), fixed),
            pl.BlockSpec(arrived.shape, lambda i: (0, 0, 0)),
        ],
        out_specs=pl.BlockSpec((chunk, width), lambda i: (i, 0)),
        scratch_shapes=[pltpu.VMEM((parents, width), BF)],
        compiler_params=ROOM,
        cost_estimate=cost(2 * rows * parents * width, 4 * rows * width),
    )(span, arrived)


def settle_kernel(per_owner, arrived_ref, shared_ref, norm_ref):
    devices, tall, width = arrived_ref.shape
    low = whole_tiles(per_owner)
    total = arrived_ref[0, low:, :].astype(F32)
    for d in range(1, devices):
        total = total + arrived_ref[d, low:, :].astype(F32)
    weight_rows = shared_ref.shape[1]
    weight = total[:weight_rows].astype(BF)
    for d in range(devices):
        shared_ref[d] = weight
    norm = total[weight_rows : weight_rows + 8]
    sides = norm_ref.shape[1] // width
    for row in range(2):
        for side in range(sides):
            i = row * sides + side
            value = norm[i : i + 1] + norm[2 * sides + i : 2 * sides + i + 1]
            norm_ref[row : row + 1, side * width : (side + 1) * width] = value


def settle(arrived, per_owner, weight_rows, wide):
    devices, tall, width = arrived.shape
    return pl.pallas_call(
        functools.partial(settle_kernel, per_owner),
        out_shape=(
            jax.ShapeDtypeStruct((devices, weight_rows, width), BF),
            jax.ShapeDtypeStruct((2, wide), F32),
        ),
        in_specs=[VMEM],
        out_specs=(VMEM, VMEM),
        compiler_params=ROOM,
        cost_estimate=cost(arrived.size, 2 * arrived.size),
    )(arrived)


def piece_seats(info, codes, blocks, per_owner):
    devices = codes.shape[0]
    parents = devices * per_owner
    me = lax.axis_index("pts")
    packed = info.reshape(devices, parents)
    span = blocks * ROWS
    lane = jnp.arange(blocks)

    def at_block(block):
        found = jnp.where(block[:, :, None] == lane, codes[:, None, :], 0)
        return jnp.sum(found, axis=2)

    first = packed // 16
    end = first + packed % 16 - 1
    near = at_block(first // ROWS)
    far = at_block(end // ROWS)
    split = first // ROWS != end // ROWS
    holders = jnp.arange(devices)
    by_owner = lambda value: value.reshape(devices, devices, per_owner, 1)
    filled = (by_owner(near // blocks) == holders).astype(jnp.int32)
    filled += (by_owner(jnp.where(split, far // blocks, -1)) == holders).astype(jnp.int32)
    rounds = (jnp.max(jnp.sum(filled, axis=(0, 2))) + SEAT - 1) // SEAT

    mine = lambda value: lax.dynamic_slice_in_dim(value, me * per_owner, per_owner, axis=1)
    near, far, split, first, packed = map(mine, (near, far, split, first, packed))
    near_key = near * ROWS + first % ROWS
    far_key = jnp.where(split, far * ROWS, devices * span)
    near_key, far_key = near_key.reshape(parents, 1), far_key.reshape(parents, 1)
    every = jnp.concatenate([near_key, far_key], axis=0).reshape(1, 2 * parents)

    def place(key):
        holder = key // span
        rank = jnp.sum((every < key) & (every >= holder * span), axis=1, keepdims=True)
        return holder, jnp.where(holder < devices, rank, -1)

    length = (packed % 16).reshape(parents, 1)
    columns = (length,) + place(near_key) + place(far_key)
    wide = iota((parents, 128), 1)
    about = jnp.zeros((parents, 128), jnp.int32)
    for i, column in enumerate(columns):
        about = jnp.where(wide == i, column, about)
    return about.astype(F32), rounds.astype(jnp.int32)


def swap(parts):
    return lax.all_to_all(parts, "pts", split_axis=0, concat_axis=0, tiled=True)


def exchange(rows, devices):
    return swap(rows.reshape(devices, rows.shape[0] // devices, rows.shape[1])).reshape(rows.shape)


def received_index(codes, blocks, capacity):
    devices = codes.shape[0]
    me = lax.axis_index("pts")
    mine = codes // blocks == me
    slots = codes % blocks
    lane = jnp.arange(blocks)
    rank = jnp.sum(mine[:, None, :] & (lane[None, :] < lane[:, None])[None], axis=2)
    index = jnp.arange(devices)[:, None] * capacity + rank
    both = index * blocks + lane[None, :]
    hit = mine[:, :, None] & (slots[:, :, None] == lane[None, None, :])
    both = jnp.sum(jnp.where(hit, both[:, :, None], 0), axis=(0, 1)).astype(jnp.int32)
    return both // blocks, both % blocks


def local(
    points,
    hil_dest,
    hil_slot,
    patch_ids,
    child_counts,
    parent_order,
    w_qkv,
    w_out,
    w_pool,
    norm_gain,
    norm_shift,
    cotangent,
):
    devices = lax.axis_size("pts")
    blocks = hil_dest.shape[0]
    rows, width = points.shape
    wide = w_pool.shape[1]
    parents = child_counts.shape[1]
    per_owner = parents // devices
    capacity = (blocks + devices - 1) // devices

    me = lax.axis_index("pts")
    info, span = order_tables(child_counts, parent_order, hil_dest, hil_slot, devices)
    info = swap(info)
    payload = pack_blocks(hil_dest, points, devices, capacity)
    received = exchange(payload, devices)
    lines = parents // 256
    codes = info[:, lines, :blocks]
    packed = info[:, :lines]
    info = jnp.concatenate(
        [packed & 65535, lax.shift_right_logical(packed, jnp.int32(16))], axis=1
    )
    index, block = received_index(codes, blocks, capacity)
    source = index // capacity
    table, local_run, base, low, count, turn, turned = seat_rows(
        source, block, info.reshape(-1, 128), patch_ids, per_owner
    )
    code = plan_seats(jnp.zeros((1,), jnp.int32), base, table)
    about, rounds = piece_seats(info, codes, blocks, per_owner)
    more = jnp.broadcast_to(about[:, 127:], (parents, width))
    index, low, count, turn, turned, base, local_run, code, about, rounds, more = (
        lax.optimization_barrier(
            (index, low, count, turn, turned, base, local_run, code, about, rounds, more)
        )
    )
    local_run = local_run.reshape(patch_ids.shape)
    sums = attend(index, low, count, base, turn, local_run, turned, w_qkv, w_out, received)
    pieces = exchange(route_sums(base, code, sums, devices), devices)

    def turn_again(carry):
        step, before = carry
        step = step.reshape(1)
        late = exchange(route_sums(base, plan_seats(step, base, table), sums, devices), devices)
        return step[0] + 1, fold_pieces(step, late, about, before)

    _, more = lax.while_loop(
        lambda carry: carry[0] < rounds, turn_again, (jnp.int32(1), more)
    )
    pooled, outgoing = pool(
        pieces, more, about, w_pool, norm_gain[None], norm_shift[None], cotangent
    )
    arrived = swap(outgoing)
    each = width // devices
    tall = whole_tiles(each)
    sides = wide // width
    shared, grad_norm = settle(arrived, per_owner, sides * tall, wide)
    shared = swap(shared)
    grad_weight = jnp.concatenate(
        [shared[:, side * tall : side * tall + each] for side in range(sides)], axis=2
    )
    grad_weight = grad_weight.reshape(width, wide).astype(F32)
    grad_points = spread_grads(span, arrived, rows)
    return (pooled, grad_points, grad_weight, grad_norm)


def solution(mesh):
    in_specs = (
        P(("grp", "pts"), None),
        P(("grp", "pts")),
        P(("grp", "pts")),
        P(("grp", "pts"), None),
        P(("grp", "pts"), None),
        P(("grp", "pts"), None),
        P(),
        P(),
        P(),
        P(),
        P(),
        P(("grp", "pts"), None),
    )
    out_specs = (P(("grp", "pts"), None), P(("grp", "pts"), None), P("grp", None), P("grp", None))
    return jax.shard_map(local, mesh=mesh, in_specs=in_specs, out_specs=out_specs, check_vma=False)
```

```python
import functools
import math

import jax
import jax.numpy as jnp
from jax import lax
from jax.experimental import pallas as pl
from jax.experimental.pallas import tpu as pltpu
from jax.sharding import PartitionSpec as P

HDIM = 16
HEAD_GROUP = 8
ROWS = 128
SEAT = 96
TURN = 16 * SEAT
INFO = 8
ALIGN = 16
CHUNK = 512
WINDOW = 256
PATCHES = 4
FAR = 2.0**100
SCORE_SCALE = HDIM**-0.5 * math.log2(math.e)
SCORE_SAFE = 98.0

inv_sqrt_two = 0.7071067811865476
inv_sqrt_tau = 0.3989422804014327
norm_eps = 1e-05

BF = jnp.bfloat16
F32 = jnp.float32
NT = (((1,), (1,)), ((), ()))
TN = (((0,), (0,)), ((), ()))
VMEM = pl.BlockSpec(memory_space=pltpu.VMEM)
HBM = pl.BlockSpec(memory_space=pltpu.HBM)
SMEM = pl.BlockSpec(memory_space=pltpu.SMEM)
ANY = pl.BlockSpec(memory_space=pl.ANY)
ROOM = pltpu.CompilerParams(vmem_limit_bytes=48 << 20)
FULL = pltpu.CompilerParams(vmem_limit_bytes=60 << 20)


def iota(shape, dim):
    return lax.broadcasted_iota(jnp.int32, shape, dim)


def mm(a, b, dims=(((1,), (0,)), ((), ()))):
    return lax.dot_general(a, b, dims, preferred_element_type=F32)


def cost(flops, bytes_accessed, transcendentals=0):
    return pl.CostEstimate(
        flops=int(flops), bytes_accessed=int(bytes_accessed), transcendentals=int(transcendentals)
    )


def order_kernel(counts_ref, order_ref, dest_ref, slot_ref, info_ref, span_ref):
    parents = counts_ref.shape[1]
    blocks = dest_ref.shape[1]
    counts = jnp.broadcast_to(counts_ref[...], (8, parents)).astype(F32)
    upper = jnp.where(iota((parents, parents), 0) <= iota((parents, parents), 1), 1.0, 0.0)
    starts = mm(counts.astype(BF), upper.astype(BF)) - counts
    coarse = jnp.floor(starts * (1.0 / 64.0))
    which = iota((8, parents), 0)
    fields = jnp.where(which == 0, coarse, jnp.where(which == 1, starts - 64.0 * coarse, counts))
    pick = jnp.where(iota((parents, parents), 0) == order_ref[...], 1.0, 0.0).astype(BF)
    ordered = mm(fields.astype(BF), pick).astype(jnp.int32)
    first = 64 * ordered[0:1] + ordered[1:2]
    length = ordered[2:3]
    span_ref[...] = jnp.where(which == 0, first, jnp.where(which == 1, first + length, length))
    both = 16 * first + length
    both = both[:, : parents // 2] | (both[:, parents // 2 :] << 16)
    lines = parents // 256
    info_ref[0, lines:, :] = jnp.zeros((INFO - lines, 128), jnp.int32)
    info_ref[0, lines : lines + 1, :blocks] = dest_ref[...] * blocks + slot_ref[...]
    for i in range(lines):
        info_ref[0, i : i + 1, :] = both[:, i * 128 : (i + 1) * 128]
    tile = info_ref[0]
    for d in range(1, info_ref.shape[0]):
        info_ref[d] = tile


def order_tables(child_counts, parent_order, hil_dest, hil_slot, devices):
    parents = child_counts.shape[1]
    return pl.pallas_call(
        order_kernel,
        out_shape=(
            jax.ShapeDtypeStruct((devices, INFO, 128), jnp.int32),
            jax.ShapeDtypeStruct((8, parents), jnp.int32),
        ),
        in_specs=[VMEM] * 4,
        out_specs=(VMEM, VMEM),
        compiler_params=FULL,
        cost_estimate=cost(32 * parents * parents, 8 * parents),
    )(child_counts, parent_order, hil_dest[None], hil_slot[None])


def pack_kernel(capacity, dest_ref, points_ref, payload_ref, used, sem):
    blocks = dest_ref.shape[0]

    def clear(d, _):
        used[d] = 0
        return 0

    lax.fori_loop(0, used.shape[0], clear, 0)

    def send(b, _):
        d = dest_ref[b]
        place = d * capacity + used[d]
        used[d] = used[d] + 1
        pltpu.make_async_copy(
            points_ref.at[pl.ds(pl.multiple_of(b * ROWS, ROWS), ROWS)],
            payload_ref.at[pl.ds(pl.multiple_of(place * ROWS, ROWS), ROWS)],
            sem,
        ).start()
        return 0

    lax.fori_loop(0, blocks, send, 0)
    whole = pl.ds(0, blocks * ROWS)
    pltpu.make_async_copy(points_ref.at[whole], payload_ref.at[whole], sem).wait()


def pack_blocks(hil_dest, points, devices, capacity):
    return pl.pallas_call(
        functools.partial(pack_kernel, capacity),
        out_shape=jax.ShapeDtypeStruct((devices * capacity * ROWS, points.shape[1]), BF),
        in_specs=[SMEM, HBM],
        out_specs=VMEM,
        scratch_shapes=[pltpu.SMEM((devices,), jnp.int32), pltpu.SemaphoreType.DMA],
        compiler_params=FULL,
        cost_estimate=cost(0, 4 * points.size),
    )(hil_dest, points)


def key_windows(ids_ref, low_ref, count_ref, turn_ref, turned_ref):
    tiles, span = ids_ref.shape
    lane = iota((1, span), 1)
    for t in range(tiles):
        ids = ids_ref[t : t + 1, :]
        sizes = [
            jnp.sum(jnp.where(ids == c, 1.0, 0.0)).astype(jnp.int32) for c in range(PATCHES)
        ]
        starts = [jnp.int32(0)]
        for c in range(1, PATCHES):
            starts.append(starts[-1] + sizes[c - 1])
        most, turn = sizes[0], starts[0]
        for c in range(1, PATCHES):
            turn = jnp.where(sizes[c] > most, starts[c], turn)
            most = jnp.maximum(most, sizes[c])
        firsts = [lax.rem(start - turn + span, span) for start in starts]
        ends = [first + size for first, size in zip(firsts, sizes)]
        turned = jnp.zeros((1, span), jnp.int32)
        for c in range(1, PATCHES):
            turned = jnp.where((lane >= firsts[c]) & (lane < ends[c]), c, turned)
        turned_ref[t : t + 1, :] = turned
        turn_ref[t] = turn
        for b in range(span // ROWS):
            top, bottom = b * ROWS, (b + 1) * ROWS - 1
            low, high = jnp.int32(0), jnp.int32(span)
            for c in range(PATCHES):
                low = jnp.where((firsts[c] <= top) & (top < ends[c]), firsts[c], low)
                high = jnp.where((firsts[c] <= bottom) & (bottom < ends[c]), ends[c], high)
            low = low // ROWS * ROWS
            count = (high - low + WINDOW - 1) // WINDOW
            low_ref[t * (span // ROWS) + b] = jnp.minimum(low, span - count * WINDOW)
            count_ref[t * (span // ROWS) + b] = count


def seat_kernel(
    per_owner,
    source_ref,
    block_ref,
    info_ref,
    ids_ref,
    table_ref,
    local_ref,
    base_ref,
    low_ref,
    count_ref,
    turn_ref,
    turned_ref,
    owner,
    place,
    seats,
):
    blocks = owner.shape[0]
    parents = 128 * 8
    devices = info_ref.shape[0] // 8
    which = iota((16, parents), 0)
    rank = iota((16, parents), 1)
    fields = jnp.where(which == 0, rank // per_owner, jnp.where(which == 1, rank % per_owner, 0))
    fields = fields.astype(F32).astype(BF)

    def one(v, _):
        source = source_ref[v]
        packed = info_ref[pl.ds(pl.multiple_of(source * 8, 8), 8), :]
        line = jnp.concatenate([packed[i : i + 1] for i in range(8)], axis=1)
        first = line // 16
        row = block_ref[v] * ROWS + iota((ROWS, parents), 0)
        inside = (row >= first) & (row < first + line % 16)
        found = mm(fields, jnp.where(inside, 1.0, 0.0).astype(BF), NT)
        owner[pl.ds(v, 1), :] = found[0:1]
        place[pl.ds(v, 1), :] = found[1:2]
        return 0

    lax.fori_loop(0, blocks, one, 0)
    own = owner[...]
    run = own * per_owner + place[...]
    opens = (iota((blocks, ROWS), 1) == 0) | (run != pltpu.roll(run, 1, 1))
    opened = jnp.where(opens, 1.0, 0.0)
    upper = jnp.where(iota((ROWS, ROWS), 0) <= iota((ROWS, ROWS), 1), 1.0, 0.0).astype(BF)
    every = jnp.ones((ROWS, ROWS), BF)
    before = jnp.where(iota((blocks, blocks), 1) < iota((blocks, blocks), 0), 1.0, 0.0).astype(BF)
    local_ref[...] = (mm(opened.astype(BF), upper) - 1.0).astype(jnp.int32)

    def count(e, seat):
        here = own == e.astype(F32)
        marks = jnp.where(here, opened, 0.0).astype(BF)
        total = mm(marks, upper) + mm(before, mm(marks, every).astype(BF))
        return jnp.where(here, total - 1.0, seat)

    seats[...] = lax.fori_loop(0, devices, count, jnp.zeros((blocks, ROWS), F32))
    table_ref[...] = jnp.zeros_like(table_ref)
    field = iota((ROWS, ROWS), 0)

    def lay(v, base):
        base = pl.multiple_of(base, ALIGN)
        base_ref[v] = base
        at = pl.ds(v, 1)
        local = local_ref[at, :]
        seat = seats[at, :]
        coarse = jnp.floor(seat * (1.0 / 64.0))
        lines = (owner[at, :], coarse, seat - 64.0 * coarse)
        values = jnp.ones((ROWS, ROWS), F32)
        for i, line in enumerate(lines):
            values = jnp.where(field == i, line, values)
        previous = jnp.where(iota((1, ROWS), 1) == 0, -1, pltpu.roll(local, 1, 1))
        begins = (field == local) & (local != previous)
        found = mm(jnp.where(begins, 1.0, 0.0).astype(BF), values.astype(BF), NT)
        table_ref[pl.ds(base, ROWS), :] = found.astype(BF)
        return base + (jnp.max(local) + ALIGN) // ALIGN * ALIGN

    base_ref[blocks] = lax.fori_loop(0, blocks, lay, 0)
    key_windows(ids_ref, low_ref, count_ref, turn_ref, turned_ref)


def seat_rows(source, block, info, ids, per_owner):
    blocks = source.shape[0]
    rows = blocks * ROWS
    return pl.pallas_call(
        functools.partial(seat_kernel, per_owner),
        out_shape=(
            jax.ShapeDtypeStruct((rows + CHUNK, 128), BF),
            jax.ShapeDtypeStruct((blocks, ROWS), jnp.int32),
            jax.ShapeDtypeStruct((blocks + 1,), jnp.int32),
            jax.ShapeDtypeStruct((blocks,), jnp.int32),
            jax.ShapeDtypeStruct((blocks,), jnp.int32),
            jax.ShapeDtypeStruct((ids.shape[0],), jnp.int32),
            jax.ShapeDtypeStruct(ids.shape, jnp.int32),
        ),
        in_specs=[SMEM, SMEM, VMEM, VMEM],
        out_specs=(VMEM, VMEM, SMEM, SMEM, SMEM, SMEM, VMEM),
        scratch_shapes=[pltpu.VMEM((blocks, ROWS), F32)] * 3,
        compiler_params=ROOM,
        cost_estimate=cost(40 * rows * 1024, 8 * rows),
    )(source, block, info, ids)


def plan_kernel(round_ref, base_ref, table_ref, code_ref):
    first = (SEAT * round_ref[0]).astype(F32)
    chunks = (base_ref[base_ref.shape[0] - 1] + CHUNK - 1) // CHUNK
    pick = jnp.where(iota((16, 128), 0) == iota((16, 128), 1), 1.0, 0.0).astype(BF)

    def step(c, _):
        at = pl.ds(pl.multiple_of(c * CHUNK, CHUNK), CHUNK)
        lines = mm(pick, table_ref[at, :], NT)
        seat = 64.0 * lines[1:2] + lines[2:3] - first
        seated = (lines[3:4] > 0.5) & (seat >= 0.0) & (seat < float(SEAT))
        code = jnp.where(seated, lines[0:1] * float(SEAT) + seat, -1.0).astype(jnp.int32)
        code_ref[:, at] = jnp.broadcast_to(code, (8, CHUNK))
        return 0

    lax.fori_loop(0, chunks, step, 0)


def plan_seats(step, base, table):
    return pl.pallas_call(
        plan_kernel,
        out_shape=jax.ShapeDtypeStruct((8, table.shape[0]), jnp.int32),
        in_specs=[SMEM, SMEM, VMEM],
        out_specs=VMEM,
        compiler_params=ROOM,
        cost_estimate=cost(64 * table.size, 4 * table.size),
    )(step, base, table)


def rotate_rows(doubled, turn, span):
    coarse = pl.multiple_of(turn // 8 * 8, 8)
    fine = turn % 8
    width = doubled.shape[1]
    rows = doubled[pl.ds(coarse, span + 8), :].reshape(span // 8 + 1, 8, width)
    rolled = pltpu.roll(rows, (8 - fine) % 8, 1)
    kept = iota((span // 8, 8, width), 1) < 8 - fine
    return jnp.where(kept, rolled[:-1], rolled[1:]).reshape(span, width)


def attend_kernel(
    index_ref,
    low_ref,
    count_ref,
    base_ref,
    turn_ref,
    local_ref,
    ids_ref,
    w_ref,
    wo_ref,
    rows_ref,
    out_ref,
    x,
    qx,
    kx,
    vx,
    att,
    doubled,
    wrapped,
    code,
    sems,
):
    tiles, span = ids_ref.shape
    width = w_ref.shape[0]
    cols = HEAD_GROUP * HDIM
    groups = width // cols
    heads = width // HDIM
    per_tile = span // ROWS

    def fetch(t):
        for s in range(t * per_tile, (t + 1) * per_tile):
            pltpu.make_async_copy(
                rows_ref.at[pl.ds(pl.multiple_of(index_ref[s] * ROWS, ROWS), ROWS)],
                x.at[pl.ds(s * ROWS, ROWS)],
                sems.at[t],
            ).start()

    fetch(0)
    out_ref[...] = jnp.zeros_like(out_ref)
    lane = iota((ROWS, 2 * cols), 1)
    of_head = [(lane // HDIM == h) | (lane >= cols) for h in range(HEAD_GROUP)]
    lane_out = lane % cols // HDIM
    for g in range(groups):
        vx[g, :, cols:] = jnp.ones((tiles * span, cols), BF)
    r_i = iota((cols, cols), 0)
    c_i = iota((cols, cols), 1)
    far = jnp.where((r_i != c_i) & (c_i < PATCHES), -FAR, 0.0).astype(BF)
    bounds = []

    for t in range(tiles):
        at = slice(t * span, (t + 1) * span)
        if t + 1 < tiles:
            fetch(t + 1)
        pltpu.make_async_copy(
            rows_ref.at[pl.ds(0, span)], x.at[pl.ds(t * span, span)], sems.at[t]
        ).wait()
        whole = x[at, :].astype(F32)
        doubled[:span, :] = whole
        doubled[span:, :] = whole
        tile_rows = rotate_rows(doubled, turn_ref[t], span).astype(BF)
        x[at, :] = tile_rows
        same = ids_ref[t : t + 1, :] == iota((cols, span), 0)
        patch_hot = jnp.where(same, 1.0, 0.0).astype(BF)
        query = mm(tile_rows, w_ref[:, :width])
        keys = mm(w_ref[:, width : 2 * width], tile_rows, (((0,), (1,)), ((), ())))
        value = mm(tile_rows, w_ref[:, 2 * width :]).astype(BF)
        patch_far = mm(patch_hot, far, TN).astype(BF)
        for g in range(groups):
            some = slice(g * cols, (g + 1) * cols)
            qx[g, at, :cols] = query[:, some].astype(BF)
            qx[g, at, cols:] = patch_far
            kx[g, :cols, at] = keys[some].astype(BF)
            kx[g, cols:, at] = patch_hot
            vx[g, at, :cols] = value[:, some]
        query_most = jnp.max(jnp.abs(query), axis=0, keepdims=True)
        key_most = jnp.max(jnp.abs(keys), axis=1, keepdims=True)
        by_head = jnp.where(
            iota((heads, width), 1) // HDIM == iota((heads, width), 0), query_most, 0.0
        )
        bounds.append(mm(by_head.astype(BF), jnp.broadcast_to(key_most, (width, 128)).astype(BF)))
    bound = bounds[0]
    for other in bounds[1:]:
        bound = jnp.maximum(bound, other)
    safe = jnp.max(bound) * SCORE_SCALE < SCORE_SAFE

    def block(s, _):
        start = pl.multiple_of(s // per_tile * span, span)
        steps = count_ref[s]
        here = pl.ds(pl.multiple_of(s * ROWS, ROWS), ROWS)

        def run(first, length, exact):
            at = pl.ds(pl.multiple_of(start + first, ROWS), length)
            scores = []
            for g in range(groups):
                q = qx[g, here, :]
                stacked = jnp.concatenate(
                    [jnp.where(of_head[h], q, jnp.zeros_like(q)) for h in range(HEAD_GROUP)],
                    axis=0,
                )
                scores.append(mm(stacked, kx[g, :, at]))
            for g in range(groups):
                level = scores[g] * SCORE_SCALE
                if exact:
                    level = level - jnp.max(level, axis=1, keepdims=True)
                weights = jnp.exp2(level).astype(BF)
                mixed = mm(weights, vx[g, at, :])
                mixed = mixed.reshape(HEAD_GROUP, ROWS, 2 * cols)
                own = mixed[0]
                for h in range(1, HEAD_GROUP):
                    own = jnp.where(lane_out == h, mixed[h], own)
                att[here, g * cols : (g + 1) * cols] = (own[:, :cols] / own[:, cols:]).astype(BF)

        for i in range(span // WINDOW):
            pl.when(safe & (steps == i + 1))(
                functools.partial(run, low_ref[s], (i + 1) * WINDOW, False)
            )
        pl.when(jnp.logical_not(safe))(functools.partial(run, 0, span, True))
        return 0

    lax.fori_loop(0, tiles * per_tile, block, 0)

    for t in range(tiles):
        at = slice(t * span, (t + 1) * span)
        turn = turn_ref[t]
        mixed = (x[at, :].astype(F32) + mm(att[at, :], wo_ref[...])).astype(BF)
        wrapped[t, :span, :] = mixed
        wrapped[t, span:, :] = mixed[:ROWS]
        runs = local_ref[t : t + 1, :] + iota((1, span), 1) // ROWS * ROWS
        runs = pltpu.roll(jnp.broadcast_to(runs, (8, span)), lax.rem(span - turn, span), 1)
        code[t, :, :span] = runs
        code[t, :, span:] = runs[:, :ROWS]
        for b in range(per_tile):
            first = lax.rem(b * ROWS + span - turn, span) // ROWS * ROWS
            window = pl.ds(pl.multiple_of(first, ROWS), 2 * ROWS)
            run = iota((ROWS, 2 * ROWS), 0) + b * ROWS == code[t, 0:1, window]
            sums = mm(jnp.where(run, 1.0, 0.0).astype(BF), wrapped[t, window, :])
            put = pl.multiple_of(base_ref[t * per_tile + b], ALIGN)
            out_ref[pl.ds(put, ROWS), :] = sums.astype(BF)


def attend(index, low, count, base, turn, local, ids, w_qkv, w_out, rows):
    tiles, span = ids.shape
    width = rows.shape[1]
    cols = HEAD_GROUP * HDIM
    groups = width // cols
    pairs = tiles * span * span * HEAD_GROUP
    return pl.pallas_call(
        attend_kernel,
        out_shape=jax.ShapeDtypeStruct((tiles * span + CHUNK, width), BF),
        in_specs=[SMEM, SMEM, SMEM, SMEM, SMEM, VMEM, VMEM, VMEM, VMEM, HBM],
        out_specs=VMEM,
        scratch_shapes=[
            pltpu.VMEM((tiles * span, width), BF),
            pltpu.VMEM((groups, tiles * span, 2 * cols), BF),
            pltpu.VMEM((groups, 2 * cols, tiles * span), BF),
            pltpu.VMEM((groups, tiles * span, 2 * cols), BF),
            pltpu.VMEM((tiles * span, width), BF),
            pltpu.VMEM((2 * span, width), F32),
            pltpu.VMEM((tiles, span + ROWS, width), BF),
            pltpu.VMEM((tiles, 8, span + ROWS), jnp.int32),
            pltpu.SemaphoreType.DMA((tiles,)),
        ],
        compiler_params=ROOM,
        cost_estimate=cost(pairs * 1024, 4 * rows.size, pairs),
    )(index, low, count, base, turn, local, ids, w_qkv, w_out, rows)


def route_kernel(base_ref, code_ref, sums_ref, out_ref, acc):
    total = out_ref.shape[0]
    chunks = (base_ref[base_ref.shape[0] - 1] + CHUNK - 1) // CHUNK
    seat = iota((total, 1), 0) + pl.program_id(0) * total
    acc[...] = jnp.zeros_like(acc)

    def step(c, _):
        at = pl.ds(pl.multiple_of(c * CHUNK, CHUNK), CHUNK)
        member = jnp.where(seat == code_ref[0:1, at], 1.0, 0.0).astype(BF)
        acc[...] += mm(member, sums_ref[at, :])
        return 0

    lax.fori_loop(0, chunks, step, 0)
    out_ref[...] = acc[...].astype(BF)


def route_sums(base, code, sums, devices):
    count, width = sums.shape
    total = devices * SEAT
    part = min(TURN, total)
    return pl.pallas_call(
        route_kernel,
        grid=(total // part,),
        out_shape=jax.ShapeDtypeStruct((total, width), BF),
        in_specs=[SMEM, VMEM, VMEM],
        out_specs=pl.BlockSpec((part, width), lambda i: (i, 0)),
        scratch_shapes=[pltpu.VMEM((part, width), F32)],
        compiler_params=ROOM,
        cost_estimate=cost(total * count * width, 4 * count * width),
    )(base, code, sums)


def fold_rows(step, pieces_ref, about):
    total = 0.0
    part = min(TURN, pieces_ref.shape[0])
    first = step * SEAT
    seats = []
    for i in (1, 3):
        seat = about[:, i + 1 : i + 2].astype(jnp.int32) - first
        seated = (seat >= 0) & (seat < SEAT)
        seats.append(jnp.where(seated, about[:, i : i + 1].astype(jnp.int32) * SEAT + seat, -1))
    for low in range(0, pieces_ref.shape[0], part):
        column = iota((1, part), 1) + low
        member = (column == seats[0]) | (column == seats[1])
        member = jnp.where(member, 1.0, 0.0).astype(BF)
        total = total + mm(member, pieces_ref[low : low + part, :])
    return total


def fold_kernel(step_ref, pieces_ref, about_ref, before_ref, out_ref):
    out_ref[...] = before_ref[...] + fold_rows(step_ref[0], pieces_ref, about_ref[...])


def fold_pieces(step, pieces, about, before):
    parents, width = before.shape
    chunk = 256
    along = lambda i: (i, 0)
    return pl.pallas_call(
        fold_kernel,
        grid=(parents // chunk,),
        out_shape=jax.ShapeDtypeStruct((parents, width), F32),
        in_specs=[
            SMEM,
            pl.BlockSpec(pieces.shape, lambda i: (0, 0)),
            pl.BlockSpec((chunk, 128), along),
            pl.BlockSpec((chunk, width), along),
        ],
        out_specs=pl.BlockSpec((chunk, width), along),
        compiler_params=ROOM,
        cost_estimate=cost(2 * parents * pieces.size, 4 * pieces.size),
    )(step, pieces, about, before)


def whole_tiles(rows):
    return (rows + 15) // 16 * 16


def pad_rows(value):
    spare = whole_tiles(value.shape[0]) - value.shape[0]
    if spare == 0:
        return value
    return jnp.concatenate([value, jnp.zeros((spare, value.shape[1]), value.dtype)], axis=0)


def pool_kernel(
    per_owner,
    pieces_ref,
    more_ref,
    about_ref,
    w_ref,
    gain_ref,
    shift_ref,
    cot_ref,
    pooled_ref,
    sent_ref,
    acc,
    sums,
):
    step = pl.program_id(0)

    @pl.when(step == 0)
    def _():
        acc[...] = jnp.zeros_like(acc)
        sums[...] = jnp.zeros_like(sums)

    chunk, width = more_ref.shape
    about = about_ref[...]
    total = more_ref[...] + fold_rows(0, pieces_ref, about)
    lengths = about[:, 0:1]
    parent_in = (total / lengths).astype(BF)
    w_pool = w_ref[...]
    gain = gain_ref[...]
    projected = mm(parent_in, w_pool)
    centred = projected - jnp.mean(projected, axis=-1, keepdims=True)
    variance = jnp.mean(centred * centred, axis=-1, keepdims=True)
    inv_std = lax.rsqrt(variance + norm_eps)
    normed = centred * inv_std
    shifted = normed * gain + shift_ref[...]
    normal_cdf = 0.5 * (1.0 + lax.erf(shifted * inv_sqrt_two))
    pooled_ref[...] = (shifted * normal_cdf).astype(BF)
    grad_act = cot_ref[...].astype(F32) * (
        normal_cdf + shifted * jnp.exp(-0.5 * shifted * shifted) * inv_sqrt_tau
    )
    sums[0:1, :] += jnp.sum(grad_act * normed, axis=0, keepdims=True)
    sums[1:2, :] += jnp.sum(grad_act, axis=0, keepdims=True)
    scaled = grad_act * gain
    grad_proj = (
        (
            scaled
            - jnp.mean(scaled, axis=-1, keepdims=True)
            - normed * jnp.mean(scaled * normed, axis=-1, keepdims=True)
        )
        * inv_std
    ).astype(BF)
    acc[...] += mm(parent_in, grad_proj, TN)
    back = mm(grad_proj, w_pool, NT)
    devices, _, width = sent_ref.shape
    fits = chunk // per_owner
    for d in range(fits):
        part = back[d * per_owner : (d + 1) * per_owner]
        sent_ref[step * fits + d, : whole_tiles(per_owner), :] = pad_rows(part).astype(BF)

    @pl.when(step == pl.num_programs(0) - 1)
    def _():
        each = acc.shape[0] // devices
        exact = sums[0:2, :]
        high = exact.astype(BF).astype(F32)
        parts = []
        for value in (high, exact - high):
            for row in range(2):
                for low in range(0, acc.shape[1], width):
                    parts.append(value[row : row + 1, low : low + width])
        norm = jnp.concatenate(parts, axis=0)
        for d in range(devices):
            parts = []
            for side in range(0, acc.shape[1], width):
                parts.append(pad_rows(acc[d * each : (d + 1) * each, side : side + width]))
            rest = jnp.concatenate(parts + [norm], axis=0)
            sent_ref[d, whole_tiles(per_owner) :, :] = rest.astype(BF)


def pool(pieces, more, about, w_pool, gain, shift, cotangent):
    parents, width = more.shape
    wide = w_pool.shape[1]
    chunk = parents
    devices = pieces.shape[0] // SEAT
    tall = whole_tiles(parents // devices) + wide // width * whole_tiles(width // devices)
    tall += 4 * wide // width
    fixed = lambda i: (0, 0)
    along = lambda i: (i, 0)
    return pl.pallas_call(
        functools.partial(pool_kernel, parents * SEAT // pieces.shape[0]),
        grid=(parents // chunk,),
        out_shape=(
            jax.ShapeDtypeStruct((parents, wide), BF),
            jax.ShapeDtypeStruct((devices, tall, width), BF),
        ),
        in_specs=[
            pl.BlockSpec(pieces.shape, fixed),
            pl.BlockSpec((chunk, width), along),
            pl.BlockSpec((chunk, 128), along),
            pl.BlockSpec((width, wide), fixed),
            pl.BlockSpec((1, wide), fixed),
            pl.BlockSpec((1, wide), fixed),
            pl.BlockSpec((chunk, wide), along),
        ],
        out_specs=(
            pl.BlockSpec((chunk, wide), along),
            pl.BlockSpec((devices, tall, width), lambda i: (0, 0, 0)),
        ),
        scratch_shapes=[
            pltpu.VMEM((width, wide), F32),
            pltpu.VMEM((8, wide), F32),
        ],
        compiler_params=FULL,
        cost_estimate=cost(6 * parents * width * wide, 8 * parents * wide, 2 * parents * wide),
    )(pieces, more, about, w_pool, gain, shift, cotangent)


def spread_kernel(span_ref, grad_ref, out_ref, share):
    step = pl.program_id(0)
    chunk = out_ref.shape[0]
    parents, width = share.shape

    @pl.when(step == 0)
    def _():
        pick = jnp.where(iota((8, width), 0) == 2, 1.0, 0.0).astype(BF)
        lengths = mm(jnp.minimum(span_ref[...], 64).astype(F32).astype(BF), pick, TN)
        per_owner = parents // grad_ref.shape[0]
        grads = [grad_ref[d, :per_owner, :].astype(F32) for d in range(grad_ref.shape[0])]
        share[...] = (jnp.concatenate(grads, axis=0) / lengths).astype(BF)

    row = iota((chunk, parents), 0) + step * chunk
    inside = (row >= span_ref[0:1, :]) & (row < span_ref[1:2, :])
    out_ref[...] = mm(jnp.where(inside, 1.0, 0.0).astype(BF), share[...]).astype(BF)


def spread_grads(span, arrived, rows):
    parents = span.shape[1]
    width = arrived.shape[2]
    chunk = 512
    fixed = lambda i: (0, 0)
    return pl.pallas_call(
        spread_kernel,
        grid=(rows // chunk,),
        out_shape=jax.ShapeDtypeStruct((rows, width), BF),
        in_specs=[
            pl.BlockSpec((8, parents), fixed),
            pl.BlockSpec(arrived.shape, lambda i: (0, 0, 0)),
        ],
        out_specs=pl.BlockSpec((chunk, width), lambda i: (i, 0)),
        scratch_shapes=[pltpu.VMEM((parents, width), BF)],
        compiler_params=ROOM,
        cost_estimate=cost(2 * rows * parents * width, 4 * rows * width),
    )(span, arrived)


def settle_kernel(per_owner, arrived_ref, shared_ref, norm_ref):
    devices, tall, width = arrived_ref.shape
    low = whole_tiles(per_owner)
    total = arrived_ref[0, low:, :].astype(F32)
    for d in range(1, devices):
        total = total + arrived_ref[d, low:, :].astype(F32)
    weight_rows = shared_ref.shape[1]
    weight = total[:weight_rows].astype(BF)
    for d in range(devices):
        shared_ref[d] = weight
    norm = total[weight_rows : weight_rows + 8]
    sides = norm_ref.shape[1] // width
    for row in range(2):
        for side in range(sides):
            i = row * sides + side
            value = norm[i : i + 1] + norm[2 * sides + i : 2 * sides + i + 1]
            norm_ref[row : row + 1, side * width : (side + 1) * width] = value


def settle(arrived, per_owner, weight_rows, wide):
    devices, tall, width = arrived.shape
    return pl.pallas_call(
        functools.partial(settle_kernel, per_owner),
        out_shape=(
            jax.ShapeDtypeStruct((devices, weight_rows, width), BF),
            jax.ShapeDtypeStruct((2, wide), F32),
        ),
        in_specs=[VMEM],
        out_specs=(VMEM, VMEM),
        compiler_params=ROOM,
        cost_estimate=cost(arrived.size, 2 * arrived.size),
    )(arrived)


def piece_seats(info, codes, blocks, per_owner):
    devices = codes.shape[0]
    parents = devices * per_owner
    me = lax.axis_index("pts")
    packed = info.reshape(devices, parents)
    span = blocks * ROWS
    lane = jnp.arange(blocks)

    def at_block(block):
        found = jnp.where(block[:, :, None] == lane, codes[:, None, :], 0)
        return jnp.sum(found, axis=2)

    first = packed // 16
    end = first + packed % 16 - 1
    near = at_block(first // ROWS)
    far = at_block(end // ROWS)
    split = first // ROWS != end // ROWS
    holders = jnp.arange(devices)
    by_owner = lambda value: value.reshape(devices, devices, per_owner, 1)
    filled = (by_owner(near // blocks) == holders).astype(jnp.int32)
    filled += (by_owner(jnp.where(split, far // blocks, -1)) == holders).astype(jnp.int32)
    rounds = (jnp.max(jnp.sum(filled, axis=(0, 2))) + SEAT - 1) // SEAT

    mine = lambda value: lax.dynamic_slice_in_dim(value, me * per_owner, per_owner, axis=1)
    near, far, split, first, packed = map(mine, (near, far, split, first, packed))
    near_key = near * ROWS + first % ROWS
    far_key = jnp.where(split, far * ROWS, devices * span)
    near_key, far_key = near_key.reshape(parents, 1), far_key.reshape(parents, 1)
    every = jnp.concatenate([near_key, far_key], axis=0).reshape(1, 2 * parents)

    def place(key):
        holder = key // span
        rank = jnp.sum((every < key) & (every >= holder * span), axis=1, keepdims=True)
        return holder, jnp.where(holder < devices, rank, -1)

    length = (packed % 16).reshape(parents, 1)
    columns = (length,) + place(near_key) + place(far_key)
    wide = iota((parents, 128), 1)
    about = jnp.zeros((parents, 128), jnp.int32)
    for i, column in enumerate(columns):
        about = jnp.where(wide == i, column, about)
    return about.astype(F32), rounds.astype(jnp.int32)


def swap(parts):
    return lax.all_to_all(parts, "pts", split_axis=0, concat_axis=0, tiled=True)


def exchange(rows, devices):
    return swap(rows.reshape(devices, rows.shape[0] // devices, rows.shape[1])).reshape(rows.shape)


def received_index(codes, blocks, capacity):
    devices = codes.shape[0]
    me = lax.axis_index("pts")
    mine = codes // blocks == me
    slots = codes % blocks
    lane = jnp.arange(blocks)
    rank = jnp.sum(mine[:, None, :] & (lane[None, :] < lane[:, None])[None], axis=2)
    index = jnp.arange(devices)[:, None] * capacity + rank
    both = index * blocks + lane[None, :]
    hit = mine[:, :, None] & (slots[:, :, None] == lane[None, None, :])
    both = jnp.sum(jnp.where(hit, both[:, :, None], 0), axis=(0, 1)).astype(jnp.int32)
    return both // blocks, both % blocks


def local(
    points,
    hil_dest,
    hil_slot,
    patch_ids,
    child_counts,
    parent_order,
    w_qkv,
    w_out,
    w_pool,
    norm_gain,
    norm_shift,
    cotangent,
):
    devices = lax.axis_size("pts")
    blocks = hil_dest.shape[0]
    rows, width = points.shape
    wide = w_pool.shape[1]
    parents = child_counts.shape[1]
    per_owner = parents // devices
    capacity = (blocks + devices - 1) // devices

    me = lax.axis_index("pts")
    info, span = order_tables(child_counts, parent_order, hil_dest, hil_slot, devices)
    info = swap(info)
    payload = pack_blocks(hil_dest, points, devices, capacity)
    received = exchange(payload, devices)
    lines = parents // 256
    codes = info[:, lines, :blocks]
    packed = info[:, :lines]
    info = jnp.concatenate(
        [packed & 65535, lax.shift_right_logical(packed, jnp.int32(16))], axis=1
    )
    index, block = received_index(codes, blocks, capacity)
    source = index // capacity
    table, local_run, base, low, count, turn, turned = seat_rows(
        source, block, info.reshape(-1, 128), patch_ids, per_owner
    )
    code = plan_seats(jnp.zeros((1,), jnp.int32), base, table)
    about, rounds = piece_seats(info, codes, blocks, per_owner)
    more = jnp.broadcast_to(about[:, 127:], (parents, width))
    index, low, count, turn, turned, base, local_run, code, about, rounds, more = (
        lax.optimization_barrier(
            (index, low, count, turn, turned, base, local_run, code, about, rounds, more)
        )
    )
    local_run = local_run.reshape(patch_ids.shape)
    sums = attend(index, low, count, base, turn, local_run, turned, w_qkv, w_out, received)
    pieces = exchange(route_sums(base, code, sums, devices), devices)

    def turn_again(carry):
        step, before = carry
        step = step.reshape(1)
        late = exchange(route_sums(base, plan_seats(step, base, table), sums, devices), devices)
        return step[0] + 1, fold_pieces(step, late, about, before)

    _, more = lax.while_loop(
        lambda carry: carry[0] < rounds, turn_again, (jnp.int32(1), more)
    )
    pooled, outgoing = pool(
        pieces, more, about, w_pool, norm_gain[None], norm_shift[None], cotangent
    )
    arrived = swap(outgoing)
    each = width // devices
    tall = whole_tiles(each)
    sides = wide // width
    shared, grad_norm = settle(arrived, per_owner, sides * tall, wide)
    shared = swap(shared)
    grad_weight = jnp.concatenate(
        [shared[:, side * tall : side * tall + each] for side in range(sides)], axis=2
    )
    grad_weight = grad_weight.reshape(width, wide).astype(F32)
    grad_points = spread_grads(span, arrived, rows)
    return (pooled, grad_points, grad_weight, grad_norm)


def solution(mesh):
    in_specs = (
        P(("grp", "pts"), None),
        P(("grp", "pts")),
        P(("grp", "pts")),
        P(("grp", "pts"), None),
        P(("grp", "pts"), None),
        P(("grp", "pts"), None),
        P(),
        P(),
        P(),
        P(),
        P(),
        P(("grp", "pts"), None),
    )
    out_specs = (P(("grp", "pts"), None), P(("grp", "pts"), None), P("grp", None), P("grp", None))
    return jax.shard_map(local, mesh=mesh, in_specs=in_specs, out_specs=out_specs, check_vma=False)
```
